32 devices in a mesh: genome: 8 (over y, x, core), offset: 4 (over z).
Axes of the slice: x: 2, y: 2, z: 4, core: 2. Of those that a mesh axis runs over, the one named last changes fastest.
Arguments:
- contacts: bfloat16 [5120, 5120], P('offset', 'genome'), as said below
- masked_bins: int32 [128], replicated, may hold values from 0 to 5119
- chrom_bounds: int32 [2], replicated, may hold values from 1 to 5119
Outputs:
- peak_score: float32 [5120, 5120], P('offset', 'genome')
- bias: float32 [5120], P('genome')
The draws below stay inside these ranges and needn't reach their ends.
Inputs may be any that keep to these rules, and one draw needn't show every extreme that they name: `contacts`: every entry is positive.
All inputs are finite; a program needn't handle non-finite values.
Results may differ from the reference program's by a relative error of at most 0.0003.
Values sent between devices are 32-bit elements; how exact they have to be, the bound alone decides.
No kernel may reach another device: no remote copies, remote signals or barrier semaphores. Data moves between devices by JAX's collectives and lax.ppermute only.
A program may use at most 128 MiB of HBM per device.

```python
import math
import jax
import jax.numpy as jnp
from jax import lax

W = 5120
P1 = 2
P2 = 5
SWEEPS = 2
NCHB = 2
NB = 5120
NMASK = 128


def draw_contacts(key, part):
    key_rows, key_noise = jax.random.split(key, 2)
    window_span = NB + W
    row_factor = jnp.exp(jax.random.uniform(key_rows, (window_span,), jnp.float32, 0.0, math.log(10.0)))
    diag_ids = jnp.arange(W, dtype=jnp.int32)[:, None]
    bin_ids = jnp.arange(NB, dtype=jnp.int32)[None, :]
    decay_law = (diag_ids.astype(jnp.float32) + 1.0) ** (-0.8)
    noise_field = jnp.exp(0.5 * jnp.clip(jax.random.normal(key_noise, (W, NB), jnp.float32), -4.0, 4.0))
    values = 4.0 * row_factor[bin_ids] * row_factor[bin_ids + diag_ids] * decay_law * noise_field
    return values.astype(jnp.bfloat16)


def plant(entries, rng, low, largest):
    dims = entries.shape
    spot = [jax.random.randint(jax.random.fold_in(rng, axis), (), 0, dims[axis]) for axis in range(len(dims))]
    entries = entries.at[tuple(spot)].set(low)
    longest = dims.index(max(dims))
    spot[longest] = (spot[longest] + 1) % dims[longest]
    return entries.at[tuple(spot)].set(largest)


def setup_inputs(seed: int = 0) -> dict:
    key_of = jax.random.split(jax.random.key(seed), 4)
    contacts = draw_contacts(jax.random.fold_in(key_of[3], 71), 0)
    masked_bins = plant(jax.random.randint(key_of[1], (NMASK,), 0, NB), jax.random.fold_in(key_of[1], 1), 0, NB - 1).astype(jnp.int32)
    chrom_bounds = jax.random.randint(key_of[2], (NCHB,), 1, NB).astype(jnp.int32)
    return dict(contacts=contacts, masked_bins=masked_bins, chrom_bounds=chrom_bounds)


def filter_offsets(inner_width, outer_width):
    span_range = range(-outer_width, outer_width + 1)
    donut_set = [(row_shift, col_shift) for row_shift in span_range for col_shift in span_range
                 if row_shift != 0 and col_shift != 0
                 and not (abs(row_shift) <= inner_width and abs(col_shift) <= inner_width)]
    lower_left = [(row_shift, col_shift) for row_shift in range(1, outer_width + 1)
                  for col_shift in range(-outer_width, 0)
                  if not (row_shift <= inner_width and col_shift >= -inner_width)]
    horizontal = [(row_shift, col_shift) for row_shift in (-1, 0, 1) for col_shift in span_range
                  if abs(col_shift) > inner_width]
    vertical = [(row_shift, col_shift) for row_shift in span_range if abs(row_shift) > inner_width
                for col_shift in (-1, 0, 1)]
    return [donut_set, lower_left, horizontal, vertical]


def window_sum(padded, offsets, halo_width, row_count, col_count):
    running_total = None
    for row_shift, col_shift in offsets:
        start = halo_width + col_shift - row_shift
        piece = padded[start:start + row_count, halo_width + row_shift:halo_width + row_shift + col_count]
        running_total = piece if running_total is None else running_total + piece
    return running_total


def reference(contacts, masked_bins, chrom_bounds):
    band_width, total_bins = contacts.shape
    halo_width = 2 * P2
    keep_full = jnp.ones((total_bins,), jnp.float32).at[masked_bins].set(0.0)
    bin_line = jnp.arange(total_bins, dtype=jnp.int32)
    chrom_full = jnp.sum((bin_line[:, None] >= chrom_bounds[None, :]).astype(jnp.int32), axis=1)
    diag_ids = jnp.arange(band_width, dtype=jnp.int32)[:, None]
    bin_ids = bin_line[None, :]
    partner_ids = diag_ids + bin_ids
    inside = partner_ids < total_bins
    clipped = jnp.minimum(partner_ids, total_bins - 1)
    same_chrom = (chrom_full[None, :] == chrom_full[clipped]).astype(jnp.float32)
    valid_mask = keep_full[None, :] * jnp.where(inside, keep_full[clipped], 0.0) * same_chrom
    weighted = contacts.astype(jnp.float32) * valid_mask
    off_main = (diag_ids >= 1).astype(jnp.float32)
    kept_count = jnp.sum(keep_full)

    def balance(bias_full):
        return weighted * bias_full[None, :] * bias_full[clipped]

    bias_full = keep_full
    for sweep_index in range(SWEEPS):
        balanced = balance(bias_full)
        own_sums = jnp.sum(balanced, axis=0)
        partner_sums = jax.ops.segment_sum((balanced * off_main).reshape(-1), partner_ids.reshape(-1),
                                           num_segments=total_bins + band_width)[:total_bins]
        row_sums = own_sums + partner_sums
        level = jnp.sum(row_sums * keep_full) / kept_count
        safe_sums = jnp.where(keep_full > 0, row_sums, 1.0)
        bias_full = jnp.where(keep_full > 0, bias_full * level / safe_sums, 0.0)
    balanced = balance(bias_full)
    expected = jnp.sum(balanced, axis=1) / jnp.maximum(jnp.sum(valid_mask, axis=1), 1.0)
    local_expected = expected[:, None] * valid_mask
    observed_pad = jnp.pad(balanced, halo_width)
    expected_pad = jnp.pad(local_expected, halo_width)
    offset_lists = filter_offsets(P1, P2)
    block_bins = 128
    block_count = total_bins // block_bins

    def one_block(block_index):
        start = (block_index * block_bins).astype(jnp.int32)
        zero = jnp.zeros((), jnp.int32)
        observed_block = lax.dynamic_slice(observed_pad, (zero, start), (band_width + 2 * halo_width, block_bins + 2 * halo_width))
        expected_block = lax.dynamic_slice(expected_pad, (zero, start), (band_width + 2 * halo_width, block_bins + 2 * halo_width))
        center = lax.dynamic_slice(balanced, (zero, start), (band_width, block_bins))
        valid_block = lax.dynamic_slice(valid_mask, (zero, start), (band_width, block_bins))
        center_expected = jnp.where(valid_block > 0, expected[:, None], 1.0)
        score = None
        for offsets in offset_lists:
            observed_sum = window_sum(observed_block, offsets, halo_width, band_width, block_bins)
            expected_sum = window_sum(expected_block, offsets, halo_width, band_width, block_bins)
            ratio = center * (expected_sum + center_expected) / (center_expected * (observed_sum + center_expected))
            score = ratio if score is None else jnp.minimum(score, ratio)
        return jnp.where(valid_block > 0, score, 0.0)

    blocks = lax.map(one_block, jnp.arange(block_count, dtype=jnp.int32), batch_size=8)
    peak_score = jnp.transpose(blocks, (1, 0, 2)).reshape(band_width, total_bins)
    return peak_score, bias_full
```

```python
import functools

import jax
import jax.numpy as jnp
from jax import lax
from jax.experimental import pallas as pl
from jax.experimental.pallas import tpu as pltpu
from jax.sharding import PartitionSpec as P

RIM = 16
SIDE = 8
LANES = 128
F32 = jnp.float32
BF16 = jnp.bfloat16
TINY = 2.0**-126
VMEM = pl.BlockSpec(memory_space=pltpu.VMEM)
SMEM = pl.BlockSpec(memory_space=pltpu.SMEM)
NT = (((1,), (1,)), ((), ()))


def params(mib=48):
    return pltpu.CompilerParams(vmem_limit_bytes=mib << 20)


def iota(shape, dim):
    return lax.broadcasted_iota(jnp.int32, shape, dim)


def split3(x):
    hi = x.astype(BF16)
    rest = x - hi.astype(F32)
    mid = rest.astype(BF16)
    low = (rest - mid.astype(F32)).astype(BF16)
    return hi, mid, low


def place(nd, nb):
    first = lax.axis_index("genome") * nb
    partner = first + lax.axis_index("offset") * nd
    return first // LANES, partner // LANES, partner % LANES


def roll(x, shift):
    length = x.shape[1]
    if isinstance(shift, int):
        shift = shift % length
        if shift == 0:
            return x
    return pltpu.roll(x, shift, 1)


def hankel(rows_ref, row0, lane0, tiles, out_ref):
    extra = 1 if lane0 is None else 2
    base = jnp.concatenate(
        [jnp.broadcast_to(rows_ref[pl.ds(row0 + t, 1), :], (8, LANES)) for t in range(tiles + extra)],
        axis=1,
    )
    length = base.shape[1]
    if lane0 is not None:
        base = roll(base, length - lane0)
    sub = iota(base.shape, 0)
    for bit in (1, 2, 4):
        base = jnp.where((sub & bit) > 0, roll(base, length - bit), base)
    for r in range(16):
        out_ref[8 * r : 8 * r + 8, : tiles * LANES] = roll(base, length - 8 * r)[:, : tiles * LANES]


def antidiagonal(acc_ref, tiles, lane0):
    extra = 1 if lane0 is None else 2
    pad = jnp.zeros((8, extra * LANES), F32)
    total = None
    for r in range(15, -1, -1):
        part = jnp.concatenate([acc_ref[8 * r : 8 * r + 8, : tiles * LANES], pad], axis=1)
        total = part if total is None else roll(total, 8) + part
    sub = iota(total.shape, 0)
    for bit in (4, 2, 1):
        total = jnp.where((sub & bit) > 0, roll(total, bit), total)
    total = jnp.sum(total, axis=0, keepdims=True)
    if lane0 is not None:
        total = roll(total, lane0)
    return total


def spread(own, partner, row_own, row_partner, placed_ref, out_ref):
    placed_ref[...] = jnp.zeros_like(placed_ref)
    for t in range(partner.shape[1] // LANES):
        placed_ref[pl.ds(row_partner + t, 1), :] = partner[:, t * LANES : (t + 1) * LANES]
    for c in range(own.shape[1] // LANES):
        placed_ref[pl.ds(row_own + c, 1), :] += own[:, c * LANES : (c + 1) * LANES]
    out_ref[...] = placed_ref[: out_ref.shape[0], :]


def sweep(nd, nb, entry, weigh_own, weigh_partner, acc_ref):
    cols = nb // LANES
    full, rest = nd // LANES, nd % LANES
    first_diag = lax.axis_index("offset") * nd
    sub = iota((16, LANES), 0)

    def body(ms, fresh, r, own):
        own = list(own)
        q0 = pl.multiple_of(16 * r, 16)
        sums = {}
        for m in ms:
            for c in range(cols):
                w = entry(m, c, q0)
                own[c] = own[c] + weigh_own(w, m, c, q0)
                g = weigh_partner(w, c)
                if m == 0:
                    g = jnp.where(sub + q0 + first_diag > 0, g, 0.0)
                sums[m + c] = sums[m + c] + g if m + c in sums else g
        for t, value in sums.items():
            tile = (pl.ds(q0, 16), slice(t * LANES, (t + 1) * LANES))
            acc_ref[tile] = value if fresh else acc_ref[tile] + value
        return tuple(own)

    own = tuple(jnp.zeros((16, LANES), F32) for _ in range(cols))
    if rest:
        acc_ref[...] = jnp.zeros_like(acc_ref)
    own = lax.fori_loop(0, 8, functools.partial(body, range(full), not rest), own)
    if rest:
        own = lax.fori_loop(0, rest // 16, functools.partial(body, [full], False), own)
    return jnp.concatenate([jnp.sum(o, axis=0, keepdims=True) for o in own], axis=1)


def keep_of(masked, rows):
    count = masked.shape[1]
    in_row = (jnp.broadcast_to(masked >> 7, (rows, count)) == iota((rows, count), 0))
    in_lane = (jnp.broadcast_to(masked & 127, (LANES, count)) == iota((LANES, count), 0))
    hits = lax.dot_general(
        in_row.astype(F32).astype(BF16), in_lane.astype(F32).astype(BF16), NT, preferred_element_type=F32
    )
    return jnp.where(hits > 0.0, 0.0, 1.0)


def first_kernel(nd, nb, bounds_ref, x_ref, masked_ref, w_ref, part_ref, keep_ref, top_ref, bottom_ref,
                 codes_ref, hank_ref, acc_ref, placed_ref):
    rows = keep_ref.shape[0]
    cols = nb // LANES
    span = -(-nd // LANES) + cols - 1
    row_own, row_partner, lane0 = place(nd, nb)
    lane0 = lane0 if nd % LANES else None
    keep = keep_of(masked_ref[...], rows)
    keep_ref[...] = keep
    bins = iota((rows, LANES), 0) * LANES + iota((rows, LANES), 1)
    chrom = jnp.zeros((rows, LANES), F32)
    for k in range(bounds_ref.shape[0]):
        chrom = chrom + jnp.where(bins >= bounds_ref[k], 1.0, 0.0)
    codes_ref[...] = jnp.full_like(codes_ref, -2.0)
    codes_ref[:rows, :] = jnp.where(keep > 0.0, chrom, -2.0)
    hankel(codes_ref, row_partner, lane0, span, hank_ref)
    code_own = []
    for c in range(cols):
        code = codes_ref[pl.ds(row_own + c, 1), :]
        code = jnp.where(code < 0.0, -1.0, code)
        code_own.append(jnp.broadcast_to(code, (16, LANES)))

    def entry(m, c, q0):
        here = (pl.ds(q0 + m * LANES, 16), slice(c * LANES, (c + 1) * LANES))
        code = hank_ref[pl.ds(q0, 16), (m + c) * LANES : (m + c + 1) * LANES]
        value = jnp.maximum(x_ref[here].astype(F32), TINY)
        w = jnp.where(code == code_own[c], value, 0.0)
        w_ref[here] = w.astype(BF16)
        return w

    own = sweep(nd, nb, entry, lambda w, m, c, q0: w, lambda w, c: w, acc_ref)
    spread(own, antidiagonal(acc_ref, span, lane0), row_own, row_partner, placed_ref, part_ref)
    top_ref[...] = w_ref[:RIM, :].astype(F32)
    bottom_ref[...] = w_ref[nd - RIM :, :].astype(F32)


def next_bias(keep, bias, sums):
    level = jnp.sum(sums * keep, keepdims=True) / jnp.sum(keep, keepdims=True)
    safe = jnp.where(keep > 0.0, sums, 1.0)
    return jnp.where(keep > 0.0, bias * level / safe, 0.0)


def second_kernel(nd, nb, w_ref, sums_ref, keep_ref, part_ref, bias_ref, window_ref, hank_ref, acc_ref, placed_ref):
    rows = keep_ref.shape[0]
    cols = nb // LANES
    span = -(-nd // LANES) + cols - 1
    row_own, row_partner, lane0 = place(nd, nb)
    lane0 = lane0 if nd % LANES else None
    bias = next_bias(keep_ref[...], keep_ref[...], sums_ref[...])
    bias_ref[...] = bias
    window_ref[...] = jnp.zeros_like(window_ref)
    window_ref[:rows, :] = bias
    hankel(window_ref, row_partner, lane0, span, hank_ref)
    rows_own = [window_ref[pl.ds(row_own + c, 1), :] for c in range(cols)]
    own_bias = [jnp.broadcast_to(b, (16, LANES)) for b in rows_own]

    def entry(m, c, q0):
        return w_ref[pl.ds(q0 + m * LANES, 16), c * LANES : (c + 1) * LANES].astype(F32)

    def weigh_own(w, m, c, q0):
        return w * hank_ref[pl.ds(q0, 16), (m + c) * LANES : (m + c + 1) * LANES]

    own = sweep(nd, nb, entry, weigh_own, lambda w, c: w * own_bias[c], acc_ref)
    own = own * jnp.concatenate(rows_own, axis=1)
    partner = antidiagonal(acc_ref, span, lane0)
    tiles = partner.shape[1] // LANES
    partner = partner * jnp.concatenate(
        [window_ref[pl.ds(row_partner + t, 1), :] for t in range(tiles)], axis=1
    )
    spread(own, partner, row_own, row_partner, placed_ref, part_ref)


def side_kernel(nd, nb, w_ref, top_ref, bottom_ref, left_ref, right_ref):
    row, lane = iota((SIDE, LANES), 0), iota((SIDE, LANES), 1)
    for out_ref, pick, first in (
        (left_ref, row == lane, 0),
        (right_ref, row + LANES - SIDE == lane, nb - LANES),
    ):
        pick = pick.astype(F32).astype(BF16)
        cols = slice(first, first + LANES)
        block = jnp.concatenate(
            [w_ref[:, cols], bottom_ref[:, cols].astype(BF16), top_ref[:, cols].astype(BF16)], axis=0
        )
        out_ref[...] = lax.dot_general(pick, block, NT, preferred_element_type=F32)


def strip_kernel(nd, nb, first, count, w_ref, top_ref, bottom_ref, left_ref, right_ref, out_ref, perm_ref, side_ref):
    stride = nb // LANES
    width = count * LANES
    lane = iota((nb, LANES), 1)
    row = iota((nb, LANES), 0)
    for k in range(count):
        hit = row == lane * stride + (first + k)
        perm_ref[:, k * LANES : (k + 1) * LANES] = hit.astype(F32).astype(BF16)
    perm = perm_ref[...]
    rims = []
    row, lane = iota((2 * SIDE, LANES), 0), iota((2 * SIDE, LANES), 1)
    bin_of = jnp.where(row < SIDE, row - SIDE, row - SIDE + nb)
    for k in range(count):
        rims.append((bin_of == lane * stride + (first + k)).astype(F32).astype(BF16))
    rims = jnp.concatenate(rims, axis=1)
    sides = jnp.concatenate([left_ref[...], right_ref[...]], axis=0).astype(BF16)
    outer = first < 0 or first + count > stride
    if outer:
        side_ref[...] = lax.dot_general(
            sides, rims, (((0,), (0,)), ((), ())), preferred_element_type=F32
        )

    def emit(block, at, side_at, rows):
        value = jnp.dot(block, perm, preferred_element_type=F32)
        if outer:
            value = value + side_ref[pl.ds(side_at, rows), :]
        for k in range(count):
            out_ref[k, pl.ds(at, rows), :] = value[:, k * LANES : (k + 1) * LANES].astype(BF16)

    emit(top_ref[...].astype(BF16), 0, nd + RIM, RIM)
    emit(bottom_ref[...].astype(BF16), nd + RIM, nd, RIM)
    step = 64

    def body(i, _):
        r0 = pl.multiple_of(i * step, step)
        emit(w_ref[pl.ds(r0, step), :], r0 + RIM, r0, step)
        return 0

    lax.fori_loop(0, nd // step, body, 0)


def column(row, out_ref, at):
    eye = iota((LANES, LANES), 0) == iota((LANES, LANES), 1)
    diag = jnp.where(eye, jnp.broadcast_to(row, (LANES, LANES)), 0.0)
    value = jnp.dot(
        jnp.concatenate(split3(diag), axis=1), jnp.ones((3 * LANES, LANES), BF16), preferred_element_type=F32
    )
    out_ref[at : at + LANES, :] = value


def fan(col_ref, other_ref, start, rows, stride, out_ref):
    lane = {}
    source, offset = col_ref, start
    target = other_ref
    for bit in (64, 32, 16, 8, 4, 2, 1):
        need = rows + stride * (bit - 1)
        need = -(-need // 8) * 8
        if bit == 1:
            target = out_ref
        step = 32 if need >= 32 else 8

        def move(at, size, source=source, target=target, offset=offset, bit=bit):
            low = source[pl.ds(offset + at, size), :]
            high = source[pl.ds(offset + at + stride * bit, size), :]
            odd = (iota((size, LANES), 1) & bit) > 0
            target[pl.ds(at, size), :] = jnp.where(odd, high, low)

        def body(i, _, move=move):
            move(pl.multiple_of(i * 32, 32), 32)
            return 0

        lax.fori_loop(0, need // 32, body, 0)
        for at in range(need // 32 * 32, need, 8):
            move(at, 8)
        source, target, offset = target, source, 0


def fan_rows(nd):
    return nd + 2 * RIM + 32


def third_kernel(nd, nb, mid_ref, sums_ref, keep_ref, bias_ref, own_ref, fan_ref, near_ref, diag_ref,
                 window_ref, col_ref, other_ref, ncol_ref, nother_ref, total_ref):
    rows = keep_ref.shape[0]
    cols = nb // LANES
    stride = cols
    row_own, row_partner, lane0 = place(nd, nb)
    bias = next_bias(keep_ref[...], bias_ref[...], sums_ref[...])
    window_ref[...] = jnp.zeros_like(window_ref)
    window_ref[8 : 8 + rows, :] = bias
    for c in range(cols):
        own_ref[c : c + 1, :] = window_ref[pl.ds(8 + row_own + c, 1), :]
    tiles = col_ref.shape[0] // LANES
    for t in range(tiles):
        column(window_ref[pl.ds(7 + row_partner + t, 1), :], col_ref, t * LANES)
    start = LANES - RIM - 8
    if nd % LANES:
        start = start + lane0
    fan(col_ref, other_ref, start, fan_rows(nd), stride, fan_ref)
    for t in range(ncol_ref.shape[0] // LANES):
        column(window_ref[pl.ds(7 + row_own + t, 1), :], ncol_ref, t * LANES)
    fan(ncol_ref, nother_ref, LANES - 8, near_ref.shape[0], stride, near_ref)
    total_rows = nd + 2 * RIM
    step = 32

    def body(i, _):
        r0 = pl.multiple_of(i * step, step)
        total, count = None, None
        for s in range(stride):
            w = mid_ref[s, pl.ds(r0, step), :].astype(F32)
            b = w * jnp.broadcast_to(near_ref[8 + s : 9 + s, :], (step, LANES)) * fan_ref[pl.ds(r0 + 8 + s, step), :]
            v = jnp.where(w > 0.0, 1.0, 0.0)
            total = b if total is None else total + b
            count = v if count is None else count + v
        hi, mid, low = split3(total)
        for k, part in enumerate((hi, mid, low, count.astype(BF16))):
            total_ref[pl.ds(r0, step), k * LANES : (k + 1) * LANES] = part
        return 0

    lax.fori_loop(0, total_rows // step, body, 0)
    ones = jnp.ones((8, 3 * LANES), BF16)
    padded = diag_ref.shape[1]
    if padded > total_rows:
        total_ref[total_rows:, :] = jnp.zeros((padded - total_rows, 4 * LANES), BF16)
    sums = lax.dot_general(ones, total_ref[:, : 3 * LANES], NT, preferred_element_type=F32)
    counts = lax.dot_general(ones[:, :LANES], total_ref[:, 3 * LANES :], NT, preferred_element_type=F32)
    diag_ref[...] = jnp.where(iota((8, padded), 0) == 0, sums, counts)


def windows(nd, stride, x_ref, tri_ref, u_ref, wd_ref, lp_ref):
    step = 32
    total_rows = nd + 2 * RIM

    def tri(i, _):
        r0 = pl.multiple_of(i * step + 8, 8)
        for s in range(-4, stride + 4):
            tri_ref[s + 4, pl.ds(r0, step), :] = (
                x_ref[s + 4, pl.ds(r0 + 1, step), :]
                + x_ref[s + 5, pl.ds(r0, step), :]
                + x_ref[s + 6, pl.ds(r0 - 1, step), :]
            )
        return 0

    lax.fori_loop(0, (total_rows - 32) // step, tri, 0)
    for r0, size in ((1, 7), (total_rows - 24, 23)):
        for s in range(-4, stride + 4):
            tri_ref[s + 4, r0 : r0 + size, :] = (
                x_ref[s + 4, r0 + 1 : r0 + 1 + size, :]
                + x_ref[s + 5, r0 : r0 + size, :]
                + x_ref[s + 6, r0 - 1 : r0 - 1 + size, :]
            )

    def mixed(r0, size):
        for s in range(stride):
            hp = tri_ref[s + 8, pl.ds(r0 - 4, size), :]
            hm = tri_ref[s, pl.ds(r0 + 4, size), :]
            ep = x_ref[s + 6, pl.ds(r0 - 1, size), :] + x_ref[s + 7, pl.ds(r0 - 2, size), :]
            em = x_ref[s + 4, pl.ds(r0 + 1, size), :] + x_ref[s + 3, pl.ds(r0 + 2, size), :]
            lp = hp + ep
            u_ref[s, pl.ds(r0, size), :] = hp + hm
            lp_ref[s, pl.ds(r0, size), :] = lp
            wd_ref[s, pl.ds(r0, size), :] = lp + (hm + em)

    def mixed_body(i, _):
        mixed(pl.multiple_of(i * step + RIM, 16), step)
        return 0

    lax.fori_loop(0, nd // step, mixed_body, 0)
    mixed(RIM - 8, 8)
    mixed(RIM + nd, 8)

    def runs(r0, size):
        for s in range(stride):
            wd_ref[s, pl.ds(r0, size), :] = (
                wd_ref[s, pl.ds(r0, size), :] + wd_ref[s, pl.ds(r0 + 1, size), :] + wd_ref[s, pl.ds(r0 + 2, size), :]
            )
            tri_ref[s, pl.ds(r0, size), :] = (
                tri_ref[s + 4, pl.ds(r0, size), :]
                + tri_ref[s + 4, pl.ds(r0 + 1, size), :]
                + tri_ref[s + 4, pl.ds(r0 + 2, size), :]
            )

    def runs_body(i, _):
        runs(pl.multiple_of(i * step + RIM, 16) - 5, step)
        return 0

    lax.fori_loop(0, nd // step, runs_body, 0)
    runs(RIM + nd - 5, 8)


def sums_at(s, r0, size, tri_ref, u_ref, wd_ref, lp_ref):
    at = lambda ref, k, shift: ref[k, pl.ds(r0 + shift, size), :]
    u = [at(u_ref, s, shift) for shift in (-2, -1, 0, 1, 2)]
    donut = at(wd_ref, s, -5) + at(wd_ref, s, 3) + (u[0] + u[1]) + (u[3] + u[4])
    vertical = u[1] + u[2] + u[3]
    horizontal = at(tri_ref, s, -5) + at(tri_ref, s, 3)
    lower = (at(lp_ref, s, -5) + at(lp_ref, s, -4) + at(lp_ref, s, -3)) + (
        at(tri_ref, s + 8, -6) + at(tri_ref, s + 8, -5)
    )
    return donut, lower, horizontal, vertical


def scaled(nd, strips, near_ref, fan_ref, x_ref):
    step = 32

    def body(i, _):
        r0 = pl.multiple_of(i * step, step)
        for s, (ref, k) in strips.items():
            w = ref[k, pl.ds(r0, step), :].astype(F32)
            near = jnp.broadcast_to(near_ref[8 + s : 9 + s, :], (step, LANES))
            x_ref[s + 5, pl.ds(r0, step), :] = w * near * fan_ref[pl.ds(r0 + 8 + s, step), :]
        return 0

    lax.fori_loop(0, (nd + 2 * RIM) // step, body, 0)


def strips_of(stride, low_ref, mid_ref, high_ref):
    strips = {}
    for s in range(-5, 0):
        strips[s] = (low_ref, s + 5)
    for s in range(stride):
        strips[s] = (mid_ref, s)
    for s in range(stride, stride + 5):
        strips[s] = (high_ref, s - stride)
    return strips


def observed_kernel(nd, nb, low_ref, mid_ref, high_ref, near_ref, fan_ref, center_ref,
                    donut_ref, lower_ref, horizontal_ref, vertical_ref,
                    x_ref, tri_ref, u_ref, wd_ref, lp_ref):
    stride = nb // LANES
    scaled(nd, strips_of(stride, low_ref, mid_ref, high_ref), near_ref, fan_ref, x_ref)
    windows(nd, stride, x_ref, tri_ref, u_ref, wd_ref, lp_ref)
    step = 32

    def body(i, _):
        o0 = pl.multiple_of(i * step, step)
        r0 = o0 + RIM
        for s in range(stride):
            center_ref[s, pl.ds(o0, step), :] = x_ref[s + 5, pl.ds(r0, step), :]
            sums = sums_at(s, r0, step, tri_ref, u_ref, wd_ref, lp_ref)
            for ref, value in zip((donut_ref, lower_ref, horizontal_ref, vertical_ref), sums):
                ref[s, pl.ds(o0, step), :] = value
        return 0

    lax.fori_loop(0, nd // step, body, 0)


def score_kernel(nd, nb, low_ref, mid_ref, high_ref, diag_ref, center_ref,
                 donut_ref, lower_ref, horizontal_ref, vertical_ref, out_ref,
                 col_ref, x_ref, tri_ref, u_ref, wd_ref, lp_ref, perm_ref):
    stride = nb // LANES
    total_rows = nd + 2 * RIM
    expected = diag_ref[0:1, :] / jnp.maximum(diag_ref[1:2, :], 1.0)
    for t in range(diag_ref.shape[1] // LANES):
        column(expected[:, t * LANES : (t + 1) * LANES], col_ref, t * LANES)
    strips = strips_of(stride, low_ref, mid_ref, high_ref)
    step = 32

    def fill(i, _):
        r0 = pl.multiple_of(i * step, step)
        e = col_ref[pl.ds(r0, step), :]
        for s, (ref, k) in strips.items():
            w = ref[k, pl.ds(r0, step), :].astype(F32)
            x_ref[s + 5, pl.ds(r0, step), :] = jnp.where(w > 0.0, e, 0.0)
        return 0

    lax.fori_loop(0, total_rows // step, fill, 0)
    windows(nd, stride, x_ref, tri_ref, u_ref, wd_ref, lp_ref)
    row, lane = iota((LANES, nb), 0), iota((LANES, nb), 1)
    for s in range(stride):
        perm_ref[s * LANES : (s + 1) * LANES, :] = (lane == row * stride + s).astype(F32).astype(BF16)
    perm = perm_ref[...]

    def body(i, _):
        o0 = pl.multiple_of(i * step, step)
        r0 = o0 + RIM
        e = col_ref[pl.ds(r0, step), :]
        inverse = 1.0 / e
        scores = []
        for s in range(stride):
            sums = sums_at(s, r0, step, tri_ref, u_ref, wd_ref, lp_ref)
            score = None
            for ref, value in zip((donut_ref, lower_ref, horizontal_ref, vertical_ref), sums):
                ratio = (value + e) / (ref[s, pl.ds(o0, step), :] + e)
                score = ratio if score is None else jnp.minimum(score, ratio)
            w = mid_ref[s, pl.ds(r0, step), :].astype(F32)
            score = score * (center_ref[s, pl.ds(o0, step), :] * inverse)
            scores.append(jnp.where(w > 0.0, score, 0.0))
        scores = jnp.concatenate(scores, axis=1)
        hi, mid, _ = split3(scores)
        out_ref[pl.ds(o0, step), :] = jnp.dot(hi, perm, preferred_element_type=F32) + jnp.dot(
            mid, perm, preferred_element_type=F32
        )
        return 0

    lax.fori_loop(0, nd // step, body, 0)


def exchange(x, axis, masks):
    size = lax.axis_size(axis)
    parts = [lax.ppermute(x, axis, [(i, i ^ mask) for i in range(size)]) for mask in masks]
    for part in parts:
        x = x + part
    return x


def total(x, axis):
    size = lax.axis_size(axis)
    bit = 1
    while bit < size:
        x = exchange(x, axis, [bit])
        bit *= 2
    return x


def to_neighbours(before, after, axis):
    size = lax.axis_size(axis)
    up = [(i, i + 1) for i in range(size - 1)]
    down = [(j, i) for i, j in up]
    return lax.ppermute(before, axis, down), lax.ppermute(after, axis, up)


def on_device(contacts, masked_bins, chrom_bounds):
    nd, nb = contacts.shape
    cols = nb // LANES
    bins = nb * lax.axis_size("genome")
    band = nd * lax.axis_size("offset")
    rows = bins // LANES
    span = -(-nd // LANES) + cols - 1
    tall = rows + -(-band // LANES) + 24
    total_rows = nd + 2 * RIM
    shape = jax.ShapeDtypeStruct
    f = lambda *dims: shape(dims, F32)

    w, part, keep, top, bottom = pl.pallas_call(
        functools.partial(first_kernel, nd, nb),
        out_shape=(shape((nd, nb), BF16), f(rows, LANES), f(rows, LANES), f(RIM, nb), f(RIM, nb)),
        in_specs=[SMEM, VMEM, VMEM],
        out_specs=(VMEM,) * 5,
        scratch_shapes=[
            pltpu.VMEM((tall, LANES), F32),
            pltpu.VMEM((LANES, span * LANES), F32),
            pltpu.VMEM((LANES, span * LANES), F32),
            pltpu.VMEM((tall, LANES), F32),
        ],
        compiler_params=params(),
        name="first_sums",
    )(chrom_bounds, contacts, masked_bins.reshape(1, -1))

    bottom_rim, top_rim = to_neighbours(top, bottom, "offset")
    sums = total(total(part, "genome"), "offset")

    part, bias = pl.pallas_call(
        functools.partial(second_kernel, nd, nb),
        out_shape=(f(rows, LANES), f(rows, LANES)),
        in_specs=[VMEM] * 3,
        out_specs=(VMEM,) * 2,
        scratch_shapes=[
            pltpu.VMEM((tall, LANES), F32),
            pltpu.VMEM((LANES, span * LANES), F32),
            pltpu.VMEM((LANES, span * LANES), F32),
            pltpu.VMEM((tall, LANES), F32),
        ],
        compiler_params=params(),
        name="second_sums",
    )(w, sums, keep)

    left, right = pl.pallas_call(
        functools.partial(side_kernel, nd, nb),
        out_shape=(f(SIDE, total_rows), f(SIDE, total_rows)),
        in_specs=[VMEM] * 3,
        out_specs=(VMEM,) * 2,
        compiler_params=params(),
        name="sides",
    )(w, top_rim, bottom_rim)
    right_rim, left_rim = to_neighbours(left, right, "genome")
    strips = []
    for first, count in ((-5, 5), (0, cols), (cols, 5)):
        strips.append(
            pl.pallas_call(
                functools.partial(strip_kernel, nd, nb, first, count),
                out_shape=shape((count, total_rows, LANES), BF16),
                in_specs=[VMEM] * 5,
                out_specs=VMEM,
                scratch_shapes=[
                    pltpu.VMEM((nb, count * LANES), BF16),
                    pltpu.VMEM((total_rows, count * LANES), F32),
                ],
                compiler_params=params(),
                name="strips",
            )(w, top_rim, bottom_rim, left_rim, right_rim)
        )
    low, mid, high = strips
    sums = total(total(part, "genome"), "offset")

    padded = -(-total_rows // LANES) * LANES
    fan_len = fan_rows(nd)
    reach = -(-(fan_len + cols * (LANES - 1) + 2 * LANES) // LANES) * LANES
    near = 24
    near_reach = -(-(near + cols * (LANES - 1) + LANES) // LANES) * LANES
    own, fans, nears, diag = pl.pallas_call(
        functools.partial(third_kernel, nd, nb),
        out_shape=(f(cols, LANES), f(fan_len, LANES), f(near, LANES), f(8, padded)),
        in_specs=[VMEM] * 4,
        out_specs=(VMEM,) * 4,
        scratch_shapes=[
            pltpu.VMEM((tall + 8, LANES), F32),
            pltpu.VMEM((reach, LANES), F32),
            pltpu.VMEM((reach, LANES), F32),
            pltpu.VMEM((near_reach, LANES), F32),
            pltpu.VMEM((near_reach, LANES), F32),
            pltpu.VMEM((padded, 4 * LANES), BF16),
        ],
        compiler_params=params(),
        name="diagonal_sums",
    )(mid, sums, keep, bias)
    diag = total(diag, "genome")

    scratch = [
        pltpu.VMEM((cols + 10, total_rows, LANES), F32),
        pltpu.VMEM((cols + 8, total_rows, LANES), F32),
    ] + [pltpu.VMEM((cols, total_rows, LANES), F32)] * 3
    observed = pl.pallas_call(
        functools.partial(observed_kernel, nd, nb),
        out_shape=(f(cols, nd, LANES),) * 5,
        in_specs=[VMEM] * 5,
        out_specs=(VMEM,) * 5,
        scratch_shapes=scratch,
        compiler_params=params(60),
        name="observed",
    )(low, mid, high, nears, fans)

    score = pl.pallas_call(
        functools.partial(score_kernel, nd, nb),
        out_shape=f(nd, nb),
        in_specs=[VMEM] * 9,
        out_specs=VMEM,
        scratch_shapes=[pltpu.VMEM((padded, LANES), F32)] + scratch + [pltpu.VMEM((nb, nb), BF16)],
        compiler_params=params(60),
        name="score",
    )(low, mid, high, diag, *observed)
    return score, own.reshape(nb)


def solution(mesh):
    return jax.shard_map(
        on_device,
        mesh=mesh,
        in_specs=(P("offset", "genome"), P(), P()),
        out_specs=(P("offset", "genome"), P("genome")),
        check_vma=False,
    )
```

```python
import functools

import jax
import jax.numpy as jnp
from jax import lax
from jax.experimental import pallas as pl
from jax.experimental.pallas import tpu as pltpu
from jax.sharding import PartitionSpec as P

RIM = 16
STEP = 64
SIDE = 8
LANES = 128
F32 = jnp.float32
BF16 = jnp.bfloat16
TINY = 2.0**-126
VMEM = pl.BlockSpec(memory_space=pltpu.VMEM)
HBM = pl.BlockSpec(memory_space=pltpu.HBM)
ANY = pl.BlockSpec(memory_space=pl.ANY)
NT = (((1,), (1,)), ((), ()))


def params(mib=48):
    return pltpu.CompilerParams(vmem_limit_bytes=mib << 20)


def iota(shape, dim):
    return lax.broadcasted_iota(jnp.int32, shape, dim)


def split3(x):
    hi = x.astype(BF16)
    rest = x - hi.astype(F32)
    mid = rest.astype(BF16)
    low = (rest - mid.astype(F32)).astype(BF16)
    return hi, mid, low


def place(nd, nb):
    first = lax.axis_index("genome") * nb
    partner = first + lax.axis_index("offset") * nd
    return first // LANES, partner // LANES, partner % LANES


def roll(x, shift):
    length = x.shape[1]
    if isinstance(shift, int):
        shift = shift % length
        if shift == 0:
            return x
    return pltpu.roll(x, shift, 1)


def hankel(rows_ref, row0, lane0, tiles, out_ref):
    extra = 1 if lane0 is None else 2
    base = jnp.concatenate(
        [jnp.broadcast_to(rows_ref[pl.ds(row0 + t, 1), :], (8, LANES)) for t in range(tiles + extra)],
        axis=1,
    )
    length = base.shape[1]
    if lane0 is not None:
        base = roll(base, length - lane0)
    sub = iota(base.shape, 0)
    for bit in (1, 2, 4):
        base = jnp.where((sub & bit) > 0, roll(base, length - bit), base)
    for r in range(16):
        out_ref[8 * r : 8 * r + 8, : tiles * LANES] = roll(base, length - 8 * r)[:, : tiles * LANES]


def antidiagonal(acc_ref, tiles, lane0):
    extra = 1 if lane0 is None else 2
    pad = jnp.zeros((8, extra * LANES), F32)
    total = None
    for r in range(15, -1, -1):
        part = jnp.concatenate([acc_ref[8 * r : 8 * r + 8, : tiles * LANES], pad], axis=1)
        total = part if total is None else roll(total, 8) + part
    sub = iota(total.shape, 0)
    for bit in (4, 2, 1):
        total = jnp.where((sub & bit) > 0, roll(total, bit), total)
    total = jnp.sum(total, axis=0, keepdims=True)
    if lane0 is not None:
        total = roll(total, lane0)
    return total


def spread(own, partner, row_own, row_partner, placed_ref, out_ref):
    placed_ref[...] = jnp.zeros_like(placed_ref)
    for t in range(partner.shape[1] // LANES):
        placed_ref[pl.ds(row_partner + t, 1), :] = partner[:, t * LANES : (t + 1) * LANES]
    for c in range(own.shape[1] // LANES):
        placed_ref[pl.ds(row_own + c, 1), :] += own[:, c * LANES : (c + 1) * LANES]
    out_ref[...] = placed_ref[: out_ref.shape[0], :]


def sweep(nd, nb, entry, weigh_own, weigh_partner, acc_ref):
    cols = nb // LANES
    full, rest = nd // LANES, nd % LANES
    first_diag = lax.axis_index("offset") * nd
    sub = iota((16, LANES), 0)

    def body(ms, fresh, r, own):
        own = list(own)
        q0 = pl.multiple_of(16 * r, 16)
        sums = {}
        for m in ms:
            for c in range(cols):
                w = entry(m, c, q0)
                own[c] = own[c] + weigh_own(w, m, c, q0)
                g = weigh_partner(w, c)
                if m == 0:
                    g = jnp.where(sub + q0 + first_diag > 0, g, 0.0)
                sums[m + c] = sums[m + c] + g if m + c in sums else g
        for t, value in sums.items():
            tile = (pl.ds(q0, 16), slice(t * LANES, (t + 1) * LANES))
            acc_ref[tile] = value if fresh else acc_ref[tile] + value
        return tuple(own)

    own = tuple(jnp.zeros((16, LANES), F32) for _ in range(cols))
    if rest:
        acc_ref[...] = jnp.zeros_like(acc_ref)
    own = lax.fori_loop(0, 8, functools.partial(body, range(full), not rest), own)
    if rest:
        own = lax.fori_loop(0, rest // 16, functools.partial(body, [full], False), own)
    return jnp.concatenate([jnp.sum(o, axis=0, keepdims=True) for o in own], axis=1)


def keep_of(masked, rows):
    count = masked.shape[1]
    in_row = (jnp.broadcast_to(masked >> 7, (rows, count)) == iota((rows, count), 0))
    in_lane = (jnp.broadcast_to(masked & 127, (LANES, count)) == iota((LANES, count), 0))
    hits = lax.dot_general(
        in_row.astype(F32).astype(BF16), in_lane.astype(F32).astype(BF16), NT, preferred_element_type=F32
    )
    return jnp.where(hits > 0.0, 0.0, 1.0)


def first_kernel(nd, nb, bounds_hbm, x_hbm, masked_hbm, w_ref, part_ref, keep_ref, top_ref, bottom_ref,
                 codes_ref, hank_ref, acc_ref, placed_ref, bounds_ref, x_ref, masked_ref, sems):
    copies = [
        pltpu.make_async_copy(source, target, sems.at[k])
        for k, (source, target) in enumerate(
            ((masked_hbm, masked_ref), (bounds_hbm, bounds_ref), (x_hbm, x_ref))
        )
    ]
    for copy in copies:
        copy.start()
    copies[0].wait()
    copies[1].wait()
    rows = keep_ref.shape[0]
    cols = nb // LANES
    span = -(-nd // LANES) + cols - 1
    row_own, row_partner, lane0 = place(nd, nb)
    lane0 = lane0 if nd % LANES else None
    keep = keep_of(masked_ref[...], rows)
    keep_ref[...] = keep
    bins = iota((rows, LANES), 0) * LANES + iota((rows, LANES), 1)
    chrom = jnp.zeros((rows, LANES), F32)
    for k in range(bounds_ref.shape[0]):
        chrom = chrom + jnp.where(bins >= bounds_ref[k], 1.0, 0.0)
    codes_ref[...] = jnp.full_like(codes_ref, -2.0)
    codes_ref[:rows, :] = jnp.where(keep > 0.0, chrom, -2.0)
    hankel(codes_ref, row_partner, lane0, span, hank_ref)
    code_own = []
    for c in range(cols):
        code = codes_ref[pl.ds(row_own + c, 1), :]
        code = jnp.where(code < 0.0, -1.0, code)
        code_own.append(jnp.broadcast_to(code, (16, LANES)))
    copies[2].wait()

    def entry(m, c, q0):
        here = (pl.ds(q0 + m * LANES, 16), slice(c * LANES, (c + 1) * LANES))
        code = hank_ref[pl.ds(q0, 16), (m + c) * LANES : (m + c + 1) * LANES]
        value = jnp.maximum(x_ref[here].astype(F32), TINY)
        w = jnp.where(code == code_own[c], value, 0.0)
        w_ref[here] = w.astype(BF16)
        return w

    own = sweep(nd, nb, entry, lambda w, m, c, q0: w, lambda w, c: w, acc_ref)
    spread(own, antidiagonal(acc_ref, span, lane0), row_own, row_partner, placed_ref, part_ref)
    top_ref[...] = w_ref[:RIM, :].astype(F32)
    bottom_ref[...] = w_ref[nd - RIM :, :].astype(F32)


def next_bias(keep, bias, sums):
    level = jnp.sum(sums * keep, keepdims=True) / jnp.sum(keep, keepdims=True)
    safe = jnp.where(keep > 0.0, sums, 1.0)
    return jnp.where(keep > 0.0, bias * level / safe, 0.0)


def second_kernel(nd, nb, w_ref, sums_ref, keep_ref, part_ref, bias_ref, window_ref, hank_ref, acc_ref, placed_ref):
    rows = keep_ref.shape[0]
    cols = nb // LANES
    span = -(-nd // LANES) + cols - 1
    row_own, row_partner, lane0 = place(nd, nb)
    lane0 = lane0 if nd % LANES else None
    bias = next_bias(keep_ref[...], keep_ref[...], sums_ref[...])
    bias_ref[...] = bias
    window_ref[...] = jnp.zeros_like(window_ref)
    window_ref[:rows, :] = bias
    hankel(window_ref, row_partner, lane0, span, hank_ref)
    rows_own = [window_ref[pl.ds(row_own + c, 1), :] for c in range(cols)]
    own_bias = [jnp.broadcast_to(b, (16, LANES)) for b in rows_own]

    def entry(m, c, q0):
        return w_ref[pl.ds(q0 + m * LANES, 16), c * LANES : (c + 1) * LANES].astype(F32)

    def weigh_own(w, m, c, q0):
        return w * hank_ref[pl.ds(q0, 16), (m + c) * LANES : (m + c + 1) * LANES]

    own = sweep(nd, nb, entry, weigh_own, lambda w, c: w * own_bias[c], acc_ref)
    own = own * jnp.concatenate(rows_own, axis=1)
    partner = antidiagonal(acc_ref, span, lane0)
    tiles = partner.shape[1] // LANES
    partner = partner * jnp.concatenate(
        [window_ref[pl.ds(row_partner + t, 1), :] for t in range(tiles)], axis=1
    )
    spread(own, partner, row_own, row_partner, placed_ref, part_ref)


def side_kernel(nd, nb, w_ref, top_ref, bottom_ref, left_ref, right_ref):
    row, lane = iota((SIDE, LANES), 0), iota((SIDE, LANES), 1)
    for out_ref, pick, first in (
        (left_ref, row == lane, 0),
        (right_ref, row + LANES - SIDE == lane, nb - LANES),
    ):
        pick = pick.astype(F32).astype(BF16)
        cols = slice(first, first + LANES)
        block = jnp.concatenate(
            [w_ref[:, cols], bottom_ref[:, cols].astype(BF16), top_ref[:, cols].astype(BF16)], axis=0
        )
        out_ref[...] = lax.dot_general(pick, block, NT, preferred_element_type=F32)


def strip_kernel(nd, nb, first, count, w_ref, top_ref, bottom_ref, left_ref, right_ref, out_ref, perm_ref, side_ref):
    stride = nb // LANES
    width = count * LANES
    lane = iota((nb, LANES), 1)
    row = iota((nb, LANES), 0)
    for k in range(count):
        hit = row == lane * stride + (first + k)
        perm_ref[:, k * LANES : (k + 1) * LANES] = hit.astype(F32).astype(BF16)
    perm = perm_ref[...]
    rims = []
    row, lane = iota((2 * SIDE, LANES), 0), iota((2 * SIDE, LANES), 1)
    bin_of = jnp.where(row < SIDE, row - SIDE, row - SIDE + nb)
    for k in range(count):
        rims.append((bin_of == lane * stride + (first + k)).astype(F32).astype(BF16))
    rims = jnp.concatenate(rims, axis=1)
    sides = jnp.concatenate([left_ref[...], right_ref[...]], axis=0).astype(BF16)
    outer = first < 0 or first + count > stride
    if outer:
        side_ref[...] = lax.dot_general(
            sides, rims, (((0,), (0,)), ((), ())), preferred_element_type=F32
        )

    def emit(block, at, side_at, rows):
        value = jnp.dot(block, perm, preferred_element_type=F32)
        if outer:
            value = value + side_ref[side_at : side_at + rows, :]
        for k in range(count):
            out_ref[k, at : at + rows, :] = value[:, k * LANES : (k + 1) * LANES].astype(BF16)

    emit(top_ref[...].astype(BF16), 0, nd + RIM, RIM)
    emit(bottom_ref[...].astype(BF16), nd + RIM, nd, RIM)
    emit(w_ref[...], RIM, 0, nd)


def unstrip_kernel(nb, out_ref):
    stride = nb // LANES
    row, lane = iota((LANES, nb), 0), iota((LANES, nb), 1)
    for s in range(stride):
        out_ref[s * LANES : (s + 1) * LANES, :] = (lane == row * stride + s).astype(F32).astype(BF16)


def column(row, out_ref, at):
    eye = iota((LANES, LANES), 0) == iota((LANES, LANES), 1)
    diag = jnp.where(eye, jnp.broadcast_to(row, (LANES, LANES)), 0.0)
    value = jnp.dot(
        jnp.concatenate(split3(diag), axis=1), jnp.ones((3 * LANES, LANES), BF16), preferred_element_type=F32
    )
    out_ref[at : at + LANES, :] = value


def fan(col_ref, other_ref, start, rows, stride, out_ref):
    lane = {}
    source, offset = col_ref, start
    target = other_ref
    for bit in (64, 32, 16, 8, 4, 2, 1):
        need = rows + stride * (bit - 1)
        need = -(-need // 8) * 8
        if bit == 1:
            target = out_ref
        step = 32 if need >= 32 else 8

        def move(at, size, source=source, target=target, offset=offset, bit=bit):
            low = source[pl.ds(offset + at, size), :]
            high = source[pl.ds(offset + at + stride * bit, size), :]
            odd = (iota((size, LANES), 1) & bit) > 0
            target[pl.ds(at, size), :] = jnp.where(odd, high, low)

        def body(i, _, move=move):
            move(pl.multiple_of(i * 32, 32), 32)
            return 0

        lax.fori_loop(0, need // 32, body, 0)
        for at in range(need // 32 * 32, need, 8):
            move(at, 8)
        source, target, offset = target, source, 0


def fan_rows(nd):
    return nd + 2 * RIM + 32


def third_kernel(nd, nb, mid_ref, sums_ref, keep_ref, bias_ref, own_ref, fan_ref, near_ref, diag_ref,
                 window_ref, col_ref, other_ref, ncol_ref, nother_ref, total_ref):
    rows = keep_ref.shape[0]
    cols = nb // LANES
    stride = cols
    row_own, row_partner, lane0 = place(nd, nb)
    bias = next_bias(keep_ref[...], bias_ref[...], sums_ref[...])
    window_ref[...] = jnp.zeros_like(window_ref)
    window_ref[8 : 8 + rows, :] = bias
    for c in range(cols):
        own_ref[c : c + 1, :] = window_ref[pl.ds(8 + row_own + c, 1), :]
    tiles = col_ref.shape[0] // LANES
    for t in range(tiles):
        column(window_ref[pl.ds(7 + row_partner + t, 1), :], col_ref, t * LANES)
    start = LANES - RIM - 8
    if nd % LANES:
        start = start + lane0
    fan(col_ref, other_ref, start, fan_rows(nd), stride, fan_ref)
    for t in range(ncol_ref.shape[0] // LANES):
        column(window_ref[pl.ds(7 + row_own + t, 1), :], ncol_ref, t * LANES)
    fan(ncol_ref, nother_ref, LANES - 8, near_ref.shape[0], stride, near_ref)
    total_rows = nd + 2 * RIM
    step = 32

    def body(i, _):
        r0 = pl.multiple_of(i * step, step)
        total, count = None, None
        for s in range(stride):
            w = mid_ref[s, pl.ds(r0, step), :].astype(F32)
            b = w * jnp.broadcast_to(near_ref[8 + s : 9 + s, :], (step, LANES)) * fan_ref[pl.ds(r0 + 8 + s, step), :]
            v = jnp.where(w > 0.0, 1.0, 0.0)
            total = b if total is None else total + b
            count = v if count is None else count + v
        hi, mid, low = split3(total)
        for k, part in enumerate((hi, mid, low, count.astype(BF16))):
            total_ref[pl.ds(r0, step), k * LANES : (k + 1) * LANES] = part
        return 0

    lax.fori_loop(0, total_rows // step, body, 0)
    ones = jnp.ones((8, 3 * LANES), BF16)
    padded = total_ref.shape[0]
    tiles = padded // LANES
    if padded > total_rows:
        total_ref[total_rows:, :] = jnp.zeros((padded - total_rows, 4 * LANES), BF16)
    sums = lax.dot_general(ones, total_ref[:, : 3 * LANES], NT, preferred_element_type=F32)
    counts = lax.dot_general(ones[:, :LANES], total_ref[:, 3 * LANES :], NT, preferred_element_type=F32)
    for t in range(tiles):
        diag_ref[t : t + 1, :] = sums[0:1, t * LANES : (t + 1) * LANES]
        diag_ref[tiles + t : tiles + t + 1, :] = counts[0:1, t * LANES : (t + 1) * LANES]


def over(start, count, step, run):
    steps = count // step
    if steps > 0:

        def body(i, _):
            run(pl.multiple_of(i * step + start, 8), step)
            return 0

        lax.fori_loop(0, steps, body, 0)
    if count % step:
        run(start + steps * step, count % step)


def filter_kernel(nd, nb, chunk, step, low_ref, mid_ref, high_ref, near_ref, fan_ref, diag_ref, perm_ref, out_ref,
                  col_ref, xo_ref, xe_ref, po_ref, pe_ref, ho_ref, he_ref, uo_ref, ue_ref,
                  lo_ref, le_ref, wo_ref, we_ref, to_ref, te_ref):
    stride = nb // LANES
    strips = {}
    for s in range(-5, 0):
        strips[s] = (low_ref, s + 5)
    for s in range(stride):
        strips[s] = (mid_ref, s)
    for s in range(stride, stride + 5):
        strips[s] = (high_ref, s - stride)
    base = pl.multiple_of(pl.program_id(0) * chunk, 32)

    @pl.when(pl.program_id(0) == 0)
    def _():
        tiles = diag_ref.shape[0] // 2
        expected = diag_ref[:tiles, :] / jnp.maximum(diag_ref[tiles:, :], 1.0)
        for t in range(tiles):
            column(expected[t : t + 1, :], col_ref, t * LANES)

    def fill(r0, size):
        e = col_ref[pl.ds(base + r0, size), :]
        for s, (ref, k) in strips.items():
            w = ref[k, pl.ds(base + r0, size), :].astype(F32)
            near = jnp.broadcast_to(near_ref[8 + s : 9 + s, :], (size, LANES))
            xo_ref[s + 5, pl.ds(r0, size), :] = w * near * fan_ref[pl.ds(base + r0 + 8 + s, size), :]
            xe_ref[s + 5, pl.ds(r0, size), :] = jnp.where(w > 0.0, e, 0.0)

    over(0, chunk + 2 * RIM, 32, fill)
    observed = (xo_ref, po_ref, ho_ref, uo_ref, lo_ref, wo_ref, to_ref)
    expected = (xe_ref, pe_ref, he_ref, ue_ref, le_ref, we_ref, te_ref)

    def pairs(r0, size):
        for s in range(-4, stride + 3):
            for x, p, *_ in (observed, expected):
                p[s + 4, pl.ds(r0, size), :] = x[s + 5, pl.ds(r0, size), :] + x[s + 6, pl.ds(r0 - 1, size), :]

    over(8, chunk + 24, step, pairs)

    def mix(r0, size):
        for s in range(stride):
            for x, p, h, u, l, w, t in (observed, expected):
                here = (s, pl.ds(r0, size), slice(None))
                at = lambda ref, k, shift: ref[k, pl.ds(r0 + shift, size), :]
                hp = at(p, s + 7, -3) + at(x, s + 10, -5)
                hm = at(p, s, 4) + at(x, s, 5)
                lp = hp + at(p, s + 5, -1)
                h[here] = hp
                u[here] = hp + hm
                l[here] = lp
                w[here] = lp + (hm + at(p, s + 2, 2))
                t[here] = at(p, s + 4, 0) + at(x, s + 4, 1)

    over(8, chunk + 16, step, mix)

    def runs(r0, size):
        for s in range(stride):
            for _, _, _, _, _, w, t in (observed, expected):
                for ref in (w, t):
                    at = lambda shift: ref[s, pl.ds(r0 + shift, size), :]
                    ref[s, pl.ds(r0, size), :] = at(0) + at(1) + at(2)

    over(8, chunk + 16, step, runs)

    def score(r0, size):
        e = col_ref[pl.ds(base + r0, size), :]
        inverse = 1.0 / e
        for s in range(stride):
            sums = []
            for x, p, h, u, l, w, t in (observed, expected):
                at = lambda ref, shift: ref[s, pl.ds(r0 + shift, size), :]
                below, above = at(u, -1), at(u, 1)
                donut = (at(w, -5) + at(w, 3)) + ((at(u, -2) + below) + (above + at(u, 2)))
                lower = (at(l, -5) + at(l, -4) + at(l, -3)) + (at(h, -2) + at(h, -1))
                sums.append((donut, lower, at(t, -5) + at(t, 3), below + at(u, 0) + above))
            least = None
            for seen, hoped in zip(*sums):
                ratio = (hoped + e) / (seen + e)
                least = ratio if least is None else jnp.minimum(least, ratio)
            value = least * (xo_ref[s + 5, pl.ds(r0, size), :] * inverse)
            value = jnp.where(xe_ref[s + 5, pl.ds(r0, size), :] > 0.0, value, 0.0)
            hi = value.astype(BF16)
            low = (value - hi.astype(F32)).astype(BF16)
            perm = perm_ref[s * LANES : (s + 1) * LANES, :]
            placed = jnp.dot(
                jnp.concatenate([hi, low], axis=1), jnp.concatenate([perm, perm], axis=0), preferred_element_type=F32
            )
            here = pl.ds(r0 - RIM, size)
            out_ref[here, :] = placed if s == 0 else out_ref[here, :] + placed

    over(RIM, chunk, chunk // 2, score)


def tie(x, state, names):
    x, values = lax.optimization_barrier((x, tuple(state[name] for name in names)))
    state.update(zip(names, values))
    return x


def total(x, axes, state=None, tasks={}, due={}):
    rounds = []
    for axis in axes:
        size, bit = lax.axis_size(axis), 1
        while bit < size:
            rounds.append((axis, [(i, i ^ bit) for i in range(size)]))
            bit *= 2
    for k, (axis, pairs) in enumerate(rounds):
        if k in tasks:
            x = tie(x, state, tasks[k][0])
        came = lax.ppermute(x, axis, pairs)
        if k in tasks:
            names, task = tasks[k]
            state.update(task(*[state[name] for name in names]))
        x = x + came
        if k in due:
            x = tie(x, state, due[k])
    return x


def shifted(x, axis, step):
    size = lax.axis_size(axis)
    pairs = [(i, i + 1) for i in range(size - 1)]
    return lax.ppermute(x, axis, pairs if step > 0 else [(j, i) for i, j in pairs])


def on_device(contacts, masked_bins, chrom_bounds):
    nd, nb = contacts.shape
    cols = nb // LANES
    bins = nb * lax.axis_size("genome")
    band = nd * lax.axis_size("offset")
    rows = bins // LANES
    span = -(-nd // LANES) + cols - 1
    tall = rows + -(-band // LANES) + 24
    total_rows = nd + 2 * RIM
    shape = jax.ShapeDtypeStruct
    f = lambda *dims: shape(dims, F32)

    w, part, keep, top, bottom = pl.pallas_call(
        functools.partial(first_kernel, nd, nb),
        out_shape=(shape((nd, nb), BF16), f(rows, LANES), f(rows, LANES), f(RIM, nb), f(RIM, nb)),
        in_specs=[HBM] * 3,
        out_specs=(VMEM,) * 5,
        scratch_shapes=[
            pltpu.VMEM((tall, LANES), F32),
            pltpu.VMEM((LANES, span * LANES), F32),
            pltpu.VMEM((LANES, span * LANES), F32),
            pltpu.VMEM((tall, LANES), F32),
            pltpu.SMEM(chrom_bounds.shape, jnp.int32),
            pltpu.VMEM((nd, nb), BF16),
            pltpu.VMEM((1,) + masked_bins.shape, jnp.int32),
            pltpu.SemaphoreType.DMA((3,)),
        ],
        compiler_params=params(12),
        name="first_sums",
    )(*(pltpu.with_memory_space_constraint(a, pltpu.HBM) for a in (chrom_bounds, contacts, masked_bins.reshape(1, -1))))

    def sides(w, above, below):
        return pl.pallas_call(
            functools.partial(side_kernel, nd, nb),
            out_shape=(f(SIDE, total_rows), f(SIDE, total_rows)),
            in_specs=[VMEM] * 3,
            out_specs=(VMEM,) * 2,
            compiler_params=params(16),
            name="sides",
        )(w, above, below)

    def first_side(w, above, below):
        left, right = sides(w, above, below)
        return dict(right=right, after=shifted(left, "genome", -1))

    state = dict(w=w, top=top, bottom=bottom)
    tasks = {
        0: (("bottom",), lambda bottom: dict(above=shifted(bottom, "offset", 1))),
        1: (("top",), lambda top: dict(below=shifted(top, "offset", -1))),
        3: (("w", "above", "below"), first_side),
    }
    sums = total(part, ("genome", "offset"), state, tasks, {1: ("above",), 2: ("below",)})
    w = state["w"]

    part, bias = pl.pallas_call(
        functools.partial(second_kernel, nd, nb),
        out_shape=(f(rows, LANES), f(rows, LANES)),
        in_specs=[VMEM] * 3,
        out_specs=(VMEM,) * 2,
        scratch_shapes=[
            pltpu.VMEM((tall, LANES), F32),
            pltpu.VMEM((LANES, span * LANES), F32),
            pltpu.VMEM((LANES, span * LANES), F32),
            pltpu.VMEM((tall, LANES), F32),
        ],
        compiler_params=params(),
        name="second_sums",
    )(w, sums, keep)

    def strip(name, first, count):
        def run(*operands):
            strips = pl.pallas_call(
                functools.partial(strip_kernel, nd, nb, first, count),
                out_shape=shape((count, total_rows, LANES), BF16),
                in_specs=[VMEM] * 5,
                out_specs=VMEM,
                scratch_shapes=[
                    pltpu.VMEM((nb, count * LANES), BF16),
                    pltpu.VMEM((total_rows, count * LANES), F32),
                ],
                compiler_params=params(24),
                name="strips",
            )(*operands)
            return {name: strips}

        return ("w", "above", "below") + (("above", "below") if name == "mid" else ("before", "after")), run

    def back(_, right):
        matrix = pl.pallas_call(
            functools.partial(unstrip_kernel, nb),
            out_shape=shape((nb, nb), BF16),
            out_specs=VMEM,
            compiler_params=params(8),
            name="unstrip",
        )()
        return dict(perm=matrix, before=shifted(right, "genome", 1))

    tasks = {
        0: (("keep", "right"), back),
        2: strip("mid", 0, cols),
        3: strip("high", cols, 5),
        4: strip("low", -5, 5),
    }
    state["keep"] = keep
    due = {0: ("perm", "after"), 2: ("mid", "before"), 3: ("high",), 4: ("low",)}
    sums = total(part, ("genome", "offset"), state, tasks, due)
    low, high, mid, perm, keep = (state[name] for name in ("low", "high", "mid", "perm", "keep"))

    padded = -(-total_rows // LANES) * LANES
    fan_len = fan_rows(nd)
    reach = -(-(fan_len + cols * (LANES - 1) + 2 * LANES) // LANES) * LANES
    near = 24
    near_reach = -(-(near + cols * (LANES - 1) + LANES) // LANES) * LANES
    own, fans, nears, diag = pl.pallas_call(
        functools.partial(third_kernel, nd, nb),
        out_shape=(f(cols, LANES), f(fan_len, LANES), f(near, LANES), f(2 * padded // LANES, LANES)),
        in_specs=[VMEM] * 4,
        out_specs=(VMEM,) * 4,
        scratch_shapes=[
            pltpu.VMEM((tall + 8, LANES), F32),
            pltpu.VMEM((reach, LANES), F32),
            pltpu.VMEM((reach, LANES), F32),
            pltpu.VMEM((near_reach, LANES), F32),
            pltpu.VMEM((near_reach, LANES), F32),
            pltpu.VMEM((padded, 4 * LANES), BF16),
        ],
        compiler_params=params(),
        name="diagonal_sums",
    )(mid, sums, keep, bias)
    diag = total(diag, ("genome",))

    chunk = next(c for c in (320, 256, 128, 64, 32) if nd % c == 0)
    tall = chunk + 2 * RIM
    twice = lambda tiles: [pltpu.VMEM((tiles, tall, LANES), F32)] * 2
    whole = lambda a: pl.BlockSpec(a.shape, lambda i: (0,) * a.ndim)
    operands = (low, mid, high, nears, fans, diag, perm)
    score = pl.pallas_call(
        functools.partial(filter_kernel, nd, nb, chunk, STEP),
        out_shape=f(nd, nb),
        grid=(nd // chunk,),
        in_specs=[whole(a) for a in operands],
        out_specs=pl.BlockSpec((chunk, nb), lambda i: (i, 0)),
        scratch_shapes=[pltpu.VMEM((padded, LANES), F32)]
        + twice(cols + 10) + twice(cols + 7) + twice(cols) + twice(cols) + twice(cols) + twice(cols) + twice(cols)
        ,
        compiler_params=params(44),
        name="score",
    )(*operands)
    return score, own.reshape(nb)


def solution(mesh):
    return jax.shard_map(
        on_device,
        mesh=mesh,
        in_specs=(P("offset", "genome"), P(), P()),
        out_specs=(P("offset", "genome"), P("genome")),
        check_vma=False,
    )
```

```python
import functools
import math

import jax
import jax.numpy as jnp
from jax import lax
from jax.experimental import pallas as pl
from jax.experimental.pallas import tpu as pltpu
from jax.sharding import PartitionSpec as P

RIM = 16
STEP = 176
SIDE = 8
LANES = 128
F32 = jnp.float32
BF16 = jnp.bfloat16
TINY = 2.0**-126
VMEM = pl.BlockSpec(memory_space=pltpu.VMEM)
HBM = pl.BlockSpec(memory_space=pltpu.HBM)
ANY = pl.BlockSpec(memory_space=pl.ANY)
NT = (((1,), (1,)), ((), ()))


def params(mib=48):
    return pltpu.CompilerParams(vmem_limit_bytes=mib << 20)


def iota(shape, dim):
    return lax.broadcasted_iota(jnp.int32, shape, dim)


def split3(x):
    hi = x.astype(BF16)
    rest = x - hi.astype(F32)
    mid = rest.astype(BF16)
    low = (rest - mid.astype(F32)).astype(BF16)
    return hi, mid, low


def place(nd, nb):
    first = lax.axis_index("genome") * nb
    partner = first + lax.axis_index("offset") * nd
    return first // LANES, partner // LANES, partner % LANES


def roll(x, shift):
    length = x.shape[1]
    if isinstance(shift, int):
        shift = shift % length
        if shift == 0:
            return x
    return pltpu.roll(x, shift, 1)


def hankel(rows_ref, row0, lane0, tiles, out_ref):
    extra = 1 if lane0 is None else 2
    base = jnp.concatenate(
        [jnp.broadcast_to(rows_ref[pl.ds(row0 + t, 1), :], (8, LANES)) for t in range(tiles + extra)],
        axis=1,
    )
    length = base.shape[1]
    if lane0 is not None:
        base = roll(base, length - lane0)
    sub = iota(base.shape, 0)
    for bit in (1, 2, 4):
        base = jnp.where((sub & bit) > 0, roll(base, length - bit), base)
    for r in range(16):
        out_ref[8 * r : 8 * r + 8, : tiles * LANES] = roll(base, length - 8 * r)[:, : tiles * LANES]


def antidiagonal(acc_ref, tiles, lane0):
    extra = 1 if lane0 is None else 2
    pad = jnp.zeros((8, extra * LANES), F32)
    total = None
    for r in range(15, -1, -1):
        part = jnp.concatenate([acc_ref[8 * r : 8 * r + 8, : tiles * LANES], pad], axis=1)
        total = part if total is None else roll(total, 8) + part
    sub = iota(total.shape, 0)
    for bit in (4, 2, 1):
        total = jnp.where((sub & bit) > 0, roll(total, bit), total)
    total = jnp.sum(total, axis=0, keepdims=True)
    if lane0 is not None:
        total = roll(total, lane0)
    return total


def spread(own, partner, row_own, row_partner, placed_ref, out_ref):
    placed_ref[...] = jnp.zeros_like(placed_ref)
    for t in range(partner.shape[1] // LANES):
        placed_ref[pl.ds(row_partner + t, 1), :] = partner[:, t * LANES : (t + 1) * LANES]
    for c in range(own.shape[1] // LANES):
        placed_ref[pl.ds(row_own + c, 1), :] += own[:, c * LANES : (c + 1) * LANES]
    out_ref[...] = placed_ref[: out_ref.shape[0], :]


def sweep(nd, nb, entry, weigh_own, weigh_partner, acc_ref):
    cols = nb // LANES
    full, rest = nd // LANES, nd % LANES
    first_diag = lax.axis_index("offset") * nd
    sub = iota((16, LANES), 0)

    def body(ms, fresh, r, own):
        own = list(own)
        q0 = pl.multiple_of(16 * r, 16)
        sums = {}
        for m in ms:
            for c in range(cols):
                w = entry(m, c, q0)
                own[c] = own[c] + weigh_own(w, m, c, q0)
                g = weigh_partner(w, c)
                if m == 0:
                    g = jnp.where(sub + q0 + first_diag > 0, g, 0.0)
                sums[m + c] = sums[m + c] + g if m + c in sums else g
        for t, value in sums.items():
            tile = (pl.ds(q0, 16), slice(t * LANES, (t + 1) * LANES))
            acc_ref[tile] = value if fresh else acc_ref[tile] + value
        return tuple(own)

    own = tuple(jnp.zeros((16, LANES), F32) for _ in range(cols))
    if rest:
        acc_ref[...] = jnp.zeros_like(acc_ref)
    own = lax.fori_loop(0, 8, functools.partial(body, range(full), not rest), own)
    if rest:
        own = lax.fori_loop(0, rest // 16, functools.partial(body, [full], False), own)
    return jnp.concatenate([jnp.sum(o, axis=0, keepdims=True) for o in own], axis=1)


def keep_of(masked, rows):
    count = masked.shape[1]
    in_row = (jnp.broadcast_to(masked >> 7, (rows, count)) == iota((rows, count), 0))
    in_lane = (jnp.broadcast_to(masked & 127, (LANES, count)) == iota((LANES, count), 0))
    hits = lax.dot_general(
        in_row.astype(F32).astype(BF16), in_lane.astype(F32).astype(BF16), NT, preferred_element_type=F32
    )
    return jnp.where(hits > 0.0, 0.0, 1.0)


def first_kernel(nd, nb, bounds_hbm, x_hbm, masked_hbm, w_ref, part_ref, keep_ref, top_ref, bottom_ref,
                 codes_ref, hank_ref, acc_ref, placed_ref, bounds_ref, x_ref, masked_ref, sems):
    copies = [
        pltpu.make_async_copy(source, target, sems.at[k])
        for k, (source, target) in enumerate(
            ((masked_hbm, masked_ref), (bounds_hbm, bounds_ref), (x_hbm, x_ref))
        )
    ]
    for copy in copies:
        copy.start()
    copies[0].wait()
    copies[1].wait()
    rows = keep_ref.shape[0]
    cols = nb // LANES
    span = -(-nd // LANES) + cols - 1
    row_own, row_partner, lane0 = place(nd, nb)
    lane0 = lane0 if nd % LANES else None
    keep = keep_of(masked_ref[...], rows)
    keep_ref[...] = keep
    bins = iota((rows, LANES), 0) * LANES + iota((rows, LANES), 1)
    chrom = jnp.zeros((rows, LANES), F32)
    for k in range(bounds_ref.shape[0]):
        chrom = chrom + jnp.where(bins >= bounds_ref[k], 1.0, 0.0)
    codes_ref[...] = jnp.full_like(codes_ref, -2.0)
    codes_ref[:rows, :] = jnp.where(keep > 0.0, chrom, -2.0)
    hankel(codes_ref, row_partner, lane0, span, hank_ref)
    code_own = []
    for c in range(cols):
        code = codes_ref[pl.ds(row_own + c, 1), :]
        code = jnp.where(code < 0.0, -1.0, code)
        code_own.append(jnp.broadcast_to(code, (16, LANES)))
    copies[2].wait()

    def entry(m, c, q0):
        here = (pl.ds(q0 + m * LANES, 16), slice(c * LANES, (c + 1) * LANES))
        code = hank_ref[pl.ds(q0, 16), (m + c) * LANES : (m + c + 1) * LANES]
        value = jnp.maximum(x_ref[here].astype(F32), TINY)
        w = jnp.where(code == code_own[c], value, 0.0)
        w_ref[here] = w.astype(BF16)
        return w

    own = sweep(nd, nb, entry, lambda w, m, c, q0: w, lambda w, c: w, acc_ref)
    spread(own, antidiagonal(acc_ref, span, lane0), row_own, row_partner, placed_ref, part_ref)
    top_ref[...] = w_ref[:RIM, :].astype(F32)
    bottom_ref[...] = w_ref[nd - RIM :, :].astype(F32)


def next_bias(keep, bias, sums):
    level = jnp.sum(sums * keep, keepdims=True) / jnp.sum(keep, keepdims=True)
    safe = jnp.where(keep > 0.0, sums, 1.0)
    return jnp.where(keep > 0.0, bias * level / safe, 0.0)


def second_kernel(nd, nb, w_ref, sums_ref, keep_ref, part_ref, bias_ref, window_ref, hank_ref, acc_ref, placed_ref):
    rows = keep_ref.shape[0]
    cols = nb // LANES
    span = -(-nd // LANES) + cols - 1
    row_own, row_partner, lane0 = place(nd, nb)
    lane0 = lane0 if nd % LANES else None
    bias = next_bias(keep_ref[...], keep_ref[...], sums_ref[...])
    bias_ref[...] = bias
    window_ref[...] = jnp.zeros_like(window_ref)
    window_ref[:rows, :] = bias
    hankel(window_ref, row_partner, lane0, span, hank_ref)
    rows_own = [window_ref[pl.ds(row_own + c, 1), :] for c in range(cols)]
    own_bias = [jnp.broadcast_to(b, (16, LANES)) for b in rows_own]

    def entry(m, c, q0):
        return w_ref[pl.ds(q0 + m * LANES, 16), c * LANES : (c + 1) * LANES].astype(F32)

    def weigh_own(w, m, c, q0):
        return w * hank_ref[pl.ds(q0, 16), (m + c) * LANES : (m + c + 1) * LANES]

    own = sweep(nd, nb, entry, weigh_own, lambda w, c: w * own_bias[c], acc_ref)
    own = own * jnp.concatenate(rows_own, axis=1)
    partner = antidiagonal(acc_ref, span, lane0)
    tiles = partner.shape[1] // LANES
    partner = partner * jnp.concatenate(
        [window_ref[pl.ds(row_partner + t, 1), :] for t in range(tiles)], axis=1
    )
    spread(own, partner, row_own, row_partner, placed_ref, part_ref)


def side_kernel(nd, nb, w_ref, top_ref, bottom_ref, left_ref, right_ref):
    row, lane = iota((SIDE, LANES), 0), iota((SIDE, LANES), 1)
    for out_ref, pick, first in (
        (left_ref, row == lane, 0),
        (right_ref, row + LANES - SIDE == lane, nb - LANES),
    ):
        pick = pick.astype(F32).astype(BF16)
        cols = slice(first, first + LANES)
        block = jnp.concatenate(
            [w_ref[:, cols], bottom_ref[:, cols].astype(BF16), top_ref[:, cols].astype(BF16)], axis=0
        )
        out_ref[...] = lax.dot_general(pick, block, NT, preferred_element_type=F32)


def strip_kernel(nd, nb, first, count, w_ref, top_ref, bottom_ref, left_ref, right_ref, out_ref, perm_ref, side_ref):
    stride = nb // LANES
    width = count * LANES
    lane = iota((nb, LANES), 1)
    row = iota((nb, LANES), 0)
    for k in range(count):
        hit = row == lane * stride + (first + k)
        perm_ref[:, k * LANES : (k + 1) * LANES] = hit.astype(F32).astype(BF16)
    perm = perm_ref[...]
    rims = []
    row, lane = iota((2 * SIDE, LANES), 0), iota((2 * SIDE, LANES), 1)
    bin_of = jnp.where(row < SIDE, row - SIDE, row - SIDE + nb)
    for k in range(count):
        rims.append((bin_of == lane * stride + (first + k)).astype(F32).astype(BF16))
    rims = jnp.concatenate(rims, axis=1)
    sides = jnp.concatenate([left_ref[...], right_ref[...]], axis=0).astype(BF16)
    outer = first < 0 or first + count > stride
    if outer:
        side_ref[...] = lax.dot_general(
            sides, rims, (((0,), (0,)), ((), ())), preferred_element_type=F32
        )

    def emit(block, at, side_at, rows):
        value = jnp.dot(block, perm, preferred_element_type=F32)
        if outer:
            value = value + side_ref[side_at : side_at + rows, :]
        for k in range(count):
            out_ref[k, at : at + rows, :] = value[:, k * LANES : (k + 1) * LANES].astype(BF16)

    emit(top_ref[...].astype(BF16), 0, nd + RIM, RIM)
    emit(bottom_ref[...].astype(BF16), nd + RIM, nd, RIM)
    emit(w_ref[...], RIM, 0, nd)


def unstrip_kernel(nb, out_ref):
    stride = nb // LANES
    row, lane = iota((LANES, nb), 0), iota((LANES, nb), 1)
    for s in range(stride):
        out_ref[s * LANES : (s + 1) * LANES, :] = (lane == row * stride + s).astype(F32).astype(BF16)


def columns(rows, out_ref):
    eye = iota((LANES, LANES), 0) == iota((LANES, LANES), 1)
    blocks = []
    for row in rows:
        parts = [jnp.where(eye, jnp.broadcast_to(part.astype(F32), (LANES, LANES)), 0.0) for part in split3(row)]
        blocks.append(jnp.concatenate([part.astype(BF16) for part in parts], axis=1))
    out_ref[...] = jnp.dot(
        jnp.concatenate(blocks, axis=0), jnp.ones((3 * LANES, LANES), BF16), preferred_element_type=F32
    )


def fan(col_ref, other_ref, start, rows, stride, out_ref):
    lane = {}
    source, offset = col_ref, start
    target = other_ref
    for bit in (64, 32, 16, 8, 4, 2, 1):
        need = rows + stride * (bit - 1)
        need = -(-need // 8) * 8
        if bit == 1:
            target = out_ref
        def move(at, size, source=source, target=target, offset=offset, bit=bit):
            low = source[pl.ds(offset + at, size), :]
            high = source[pl.ds(offset + at + stride * bit, size), :]
            odd = (iota((size, LANES), 1) & bit) > 0
            target[pl.ds(at, size), :] = jnp.where(odd, high, low)

        over(0, need, 208 if need > 208 else need, move)
        source, target, offset = target, source, 0


def fan_rows(nd):
    return nd + 2 * RIM + 32


def third_kernel(nd, nb, mid_ref, sums_ref, keep_ref, bias_ref, own_ref, fan_ref, near_ref, diag_ref,
                 window_ref, col_ref, other_ref, ncol_ref, nother_ref, total_ref):
    rows = keep_ref.shape[0]
    cols = nb // LANES
    stride = cols
    row_own, row_partner, lane0 = place(nd, nb)
    bias = next_bias(keep_ref[...], bias_ref[...], sums_ref[...])
    window_ref[...] = jnp.zeros_like(window_ref)
    window_ref[8 : 8 + rows, :] = bias
    for c in range(cols):
        own_ref[c : c + 1, :] = window_ref[pl.ds(8 + row_own + c, 1), :]
    tiles = col_ref.shape[0] // LANES
    columns([window_ref[pl.ds(7 + row_partner + t, 1), :] for t in range(tiles)], col_ref)
    start = LANES - RIM - 8
    if nd % LANES:
        start = start + lane0
    fan(col_ref, other_ref, start, fan_rows(nd), stride, fan_ref)
    columns([window_ref[pl.ds(7 + row_own + t, 1), :] for t in range(ncol_ref.shape[0] // LANES)], ncol_ref)
    fan(ncol_ref, nother_ref, LANES - 8, near_ref.shape[0], stride, near_ref)
    total_rows = nd + 2 * RIM

    def add(r0, size):
        total, count = None, None
        for s in range(stride):
            w = mid_ref[s, pl.ds(r0, size), :].astype(F32)
            near = jnp.broadcast_to(near_ref[8 + s : 9 + s, :], (size, LANES))
            b = w * near * fan_ref[pl.ds(r0 + 8 + s, size), :]
            v = jnp.where(w > 0.0, 1.0, 0.0)
            total = b if total is None else total + b
            count = v if count is None else count + v
        hi, mid, low = split3(total)
        for k, part in enumerate((hi, mid, low, count.astype(BF16))):
            total_ref[pl.ds(r0, size), k * LANES : (k + 1) * LANES] = part

    over(0, total_rows, 160, add)
    ones = jnp.ones((8, 3 * LANES), BF16)
    padded = total_ref.shape[0]
    tiles = padded // LANES
    if padded > total_rows:
        total_ref[total_rows:, :] = jnp.zeros((padded - total_rows, 4 * LANES), BF16)
    sums = lax.dot_general(ones, total_ref[:, : 3 * LANES], NT, preferred_element_type=F32)
    counts = lax.dot_general(ones[:, :LANES], total_ref[:, 3 * LANES :], NT, preferred_element_type=F32)
    for t in range(tiles):
        diag_ref[t : t + 1, :] = sums[0:1, t * LANES : (t + 1) * LANES]
        diag_ref[tiles + t : tiles + t + 1, :] = counts[0:1, t * LANES : (t + 1) * LANES]


def over(start, count, step, run):
    steps = count // step
    if steps > 0:

        def body(i, _):
            run(pl.multiple_of(i * step + start, math.gcd(start, step)), step)
            return 0

        lax.fori_loop(0, steps, body, 0)
    if count % step:
        run(start + steps * step, count % step)


def strips_of(stride, low_ref, mid_ref, high_ref):
    strips = {}
    for s in range(-5, 0):
        strips[s] = (low_ref, s + 5)
    for s in range(stride):
        strips[s] = (mid_ref, s)
    for s in range(stride, stride + 5):
        strips[s] = (high_ref, s - stride)
    return strips


def shift_sums(chunk, stride, step, x, p, h, u, l, w, t):
    def pairs(r0, size):
        for s in range(-4, stride + 3):
            p[s + 4, pl.ds(r0, size), :] = x[s + 5, pl.ds(r0, size), :] + x[s + 6, pl.ds(r0 - 1, size), :]

    over(8, chunk + 24, step, pairs)

    def mix(r0, size):
        for s in range(stride):
            here = (s, pl.ds(r0, size), slice(None))
            at = lambda ref, k, shift: ref[k, pl.ds(r0 + shift, size), :]
            hp = at(p, s + 7, -3) + at(x, s + 10, -5)
            hm = at(p, s, 4) + at(x, s, 5)
            lp = hp + at(p, s + 5, -1)
            h[here] = hp
            u[here] = hp + hm
            l[here] = lp
            w[here] = lp + (hm + at(p, s + 2, 2))
            t[here] = at(p, s + 4, 0) + at(x, s + 4, 1)

    over(8, chunk + 16, step, mix)

    def runs(r0, size):
        for s in range(stride):
            for ref in (w, t):
                at = lambda shift: ref[s, pl.ds(r0 + shift, size), :]
                ref[s, pl.ds(r0, size), :] = at(0) + at(1) + at(2)

    over(8, chunk + 16, step, runs)


def four_sums(s, r0, size, h, u, l, w, t):
    at = lambda ref, shift: ref[s, pl.ds(r0 + shift, size), :]
    below, above = at(u, -1), at(u, 1)
    donut = (at(w, -5) + at(w, 3)) + ((at(u, -2) + below) + (above + at(u, 2)))
    lower = (at(l, -5) + at(l, -4) + at(l, -3)) + (at(h, -2) + at(h, -1))
    return donut, lower, at(t, -5) + at(t, 3), below + at(u, 0) + above


def observed_kernel(nd, nb, chunk, step, base, low_ref, mid_ref, high_ref, near_ref, fan_ref, out_ref, x_ref, *refs):
    stride = nb // LANES
    strips = strips_of(stride, low_ref, mid_ref, high_ref)

    def fill(r0, size):
        for s, (ref, k) in strips.items():
            w = ref[k, pl.ds(base + r0, size), :].astype(F32)
            near = jnp.broadcast_to(near_ref[8 + s : 9 + s, :], (size, LANES))
            x_ref[s + 5, pl.ds(r0, size), :] = w * near * fan_ref[pl.ds(base + r0 + 8 + s, size), :]

    over(0, chunk + 2 * RIM, step, fill)
    shift_sums(chunk, stride, step, x_ref, *refs)

    def emit(r0, size):
        for s in range(stride):
            sums = four_sums(s, r0, size, *refs[1:])
            for k, value in enumerate(sums + (x_ref[s + 5, pl.ds(r0, size), :],)):
                out_ref[5 * s + k, pl.ds(r0 - RIM, size), :] = value

    over(RIM, chunk, step, emit)


def score_kernel(nd, nb, chunk, step, low_ref, mid_ref, high_ref, diag_ref, perm_ref, *rest):
    stride = nb // LANES
    count = nd // chunk
    seen_refs, out_hbm = rest[:count], rest[count]
    col_ref, out_ref, sems, x_ref = rest[count + 1 : count + 5]
    refs = rest[count + 5 :]
    strips = strips_of(stride, low_ref, mid_ref, high_ref)
    tiles = diag_ref.shape[0] // 2
    expected = diag_ref[:tiles, :] / jnp.maximum(diag_ref[tiles:, :], 1.0)
    columns([expected[t : t + 1, :] for t in range(tiles)], col_ref)

    def leave(i):
        here = (pl.ds(pl.multiple_of(i * chunk, 32), chunk), slice(None))
        return pltpu.make_async_copy(out_ref.at[here], out_hbm.at[here], sems.at[i])

    def score(seen_ref, base, r0, size):
        e = col_ref[pl.ds(base + r0, size), :]
        inverse = 1.0 / e
        for s in range(stride):
            sums = four_sums(s, r0, size, *refs[1:])
            seen = [seen_ref[5 * s + k, pl.ds(r0 - RIM, size), :] for k in range(5)]
            least = None
            for k in range(4):
                ratio = (sums[k] + e) / (seen[k] + e)
                least = ratio if least is None else jnp.minimum(least, ratio)
            value = least * (seen[4] * inverse)
            value = jnp.where(x_ref[s + 5, pl.ds(r0, size), :] > 0.0, value, 0.0)
            hi = value.astype(BF16)
            low = (value - hi.astype(F32)).astype(BF16)
            perm = perm_ref[s * LANES : (s + 1) * LANES, :]
            placed = jnp.dot(
                jnp.concatenate([hi, low], axis=1), jnp.concatenate([perm, perm], axis=0), preferred_element_type=F32
            )
            here = pl.ds(base + r0 - RIM, size)
            out_ref[here, :] = placed if s == 0 else out_ref[here, :] + placed

    def body(i, _):
        base = pl.multiple_of(i * chunk, 32)

        def fill(r0, size):
            e = col_ref[pl.ds(base + r0, size), :]
            for s, (ref, k) in strips.items():
                w = ref[k, pl.ds(base + r0, size), :].astype(F32)
                x_ref[s + 5, pl.ds(r0, size), :] = jnp.where(w > 0.0, e, 0.0)

        over(0, chunk + 2 * RIM, step, fill)
        shift_sums(chunk, stride, step, x_ref, *refs)
        for c in range(count):

            @pl.when(i == c)
            def _():
                over(RIM, chunk, chunk, functools.partial(score, seen_refs[c], base))

        leave(i).start()
        return 0

    lax.fori_loop(0, count, body, 0)
    for i in range(count):
        leave(i).wait()


def tie(x, state, names):
    x, values = lax.optimization_barrier((x, tuple(state[name] for name in names)))
    state.update(zip(names, values))
    return x


def total(x, axes, state=None, tasks={}, due={}):
    rounds = []
    for axis in axes:
        size, bit = lax.axis_size(axis), 1
        while bit < size:
            rounds.append((axis, [(i, i ^ bit) for i in range(size)]))
            bit *= 2
    for k, (axis, pairs) in enumerate(rounds):
        if k in tasks:
            x = tie(x, state, tasks[k][0])
        came = lax.ppermute(x, axis, pairs)
        if k in tasks:
            names, task = tasks[k]
            state.update(task(*[state[name] for name in names]))
        x = x + came
        if k in due:
            x = tie(x, state, due[k])
    return x


def shifted(x, axis, step):
    size = lax.axis_size(axis)
    pairs = [(i, i + 1) for i in range(size - 1)]
    return lax.ppermute(x, axis, pairs if step > 0 else [(j, i) for i, j in pairs])


def on_device(contacts, masked_bins, chrom_bounds):
    nd, nb = contacts.shape
    cols = nb // LANES
    bins = nb * lax.axis_size("genome")
    band = nd * lax.axis_size("offset")
    rows = bins // LANES
    span = -(-nd // LANES) + cols - 1
    tall = rows + -(-band // LANES) + 24
    total_rows = nd + 2 * RIM
    shape = jax.ShapeDtypeStruct
    f = lambda *dims: shape(dims, F32)

    w, part, keep, top, bottom = pl.pallas_call(
        functools.partial(first_kernel, nd, nb),
        out_shape=(shape((nd, nb), BF16), f(rows, LANES), f(rows, LANES), f(RIM, nb), f(RIM, nb)),
        in_specs=[HBM] * 3,
        out_specs=(VMEM,) * 5,
        scratch_shapes=[
            pltpu.VMEM((tall, LANES), F32),
            pltpu.VMEM((LANES, span * LANES), F32),
            pltpu.VMEM((LANES, span * LANES), F32),
            pltpu.VMEM((tall, LANES), F32),
            pltpu.SMEM(chrom_bounds.shape, jnp.int32),
            pltpu.VMEM((nd, nb), BF16),
            pltpu.VMEM((1,) + masked_bins.shape, jnp.int32),
            pltpu.SemaphoreType.DMA((3,)),
        ],
        compiler_params=params(12),
        name="first_sums",
    )(*(pltpu.with_memory_space_constraint(a, pltpu.HBM) for a in (chrom_bounds, contacts, masked_bins.reshape(1, -1))))

    def sides(w, above, below):
        return pl.pallas_call(
            functools.partial(side_kernel, nd, nb),
            out_shape=(f(SIDE, total_rows), f(SIDE, total_rows)),
            in_specs=[VMEM] * 3,
            out_specs=(VMEM,) * 2,
            compiler_params=params(16),
            name="sides",
        )(w, above, below)

    def first_side(w, above, below):
        left, right = sides(w, above, below)
        return dict(right=right, after=shifted(left, "genome", -1))

    state = dict(w=w, top=top, bottom=bottom)
    tasks = {
        0: (("bottom",), lambda bottom: dict(above=shifted(bottom, "offset", 1))),
        1: (("top",), lambda top: dict(below=shifted(top, "offset", -1))),
        3: (("w", "above", "below"), first_side),
    }
    sums = total(part, ("genome", "offset"), state, tasks, {1: ("above",), 2: ("below",)})
    w = state["w"]

    part, bias = pl.pallas_call(
        functools.partial(second_kernel, nd, nb),
        out_shape=(f(rows, LANES), f(rows, LANES)),
        in_specs=[VMEM] * 3,
        out_specs=(VMEM,) * 2,
        scratch_shapes=[
            pltpu.VMEM((tall, LANES), F32),
            pltpu.VMEM((LANES, span * LANES), F32),
            pltpu.VMEM((LANES, span * LANES), F32),
            pltpu.VMEM((tall, LANES), F32),
        ],
        compiler_params=params(),
        name="second_sums",
    )(w, sums, keep)

    def strip(name, first, count):
        def run(*operands):
            strips = pl.pallas_call(
                functools.partial(strip_kernel, nd, nb, first, count),
                out_shape=shape((count, total_rows, LANES), BF16),
                in_specs=[VMEM] * 5,
                out_specs=VMEM,
                scratch_shapes=[
                    pltpu.VMEM((nb, count * LANES), BF16),
                    pltpu.VMEM((total_rows, count * LANES), F32),
                ],
                compiler_params=params(24),
                name="strips",
            )(*operands)
            return {name: strips}

        return ("w", "above", "below") + (("above", "below") if name == "mid" else ("before", "after")), run

    def back(_, right):
        matrix = pl.pallas_call(
            functools.partial(unstrip_kernel, nb),
            out_shape=shape((nb, nb), BF16),
            out_specs=VMEM,
            compiler_params=params(8),
            name="unstrip",
        )()
        return dict(perm=matrix, before=shifted(right, "genome", 1))

    tasks = {
        0: (("keep", "right"), back),
        2: strip("mid", 0, cols),
        3: strip("high", cols, 5),
        4: strip("low", -5, 5),
    }
    state["keep"] = keep
    due = {0: ("perm", "after"), 2: ("mid", "before"), 3: ("high",), 4: ("low",)}
    sums = total(part, ("genome", "offset"), state, tasks, due)
    low, high, mid, perm, keep = (state[name] for name in ("low", "high", "mid", "perm", "keep"))

    padded = -(-total_rows // LANES) * LANES
    fan_len = fan_rows(nd)
    reach = -(-(fan_len + cols * (LANES - 1) + 2 * LANES) // LANES) * LANES
    near = 24
    near_reach = -(-(near + cols * (LANES - 1) + LANES) // LANES) * LANES
    own, fans, nears, diag = pl.pallas_call(
        functools.partial(third_kernel, nd, nb),
        out_shape=(f(cols, LANES), f(fan_len, LANES), f(near, LANES), f(2 * padded // LANES, LANES)),
        in_specs=[VMEM] * 4,
        out_specs=(VMEM,) * 4,
        scratch_shapes=[
            pltpu.VMEM((tall + 8, LANES), F32),
            pltpu.VMEM((reach, LANES), F32),
            pltpu.VMEM((reach, LANES), F32),
            pltpu.VMEM((near_reach, LANES), F32),
            pltpu.VMEM((near_reach, LANES), F32),
            pltpu.VMEM((padded, 4 * LANES), BF16),
        ],
        compiler_params=params(),
        name="diagonal_sums",
    )(mid, sums, keep, bias)
    chunk = next(c for c in (320, 256, 128, 64, 32) if nd % c == 0)
    count = nd // chunk
    tall = chunk + 2 * RIM
    scratch = [pltpu.VMEM((tiles, tall, LANES), F32) for tiles in (cols + 10, cols + 7) + (cols,) * 5]

    def observe(*which):
        def run(*operands):
            made = {}
            for c in which:
                made[f"seen{c}"] = pl.pallas_call(
                    functools.partial(observed_kernel, nd, nb, chunk, STEP, c * chunk),
                    out_shape=f(5 * cols, chunk, LANES),
                    in_specs=[VMEM] * 5,
                    out_specs=VMEM,
                    scratch_shapes=scratch,
                    compiler_params=params(20),
                    name="observed",
                )(*operands)
            return made

        return ("low", "mid", "high", "near", "fan"), run

    rounds = (lax.axis_size("genome") - 1).bit_length()
    turns = {}
    for c in range(count):
        turns.setdefault(min(c, rounds - 1), []).append(c)
    state.update(near=nears, fan=fans)
    diag = total(
        diag,
        ("genome",),
        state,
        {k: observe(*which) for k, which in turns.items()},
        {k: tuple(f"seen{c}" for c in which) for k, which in turns.items()},
    )

    operands = (low, mid, high, diag, perm) + tuple(state[f"seen{c}"] for c in range(count))
    score = pl.pallas_call(
        functools.partial(score_kernel, nd, nb, chunk, STEP),
        out_shape=f(nd, nb),
        in_specs=[VMEM] * len(operands),
        out_specs=HBM,
        scratch_shapes=[
            pltpu.VMEM((padded, LANES), F32),
            pltpu.VMEM((nd, nb), F32),
            pltpu.SemaphoreType.DMA((count,)),
        ]
        + scratch,
        compiler_params=params(24),
        name="score",
    )(*operands)
    return score, own.reshape(nb)


def solution(mesh):
    return jax.shard_map(
        on_device,
        mesh=mesh,
        in_specs=(P("offset", "genome"), P(), P()),
        out_specs=(P("offset", "genome"), P("genome")),
        check_vma=False,
    )
```

```python
import functools
import math

import jax
import jax.numpy as jnp
from jax import lax
from jax.experimental import pallas as pl
from jax.experimental.pallas import tpu as pltpu
from jax.sharding import PartitionSpec as P

RIM = 16
STEP = 176
SIDE = 8
LANES = 128
F32 = jnp.float32
BF16 = jnp.bfloat16
TINY = 2.0**-126
VMEM = pl.BlockSpec(memory_space=pltpu.VMEM)
HBM = pl.BlockSpec(memory_space=pltpu.HBM)
ANY = pl.BlockSpec(memory_space=pl.ANY)
NT = (((1,), (1,)), ((), ()))


def params(mib=48):
    return pltpu.CompilerParams(vmem_limit_bytes=mib << 20)


def iota(shape, dim):
    return lax.broadcasted_iota(jnp.int32, shape, dim)


def place(nd, nb):
    first = lax.axis_index("genome") * nb
    partner = first + lax.axis_index("offset") * nd
    return first // LANES, partner // LANES, partner % LANES


def roll(x, shift):
    length = x.shape[1]
    if isinstance(shift, int):
        shift = shift % length
        if shift == 0:
            return x
    return pltpu.roll(x, shift, 1)


def hankel(rows_ref, row0, lane0, tiles, out_ref):
    extra = 1 if lane0 is None else 2
    base = jnp.concatenate(
        [jnp.broadcast_to(rows_ref[pl.ds(row0 + t, 1), :], (8, LANES)) for t in range(tiles + extra)],
        axis=1,
    )
    length = base.shape[1]
    if lane0 is not None:
        base = roll(base, length - lane0)
    sub = iota(base.shape, 0)
    for bit in (1, 2, 4):
        base = jnp.where((sub & bit) > 0, roll(base, length - bit), base)
    for r in range(16):
        out_ref[8 * r : 8 * r + 8, : tiles * LANES] = roll(base, length - 8 * r)[:, : tiles * LANES]


def antidiagonal(acc_ref, tiles, lane0):
    extra = 1 if lane0 is None else 2
    pad = jnp.zeros((8, extra * LANES), F32)
    parts = [jnp.concatenate([acc_ref[8 * r : 8 * r + 8, : tiles * LANES], pad], axis=1) for r in range(16)]
    shift = 8
    while len(parts) > 1:
        parts = [low + roll(high, shift) for low, high in zip(parts[::2], parts[1::2])]
        shift *= 2
    total = parts[0]
    sub = iota(total.shape, 0)
    for bit in (4, 2, 1):
        total = jnp.where((sub & bit) > 0, roll(total, bit), total)
    total = jnp.sum(total, axis=0, keepdims=True)
    if lane0 is not None:
        total = roll(total, lane0)
    return total


def spread(own, partner, row_own, row_partner, placed_ref, out_ref):
    placed_ref[...] = jnp.zeros_like(placed_ref)
    for t in range(partner.shape[1] // LANES):
        placed_ref[pl.ds(row_partner + t, 1), :] = partner[:, t * LANES : (t + 1) * LANES]
    for c in range(own.shape[1] // LANES):
        placed_ref[pl.ds(row_own + c, 1), :] += own[:, c * LANES : (c + 1) * LANES]
    out_ref[...] = placed_ref[: out_ref.shape[0], :]


def sweep(nd, nb, entry, weigh_own, weigh_partner, acc_ref):
    cols = nb // LANES
    full, rest = nd // LANES, nd % LANES
    first_diag = lax.axis_index("offset") * nd
    sub = iota((16, LANES), 0)

    def body(ms, fresh, r, own):
        own = list(own)
        q0 = pl.multiple_of(16 * r, 16)
        sums = {}
        for m in ms:
            for c in range(cols):
                w = entry(m, c, q0)
                own[c] = own[c] + weigh_own(w, m, c, q0)
                g = weigh_partner(w, c)
                if m == 0:
                    g = jnp.where(sub + q0 + first_diag > 0, g, 0.0)
                sums[m + c] = sums[m + c] + g if m + c in sums else g
        for t, value in sums.items():
            tile = (pl.ds(q0, 16), slice(t * LANES, (t + 1) * LANES))
            acc_ref[tile] = value if fresh else acc_ref[tile] + value
        return tuple(own)

    own = tuple(jnp.zeros((16, LANES), F32) for _ in range(cols))
    if rest:
        acc_ref[...] = jnp.zeros_like(acc_ref)
    own = lax.fori_loop(0, 8, functools.partial(body, range(full), not rest), own)
    if rest:
        own = lax.fori_loop(0, rest // 16, functools.partial(body, [full], False), own)
    return jnp.concatenate([jnp.sum(o, axis=0, keepdims=True) for o in own], axis=1)


def keep_of(masked, rows):
    count = masked.shape[1]
    in_row = (jnp.broadcast_to(masked >> 7, (rows, count)) == iota((rows, count), 0))
    in_lane = (jnp.broadcast_to(masked & 127, (LANES, count)) == iota((LANES, count), 0))
    hits = lax.dot_general(
        in_row.astype(F32).astype(BF16), in_lane.astype(F32).astype(BF16), NT, preferred_element_type=F32
    )
    return jnp.where(hits > 0.0, 0.0, 1.0)


def first_kernel(nd, nb, bounds_hbm, x_hbm, masked_hbm, w_ref, part_ref, keep_ref, top_ref, bottom_ref,
                 codes_ref, hank_ref, acc_ref, placed_ref, bounds_ref, x_ref, masked_ref, sems):
    copies = [
        pltpu.make_async_copy(source, target, sems.at[k])
        for k, (source, target) in enumerate(
            ((masked_hbm, masked_ref), (bounds_hbm, bounds_ref), (x_hbm, x_ref))
        )
    ]
    for copy in copies:
        copy.start()
    copies[0].wait()
    copies[1].wait()
    rows = keep_ref.shape[0]
    cols = nb // LANES
    span = -(-nd // LANES) + cols - 1
    row_own, row_partner, lane0 = place(nd, nb)
    lane0 = lane0 if nd % LANES else None
    keep = keep_of(masked_ref[...], rows)
    keep_ref[...] = keep
    bins = iota((rows, LANES), 0) * LANES + iota((rows, LANES), 1)
    chrom = jnp.zeros((rows, LANES), F32)
    for k in range(bounds_ref.shape[0]):
        chrom = chrom + jnp.where(bins >= bounds_ref[k], 1.0, 0.0)
    codes_ref[...] = jnp.full_like(codes_ref, -2.0)
    codes_ref[:rows, :] = jnp.where(keep > 0.0, chrom, -2.0)
    hankel(codes_ref, row_partner, lane0, span, hank_ref)
    code_own = []
    for c in range(cols):
        code = codes_ref[pl.ds(row_own + c, 1), :]
        code = jnp.where(code < 0.0, -1.0, code)
        code_own.append(jnp.broadcast_to(code, (16, LANES)))
    copies[2].wait()

    def entry(m, c, q0):
        here = (pl.ds(q0 + m * LANES, 16), slice(c * LANES, (c + 1) * LANES))
        code = hank_ref[pl.ds(q0, 16), (m + c) * LANES : (m + c + 1) * LANES]
        value = jnp.maximum(x_ref[here].astype(F32), TINY)
        w = jnp.where(code == code_own[c], value, 0.0)
        w_ref[here] = w.astype(BF16)
        return w

    own = sweep(nd, nb, entry, lambda w, m, c, q0: w, lambda w, c: w, acc_ref)
    spread(own, antidiagonal(acc_ref, span, lane0), row_own, row_partner, placed_ref, part_ref)
    top_ref[...] = w_ref[:RIM, :].astype(F32)
    bottom_ref[...] = w_ref[nd - RIM :, :].astype(F32)


def next_bias(keep, bias, sums):
    level = jnp.sum(sums * keep, keepdims=True) / jnp.sum(keep, keepdims=True)
    safe = jnp.where(keep > 0.0, sums, 1.0)
    return jnp.where(keep > 0.0, bias * level / safe, 0.0)


def second_kernel(nd, nb, w_ref, sums_ref, keep_ref, part_ref, bias_ref, window_ref, hank_ref, acc_ref, placed_ref):
    rows = keep_ref.shape[0]
    cols = nb // LANES
    span = -(-nd // LANES) + cols - 1
    row_own, row_partner, lane0 = place(nd, nb)
    lane0 = lane0 if nd % LANES else None
    bias = next_bias(keep_ref[...], keep_ref[...], sums_ref[...])
    bias_ref[...] = bias
    window_ref[...] = jnp.zeros_like(window_ref)
    window_ref[:rows, :] = bias
    hankel(window_ref, row_partner, lane0, span, hank_ref)
    rows_own = [window_ref[pl.ds(row_own + c, 1), :] for c in range(cols)]
    own_bias = [jnp.broadcast_to(b, (16, LANES)) for b in rows_own]

    def entry(m, c, q0):
        return w_ref[pl.ds(q0 + m * LANES, 16), c * LANES : (c + 1) * LANES].astype(F32)

    def weigh_own(w, m, c, q0):
        return w * hank_ref[pl.ds(q0, 16), (m + c) * LANES : (m + c + 1) * LANES]

    own = sweep(nd, nb, entry, weigh_own, lambda w, c: w * own_bias[c], acc_ref)
    own = own * jnp.concatenate(rows_own, axis=1)
    partner = antidiagonal(acc_ref, span, lane0)
    tiles = partner.shape[1] // LANES
    partner = partner * jnp.concatenate(
        [window_ref[pl.ds(row_partner + t, 1), :] for t in range(tiles)], axis=1
    )
    spread(own, partner, row_own, row_partner, placed_ref, part_ref)


def side_kernel(nd, nb, w_ref, top_ref, bottom_ref, left_ref, right_ref):
    row, lane = iota((SIDE, LANES), 0), iota((SIDE, LANES), 1)
    for out_ref, pick, first in (
        (left_ref, row == lane, 0),
        (right_ref, row + LANES - SIDE == lane, nb - LANES),
    ):
        pick = pick.astype(F32).astype(BF16)
        cols = slice(first, first + LANES)
        block = jnp.concatenate(
            [w_ref[:, cols], bottom_ref[:, cols].astype(BF16), top_ref[:, cols].astype(BF16)], axis=0
        )
        out_ref[...] = lax.dot_general(pick, block, NT, preferred_element_type=F32)


def strip_kernel(nd, nb, first, count, w_ref, top_ref, bottom_ref, left_ref, right_ref, out_ref, perm_ref, side_ref):
    stride = nb // LANES
    width = count * LANES
    lane = iota((nb, LANES), 1)
    row = iota((nb, LANES), 0)
    for k in range(count):
        hit = row == lane * stride + (first + k)
        perm_ref[:, k * LANES : (k + 1) * LANES] = hit.astype(F32).astype(BF16)
    perm = perm_ref[...]
    rims = []
    row, lane = iota((2 * SIDE, LANES), 0), iota((2 * SIDE, LANES), 1)
    bin_of = jnp.where(row < SIDE, row - SIDE, row - SIDE + nb)
    for k in range(count):
        rims.append((bin_of == lane * stride + (first + k)).astype(F32).astype(BF16))
    rims = jnp.concatenate(rims, axis=1)
    sides = jnp.concatenate([left_ref[...], right_ref[...]], axis=0).astype(BF16)
    outer = first < 0 or first + count > stride
    if outer:
        side_ref[...] = lax.dot_general(
            sides, rims, (((0,), (0,)), ((), ())), preferred_element_type=F32
        )

    def emit(block, at, side_at, rows):
        value = jnp.dot(block, perm, preferred_element_type=F32)
        if outer:
            value = value + side_ref[side_at : side_at + rows, :]
        for k in range(count):
            out_ref[k, at : at + rows, :] = value[:, k * LANES : (k + 1) * LANES].astype(BF16)

    emit(top_ref[...].astype(BF16), 0, nd + RIM, RIM)
    emit(bottom_ref[...].astype(BF16), nd + RIM, nd, RIM)
    emit(w_ref[...], RIM, 0, nd)


def unstrip_kernel(nb, out_ref):
    stride = nb // LANES
    row, lane = iota((LANES, nb), 0), iota((LANES, nb), 1)
    for s in range(stride):
        out_ref[s * LANES : (s + 1) * LANES, :] = (lane == row * stride + s).astype(F32).astype(BF16)


def columns(rows, out_ref):
    for k, row in enumerate(rows):
        out_ref[k * LANES : (k + 1) * LANES, :] = jnp.broadcast_to(row, (LANES, LANES)).T


def fan(col_ref, other_ref, start, rows, stride, out_ref):
    lane = {}
    source, offset = col_ref, start
    target = other_ref
    for bit in (64, 32, 16, 8, 4, 2, 1):
        need = rows + stride * (bit - 1)
        need = -(-need // 8) * 8
        if bit == 1:
            target = out_ref
        def move(at, size, source=source, target=target, offset=offset, bit=bit):
            low = source[pl.ds(offset + at, size), :]
            high = source[pl.ds(offset + at + stride * bit, size), :]
            odd = (iota((size, LANES), 1) & bit) > 0
            target[pl.ds(at, size), :] = jnp.where(odd, high, low)

        move(0, need)
        source, target, offset = target, source, 0


def fan_rows(nd):
    return nd + 2 * RIM + 32


def third_kernel(nd, nb, mid_ref, sums_ref, keep_ref, bias_ref, own_ref, fan_ref, near_ref, diag_ref,
                 window_ref, col_ref, other_ref, ncol_ref, nother_ref, total_ref):
    rows = keep_ref.shape[0]
    cols = nb // LANES
    stride = cols
    row_own, row_partner, lane0 = place(nd, nb)
    bias = next_bias(keep_ref[...], bias_ref[...], sums_ref[...])
    window_ref[...] = jnp.zeros_like(window_ref)
    window_ref[8 : 8 + rows, :] = bias
    for c in range(cols):
        own_ref[c : c + 1, :] = window_ref[pl.ds(8 + row_own + c, 1), :]
    tiles = col_ref.shape[0] // LANES
    columns([window_ref[pl.ds(7 + row_partner + t, 1), :] for t in range(tiles)], col_ref)
    start = LANES - RIM - 8
    if nd % LANES:
        start = start + lane0
    fan(col_ref, other_ref, start, fan_rows(nd), stride, fan_ref)
    columns([window_ref[pl.ds(7 + row_own + t, 1), :] for t in range(ncol_ref.shape[0] // LANES)], ncol_ref)
    fan(ncol_ref, nother_ref, LANES - 8, near_ref.shape[0], stride, near_ref)
    total_rows = nd + 2 * RIM

    def add(r0, size):
        total, count = None, None
        for s in range(stride):
            w = mid_ref[s, pl.ds(r0, size), :].astype(F32)
            near = jnp.broadcast_to(near_ref[8 + s : 9 + s, :], (size, LANES))
            b = w * near * fan_ref[pl.ds(r0 + 8 + s, size), :]
            v = jnp.where(w > 0.0, 1.0, 0.0)
            total = b if total is None else total + b
            count = v if count is None else count + v
        total_ref[pl.ds(r0, size), :LANES] = total
        total_ref[pl.ds(r0, size), LANES:] = count

    over(0, total_rows, total_rows // 2, add)
    padded = total_ref.shape[0]
    tiles = padded // LANES
    if padded > total_rows:
        total_ref[total_rows:, :] = jnp.zeros((padded - total_rows, 2 * LANES), F32)
    for t in range(tiles):
        for k in range(2):
            block = total_ref[t * LANES : (t + 1) * LANES, k * LANES : (k + 1) * LANES]
            diag_ref[k * tiles + t : k * tiles + t + 1, :] = jnp.sum(block.T, axis=0, keepdims=True)


def over(start, count, step, run):
    steps = count // step
    if steps > 0:

        def body(i, _):
            run(pl.multiple_of(i * step + start, math.gcd(start, step)), step)
            return 0

        lax.fori_loop(0, steps, body, 0)
    if count % step:
        run(start + steps * step, count % step)


def strips_of(stride, low_ref, mid_ref, high_ref):
    strips = {}
    for s in range(-5, 0):
        strips[s] = (low_ref, s + 5)
    for s in range(stride):
        strips[s] = (mid_ref, s)
    for s in range(stride, stride + 5):
        strips[s] = (high_ref, s - stride)
    return strips


def shift_sums(chunk, stride, step, x, p, h, u, l, w, t):
    def pairs(r0, size):
        for s in range(-4, stride + 3):
            p[s + 4, pl.ds(r0, size), :] = x[s + 5, pl.ds(r0, size), :] + x[s + 6, pl.ds(r0 - 1, size), :]

    over(8, chunk + 24, step, pairs)

    def mix(r0, size):
        for s in range(stride):
            here = (s, pl.ds(r0, size), slice(None))
            at = lambda ref, k, shift: ref[k, pl.ds(r0 + shift, size), :]
            hp = at(p, s + 7, -3) + at(x, s + 10, -5)
            hm = at(p, s, 4) + at(x, s, 5)
            lp = hp + at(p, s + 5, -1)
            h[here] = hp
            u[here] = hp + hm
            l[here] = lp
            w[here] = lp + (hm + at(p, s + 2, 2))
            t[here] = at(p, s + 4, 0) + at(x, s + 4, 1)

    over(8, chunk + 16, step, mix)

    def runs(r0, size):
        for s in range(stride):
            for ref in (w, t):
                at = lambda shift: ref[s, pl.ds(r0 + shift, size), :]
                ref[s, pl.ds(r0, size), :] = at(0) + at(1) + at(2)

    over(8, chunk + 16, step, runs)


def four_sums(s, r0, size, h, u, l, w, t):
    at = lambda ref, shift: ref[s, pl.ds(r0 + shift, size), :]
    below, above = at(u, -1), at(u, 1)
    donut = (at(w, -5) + at(w, 3)) + ((at(u, -2) + below) + (above + at(u, 2)))
    lower = (at(l, -5) + at(l, -4) + at(l, -3)) + (at(h, -2) + at(h, -1))
    return donut, lower, at(t, -5) + at(t, 3), below + at(u, 0) + above


def observed_kernel(nd, nb, chunk, step, base, low_ref, mid_ref, high_ref, near_ref, fan_ref, out_ref, x_ref, *refs):
    stride = nb // LANES
    strips = strips_of(stride, low_ref, mid_ref, high_ref)

    def fill(r0, size):
        for s, (ref, k) in strips.items():
            w = ref[k, pl.ds(base + r0, size), :].astype(F32)
            near = jnp.broadcast_to(near_ref[8 + s : 9 + s, :], (size, LANES))
            x_ref[s + 5, pl.ds(r0, size), :] = w * near * fan_ref[pl.ds(base + r0 + 8 + s, size), :]

    over(0, chunk + 2 * RIM, step, fill)
    shift_sums(chunk, stride, step, x_ref, *refs)

    def emit(r0, size):
        for s in range(stride):
            sums = four_sums(s, r0, size, *refs[1:])
            for k, value in enumerate(sums + (x_ref[s + 5, pl.ds(r0, size), :],)):
                out_ref[5 * s + k, pl.ds(r0 - RIM, size), :] = value

    over(RIM, chunk, step, emit)


def score_kernel(nd, nb, chunk, step, low_ref, mid_ref, high_ref, diag_ref, perm_ref, *rest):
    stride = nb // LANES
    count = nd // chunk
    seen_refs, out_hbm = rest[:count], rest[count]
    col_ref, out_ref, sems, x_ref = rest[count + 1 : count + 5]
    refs = rest[count + 5 :]
    strips = strips_of(stride, low_ref, mid_ref, high_ref)
    tiles = diag_ref.shape[0] // 2
    expected = diag_ref[:tiles, :] / jnp.maximum(diag_ref[tiles:, :], 1.0)
    expected = jnp.where(expected > 0.0, expected, 1.0)
    columns([expected[t : t + 1, :] for t in range(tiles)], col_ref)

    def leave(i):
        here = (pl.ds(pl.multiple_of(i * chunk, 32), chunk), slice(None))
        return pltpu.make_async_copy(out_ref.at[here], out_hbm.at[here], sems.at[i])

    def score(seen_ref, base, r0, size):
        e = col_ref[pl.ds(base + r0, size), :]
        inverse = 1.0 / e
        for s in range(stride):
            sums = four_sums(s, r0, size, *refs[1:])
            seen = [seen_ref[5 * s + k, pl.ds(r0 - RIM, size), :] for k in range(5)]
            least = None
            for k in range(4):
                ratio = (sums[k] + e) / (seen[k] + e)
                least = ratio if least is None else jnp.minimum(least, ratio)
            value = least * (seen[4] * inverse)
            hi = value.astype(BF16)
            low = (value - hi.astype(F32)).astype(BF16)
            perm = perm_ref[s * LANES : (s + 1) * LANES, :]
            placed = jnp.dot(
                jnp.concatenate([hi, low], axis=1), jnp.concatenate([perm, perm], axis=0), preferred_element_type=F32
            )
            here = pl.ds(base + r0 - RIM, size)
            out_ref[here, :] = placed if s == 0 else out_ref[here, :] + placed

    def body(i, _):
        base = pl.multiple_of(i * chunk, 32)

        def fill(r0, size):
            e = col_ref[pl.ds(base + r0, size), :]
            for s, (ref, k) in strips.items():
                w = ref[k, pl.ds(base + r0, size), :].astype(F32)
                x_ref[s + 5, pl.ds(r0, size), :] = jnp.where(w > 0.0, e, 0.0)

        over(0, chunk + 2 * RIM, step, fill)
        shift_sums(chunk, stride, step, x_ref, *refs)
        for c in range(count):

            @pl.when(i == c)
            def _():
                over(RIM, chunk, chunk, functools.partial(score, seen_refs[c], base))

        leave(i).start()
        return 0

    lax.fori_loop(0, count, body, 0)
    for i in range(count):
        leave(i).wait()


def tie(x, state, names):
    x, values = lax.optimization_barrier((x, tuple(state[name] for name in names)))
    state.update(zip(names, values))
    return x


def total(x, axes, state=None, tasks={}, due={}):
    rounds = []
    for axis in axes:
        size, bit = lax.axis_size(axis), 1
        while bit < size:
            rounds.append((axis, [(i, i ^ bit) for i in range(size)]))
            bit *= 2
    for k, (axis, pairs) in enumerate(rounds):
        if k in tasks:
            x = tie(x, state, tasks[k][0])
        came = lax.ppermute(x, axis, pairs)
        if k in tasks:
            names, task = tasks[k]
            state.update(task(*[state[name] for name in names]))
        x = x + came
        if k in due:
            x = tie(x, state, due[k])
    return x


def shifted(x, axis, step):
    size = lax.axis_size(axis)
    pairs = [(i, i + 1) for i in range(size - 1)]
    return lax.ppermute(x, axis, pairs if step > 0 else [(j, i) for i, j in pairs])


def on_device(contacts, masked_bins, chrom_bounds):
    nd, nb = contacts.shape
    cols = nb // LANES
    bins = nb * lax.axis_size("genome")
    band = nd * lax.axis_size("offset")
    rows = bins // LANES
    span = -(-nd // LANES) + cols - 1
    tall = rows + -(-band // LANES) + 24
    total_rows = nd + 2 * RIM
    shape = jax.ShapeDtypeStruct
    f = lambda *dims: shape(dims, F32)

    w, part, keep, top, bottom = pl.pallas_call(
        functools.partial(first_kernel, nd, nb),
        out_shape=(shape((nd, nb), BF16), f(rows, LANES), f(rows, LANES), f(RIM, nb), f(RIM, nb)),
        in_specs=[HBM] * 3,
        out_specs=(VMEM,) * 5,
        scratch_shapes=[
            pltpu.VMEM((tall, LANES), F32),
            pltpu.VMEM((LANES, span * LANES), F32),
            pltpu.VMEM((LANES, span * LANES), F32),
            pltpu.VMEM((tall, LANES), F32),
            pltpu.SMEM(chrom_bounds.shape, jnp.int32),
            pltpu.VMEM((nd, nb), BF16),
            pltpu.VMEM((1,) + masked_bins.shape, jnp.int32),
            pltpu.SemaphoreType.DMA((3,)),
        ],
        compiler_params=params(12),
        name="first_sums",
    )(*(pltpu.with_memory_space_constraint(a, pltpu.HBM) for a in (chrom_bounds, contacts, masked_bins.reshape(1, -1))))

    def sides(w, above, below):
        return pl.pallas_call(
            functools.partial(side_kernel, nd, nb),
            out_shape=(f(SIDE, total_rows), f(SIDE, total_rows)),
            in_specs=[VMEM] * 3,
            out_specs=(VMEM,) * 2,
            compiler_params=params(16),
            name="sides",
        )(w, above, below)

    def first_side(w, above, below):
        left, right = sides(w, above, below)
        return dict(right=right, after=shifted(left, "genome", -1))

    state = dict(w=w, top=top, bottom=bottom)
    tasks = {
        0: (("bottom",), lambda bottom: dict(above=shifted(bottom, "offset", 1))),
        1: (("top",), lambda top: dict(below=shifted(top, "offset", -1))),
        3: (("w", "above", "below"), first_side),
    }
    sums = total(part, ("genome", "offset"), state, tasks, {1: ("above",), 2: ("below",)})
    w = state["w"]

    part, bias = pl.pallas_call(
        functools.partial(second_kernel, nd, nb),
        out_shape=(f(rows, LANES), f(rows, LANES)),
        in_specs=[VMEM] * 3,
        out_specs=(VMEM,) * 2,
        scratch_shapes=[
            pltpu.VMEM((tall, LANES), F32),
            pltpu.VMEM((LANES, span * LANES), F32),
            pltpu.VMEM((LANES, span * LANES), F32),
            pltpu.VMEM((tall, LANES), F32),
        ],
        compiler_params=params(),
        name="second_sums",
    )(w, sums, keep)

    def strip(name, first, count):
        def run(*operands):
            strips = pl.pallas_call(
                functools.partial(strip_kernel, nd, nb, first, count),
                out_shape=shape((count, total_rows, LANES), BF16),
                in_specs=[VMEM] * 5,
                out_specs=VMEM,
                scratch_shapes=[
                    pltpu.VMEM((nb, count * LANES), BF16),
                    pltpu.VMEM((total_rows, count * LANES), F32),
                ],
                compiler_params=params(24),
                name="strips",
            )(*operands)
            return {name: strips}

        side = dict(low="before", mid="above", high="after")[name]
        return ("w", "above", "below", side, side), run

    def back(_, right):
        matrix = pl.pallas_call(
            functools.partial(unstrip_kernel, nb),
            out_shape=shape((nb, nb), BF16),
            out_specs=VMEM,
            compiler_params=params(8),
            name="unstrip",
        )()
        return dict(perm=matrix, before=shifted(right, "genome", 1))

    tasks = {
        0: (("keep", "right"), back),
        1: strip("mid", 0, cols),
        2: strip("high", cols, 5),
        3: strip("low", -5, 5),
    }
    state["keep"] = keep
    due = {0: ("perm", "after"), 1: ("mid",), 2: ("high", "before"), 3: ("low",)}
    sums = total(part, ("genome", "offset"), state, tasks, due)
    low, high, mid, perm, keep = (state[name] for name in ("low", "high", "mid", "perm", "keep"))

    padded = -(-total_rows // LANES) * LANES
    fan_len = fan_rows(nd)
    reach = -(-(fan_len + cols * (LANES - 1) + 2 * LANES) // LANES) * LANES
    near = 24
    near_reach = -(-(near + cols * (LANES - 1) + LANES) // LANES) * LANES
    own, fans, nears, diag = pl.pallas_call(
        functools.partial(third_kernel, nd, nb),
        out_shape=(f(cols, LANES), f(fan_len, LANES), f(near, LANES), f(2 * padded // LANES, LANES)),
        in_specs=[VMEM] * 4,
        out_specs=(VMEM,) * 4,
        scratch_shapes=[
            pltpu.VMEM((tall + 8, LANES), F32),
            pltpu.VMEM((reach, LANES), F32),
            pltpu.VMEM((reach, LANES), F32),
            pltpu.VMEM((near_reach, LANES), F32),
            pltpu.VMEM((near_reach, LANES), F32),
            pltpu.VMEM((padded, 2 * LANES), F32),
        ],
        compiler_params=params(),
        name="diagonal_sums",
    )(mid, sums, keep, bias)
    chunk = next(c for c in (320, 256, 128, 64, 32) if nd % c == 0)
    count = nd // chunk
    tall = chunk + 2 * RIM
    scratch = [pltpu.VMEM((tiles, tall, LANES), F32) for tiles in (cols + 10, cols + 7) + (cols,) * 5]

    def observe(*which):
        def run(*operands):
            made = {}
            for c in which:
                made[f"seen{c}"] = pl.pallas_call(
                    functools.partial(observed_kernel, nd, nb, chunk, STEP, c * chunk),
                    out_shape=f(5 * cols, chunk, LANES),
                    in_specs=[VMEM] * 5,
                    out_specs=VMEM,
                    scratch_shapes=scratch,
                    compiler_params=params(20),
                    name="observed",
                )(*operands)
            return made

        return ("low", "mid", "high", "near", "fan"), run

    rounds = (lax.axis_size("genome") - 1).bit_length()
    turns = {}
    for c in range(count):
        turns.setdefault((c + 1) * (rounds - 1) // count, []).append(c)
    state.update(near=nears, fan=fans)
    diag = total(
        diag,
        ("genome",),
        state,
        {k: observe(*which) for k, which in turns.items()},
        {k: tuple(f"seen{c}" for c in which) for k, which in turns.items()},
    )

    operands = (low, mid, high, diag, perm) + tuple(state[f"seen{c}"] for c in range(count))
    score = pl.pallas_call(
        functools.partial(score_kernel, nd, nb, chunk, STEP),
        out_shape=f(nd, nb),
        in_specs=[VMEM] * len(operands),
        out_specs=HBM,
        scratch_shapes=[
            pltpu.VMEM((padded, LANES), F32),
            pltpu.VMEM((nd, nb), F32),
            pltpu.SemaphoreType.DMA((count,)),
        ]
        + scratch,
        compiler_params=params(24),
        name="score",
    )(*operands)
    return score, own.reshape(nb)


def solution(mesh):
    return jax.shard_map(
        on_device,
        mesh=mesh,
        in_specs=(P("offset", "genome"), P(), P()),
        out_specs=(P("offset", "genome"), P("genome")),
        check_vma=False,
    )
```

```python
import functools
import math

import jax
import jax.numpy as jnp
from jax import lax
from jax.experimental import pallas as pl
from jax.experimental.pallas import tpu as pltpu
from jax.sharding import PartitionSpec as P

RIM = 16
STEP = 176
SIDE = 8
LANES = 128
F32 = jnp.float32
BF16 = jnp.bfloat16
TINY = 2.0**-126
VMEM = pl.BlockSpec(memory_space=pltpu.VMEM)
HBM = pl.BlockSpec(memory_space=pltpu.HBM)
ANY = pl.BlockSpec(memory_space=pl.ANY)
NT = (((1,), (1,)), ((), ()))


def params(mib=48):
    return pltpu.CompilerParams(vmem_limit_bytes=mib << 20)


def iota(shape, dim):
    return lax.broadcasted_iota(jnp.int32, shape, dim)


def place(nd, nb):
    first = lax.axis_index("genome") * nb
    partner = first + lax.axis_index("offset") * nd
    return first // LANES, partner // LANES, partner % LANES


def roll(x, shift):
    length = x.shape[1]
    if isinstance(shift, int):
        shift = shift % length
        if shift == 0:
            return x
    return pltpu.roll(x, shift, 1)


def hankel(rows_ref, row0, lane0, tiles, out_ref):
    extra = 1 if lane0 is None else 2
    base = jnp.concatenate(
        [jnp.broadcast_to(rows_ref[pl.ds(row0 + t, 1), :], (8, LANES)) for t in range(tiles + extra)],
        axis=1,
    )
    length = base.shape[1]
    if lane0 is not None:
        base = roll(base, length - lane0)
    sub = iota(base.shape, 0)
    for bit in (1, 2, 4):
        base = jnp.where((sub & bit) > 0, roll(base, length - bit), base)
    for r in range(16):
        out_ref[8 * r : 8 * r + 8, : tiles * LANES] = roll(base, length - 8 * r)[:, : tiles * LANES]


def antidiagonal(acc_ref, tiles, lane0):
    extra = 1 if lane0 is None else 2
    pad = jnp.zeros((8, extra * LANES), F32)
    parts = [jnp.concatenate([acc_ref[8 * r : 8 * r + 8, : tiles * LANES], pad], axis=1) for r in range(16)]
    shift = 8
    while len(parts) > 1:
        parts = [low + roll(high, shift) for low, high in zip(parts[::2], parts[1::2])]
        shift *= 2
    total = parts[0]
    sub = iota(total.shape, 0)
    for bit in (4, 2, 1):
        total = jnp.where((sub & bit) > 0, roll(total, bit), total)
    total = jnp.sum(total, axis=0, keepdims=True)
    if lane0 is not None:
        total = roll(total, lane0)
    return total


def spread(own, partner, row_own, row_partner, placed_ref, out_ref):
    placed_ref[...] = jnp.zeros_like(placed_ref)
    for t in range(partner.shape[1] // LANES):
        placed_ref[pl.ds(row_partner + t, 1), :] = partner[:, t * LANES : (t + 1) * LANES]
    for c in range(own.shape[1] // LANES):
        placed_ref[pl.ds(row_own + c, 1), :] += own[:, c * LANES : (c + 1) * LANES]
    out_ref[...] = placed_ref[: out_ref.shape[0], :]


def sweep(nd, nb, entry, weigh_own, weigh_partner, acc_ref):
    cols = nb // LANES
    full, rest = nd // LANES, nd % LANES
    first_diag = lax.axis_index("offset") * nd
    sub = iota((16, LANES), 0)

    def body(ms, fresh, r, own):
        own = list(own)
        q0 = pl.multiple_of(16 * r, 16)
        sums = {}
        for m in ms:
            for c in range(cols):
                w = entry(m, c, q0)
                own[c] = own[c] + weigh_own(w, m, c, q0)
                g = weigh_partner(w, c)
                if m == 0:
                    g = jnp.where(sub + q0 + first_diag > 0, g, 0.0)
                sums[m + c] = sums[m + c] + g if m + c in sums else g
        for t, value in sums.items():
            tile = (pl.ds(q0, 16), slice(t * LANES, (t + 1) * LANES))
            acc_ref[tile] = value if fresh else acc_ref[tile] + value
        return tuple(own)

    own = tuple(jnp.zeros((16, LANES), F32) for _ in range(cols))
    if rest:
        acc_ref[...] = jnp.zeros_like(acc_ref)
    own = lax.fori_loop(0, 8, functools.partial(body, range(full), not rest), own)
    if rest:
        own = lax.fori_loop(0, rest // 16, functools.partial(body, [full], False), own)
    return jnp.concatenate([jnp.sum(o, axis=0, keepdims=True) for o in own], axis=1)


def keep_of(masked, rows):
    count = masked.shape[1]
    in_row = (jnp.broadcast_to(masked >> 7, (rows, count)) == iota((rows, count), 0))
    in_lane = (jnp.broadcast_to(masked & 127, (LANES, count)) == iota((LANES, count), 0))
    hits = lax.dot_general(
        in_row.astype(F32).astype(BF16), in_lane.astype(F32).astype(BF16), NT, preferred_element_type=F32
    )
    return jnp.where(hits > 0.0, 0.0, 1.0)


def first_kernel(nd, nb, bounds_hbm, x_hbm, masked_hbm, w_ref, part_ref, keep_ref, top_ref, bottom_ref,
                 codes_ref, hank_ref, acc_ref, placed_ref, bounds_ref, x_ref, masked_ref, sems):
    copies = [
        pltpu.make_async_copy(source, target, sems.at[k])
        for k, (source, target) in enumerate(
            ((masked_hbm, masked_ref), (bounds_hbm, bounds_ref), (x_hbm, x_ref))
        )
    ]
    for copy in copies:
        copy.start()
    copies[0].wait()
    copies[1].wait()
    rows = keep_ref.shape[0]
    cols = nb // LANES
    span = -(-nd // LANES) + cols - 1
    row_own, row_partner, lane0 = place(nd, nb)
    lane0 = lane0 if nd % LANES else None
    keep = keep_of(masked_ref[...], rows)
    keep_ref[...] = keep
    bins = iota((rows, LANES), 0) * LANES + iota((rows, LANES), 1)
    chrom = jnp.zeros((rows, LANES), F32)
    for k in range(bounds_ref.shape[0]):
        chrom = chrom + jnp.where(bins >= bounds_ref[k], 1.0, 0.0)
    codes_ref[...] = jnp.full_like(codes_ref, -2.0)
    codes_ref[:rows, :] = jnp.where(keep > 0.0, chrom, -2.0)
    hankel(codes_ref, row_partner, lane0, span, hank_ref)
    code_own = []
    for c in range(cols):
        code = codes_ref[pl.ds(row_own + c, 1), :]
        code = jnp.where(code < 0.0, -1.0, code)
        code_own.append(jnp.broadcast_to(code, (16, LANES)))
    copies[2].wait()

    def entry(m, c, q0):
        here = (pl.ds(q0 + m * LANES, 16), slice(c * LANES, (c + 1) * LANES))
        code = hank_ref[pl.ds(q0, 16), (m + c) * LANES : (m + c + 1) * LANES]
        value = jnp.maximum(x_ref[here].astype(F32), TINY)
        w = jnp.where(code == code_own[c], value, 0.0)
        w_ref[here] = w.astype(BF16)
        return w

    own = sweep(nd, nb, entry, lambda w, m, c, q0: w, lambda w, c: w, acc_ref)
    spread(own, antidiagonal(acc_ref, span, lane0), row_own, row_partner, placed_ref, part_ref)
    top_ref[...] = w_ref[:RIM, :].astype(F32)
    bottom_ref[...] = w_ref[nd - RIM :, :].astype(F32)


def next_bias(keep, bias, sums):
    level = jnp.sum(sums * keep, keepdims=True) / jnp.sum(keep, keepdims=True)
    safe = jnp.where(keep > 0.0, sums, 1.0)
    return jnp.where(keep > 0.0, bias * level / safe, 0.0)


def second_kernel(nd, nb, w_ref, sums_ref, keep_ref, part_ref, bias_ref, window_ref, hank_ref, acc_ref, placed_ref):
    rows = keep_ref.shape[0]
    cols = nb // LANES
    span = -(-nd // LANES) + cols - 1
    row_own, row_partner, lane0 = place(nd, nb)
    lane0 = lane0 if nd % LANES else None
    bias = next_bias(keep_ref[...], keep_ref[...], sums_ref[...])
    bias_ref[...] = bias
    window_ref[...] = jnp.zeros_like(window_ref)
    window_ref[:rows, :] = bias
    hankel(window_ref, row_partner, lane0, span, hank_ref)
    rows_own = [window_ref[pl.ds(row_own + c, 1), :] for c in range(cols)]
    own_bias = [jnp.broadcast_to(b, (16, LANES)) for b in rows_own]

    def entry(m, c, q0):
        return w_ref[pl.ds(q0 + m * LANES, 16), c * LANES : (c + 1) * LANES].astype(F32)

    def weigh_own(w, m, c, q0):
        return w * hank_ref[pl.ds(q0, 16), (m + c) * LANES : (m + c + 1) * LANES]

    own = sweep(nd, nb, entry, weigh_own, lambda w, c: w * own_bias[c], acc_ref)
    own = own * jnp.concatenate(rows_own, axis=1)
    partner = antidiagonal(acc_ref, span, lane0)
    tiles = partner.shape[1] // LANES
    partner = partner * jnp.concatenate(
        [window_ref[pl.ds(row_partner + t, 1), :] for t in range(tiles)], axis=1
    )
    spread(own, partner, row_own, row_partner, placed_ref, part_ref)


def side_kernel(nd, nb, w_ref, top_ref, bottom_ref, left_ref, right_ref):
    row, lane = iota((SIDE, LANES), 0), iota((SIDE, LANES), 1)
    for out_ref, pick, first in (
        (left_ref, row == lane, 0),
        (right_ref, row + LANES - SIDE == lane, nb - LANES),
    ):
        pick = pick.astype(F32).astype(BF16)
        cols = slice(first, first + LANES)
        block = jnp.concatenate(
            [w_ref[:, cols], bottom_ref[:, cols].astype(BF16), top_ref[:, cols].astype(BF16)], axis=0
        )
        out_ref[...] = lax.dot_general(pick, block, NT, preferred_element_type=F32)


def strip_kernel(nd, nb, first, count, w_ref, top_ref, bottom_ref, left_ref, right_ref, out_ref, perm_ref, side_ref):
    stride = nb // LANES
    width = count * LANES
    lane = iota((nb, LANES), 1)
    row = iota((nb, LANES), 0)
    for k in range(count):
        hit = row == lane * stride + (first + k)
        perm_ref[:, k * LANES : (k + 1) * LANES] = hit.astype(F32).astype(BF16)
    perm = perm_ref[...]
    rims = []
    row, lane = iota((2 * SIDE, LANES), 0), iota((2 * SIDE, LANES), 1)
    bin_of = jnp.where(row < SIDE, row - SIDE, row - SIDE + nb)
    for k in range(count):
        rims.append((bin_of == lane * stride + (first + k)).astype(F32).astype(BF16))
    rims = jnp.concatenate(rims, axis=1)
    sides = jnp.concatenate([left_ref[...], right_ref[...]], axis=0).astype(BF16)
    outer = first < 0 or first + count > stride
    if outer:
        side_ref[...] = lax.dot_general(
            sides, rims, (((0,), (0,)), ((), ())), preferred_element_type=F32
        )

    def emit(block, at, side_at, rows):
        value = jnp.dot(block, perm, preferred_element_type=F32)
        if outer:
            value = value + side_ref[side_at : side_at + rows, :]
        for k in range(count):
            out_ref[k, at : at + rows, :] = value[:, k * LANES : (k + 1) * LANES].astype(BF16)

    emit(top_ref[...].astype(BF16), 0, nd + RIM, RIM)
    emit(bottom_ref[...].astype(BF16), nd + RIM, nd, RIM)
    emit(w_ref[...], RIM, 0, nd)


def unstrip_kernel(nb, out_ref):
    stride = nb // LANES
    row, lane = iota((LANES, nb), 0), iota((LANES, nb), 1)
    for s in range(stride):
        out_ref[s * LANES : (s + 1) * LANES, :] = (lane == row * stride + s).astype(F32).astype(BF16)


def columns(rows, out_ref):
    for k, row in enumerate(rows):
        out_ref[k * LANES : (k + 1) * LANES, :] = jnp.broadcast_to(row, (LANES, LANES)).T


def fan(col_ref, other_ref, start, rows, stride, out_ref):
    lane = {}
    source, offset = col_ref, start
    target = other_ref
    for bit in (64, 32, 16, 8, 4, 2, 1):
        need = rows + stride * (bit - 1)
        need = -(-need // 8) * 8
        if bit == 1:
            target = out_ref
        def move(at, size, source=source, target=target, offset=offset, bit=bit):
            low = source[pl.ds(offset + at, size), :]
            high = source[pl.ds(offset + at + stride * bit, size), :]
            odd = (iota((size, LANES), 1) & bit) > 0
            target[pl.ds(at, size), :] = jnp.where(odd, high, low)

        move(0, need)
        source, target, offset = target, source, 0


def fan_rows(nd):
    return nd + 2 * RIM + 32


def third_kernel(nd, nb, mid_ref, sums_ref, keep_ref, bias_ref, own_ref, fan_ref, near_ref, diag_ref,
                 window_ref, col_ref, other_ref, ncol_ref, nother_ref, total_ref):
    rows = keep_ref.shape[0]
    cols = nb // LANES
    stride = cols
    row_own, row_partner, lane0 = place(nd, nb)
    bias = next_bias(keep_ref[...], bias_ref[...], sums_ref[...])
    window_ref[...] = jnp.zeros_like(window_ref)
    window_ref[8 : 8 + rows, :] = bias
    for c in range(cols):
        own_ref[c : c + 1, :] = window_ref[pl.ds(8 + row_own + c, 1), :]
    tiles = col_ref.shape[0] // LANES
    columns([window_ref[pl.ds(7 + row_partner + t, 1), :] for t in range(tiles)], col_ref)
    start = LANES - RIM - 8
    if nd % LANES:
        start = start + lane0
    fan(col_ref, other_ref, start, fan_rows(nd), stride, fan_ref)
    columns([window_ref[pl.ds(7 + row_own + t, 1), :] for t in range(ncol_ref.shape[0] // LANES)], ncol_ref)
    fan(ncol_ref, nother_ref, LANES - 8, near_ref.shape[0], stride, near_ref)
    total_rows = nd + 2 * RIM

    def add(r0, size):
        total, count = None, None
        for s in range(stride):
            w = mid_ref[s, pl.ds(r0, size), :].astype(F32)
            near = jnp.broadcast_to(near_ref[8 + s : 9 + s, :], (size, LANES))
            b = w * near * fan_ref[pl.ds(r0 + 8 + s, size), :]
            v = jnp.where(w > 0.0, 1.0, 0.0)
            total = b if total is None else total + b
            count = v if count is None else count + v
        total_ref[pl.ds(r0, size), :LANES] = total
        total_ref[pl.ds(r0, size), LANES:] = count

    over(0, total_rows, total_rows // 2, add)
    padded = total_ref.shape[0]
    tiles = padded // LANES
    if padded > total_rows:
        total_ref[total_rows:, :] = jnp.zeros((padded - total_rows, 2 * LANES), F32)
    for t in range(tiles):
        for k in range(2):
            block = total_ref[t * LANES : (t + 1) * LANES, k * LANES : (k + 1) * LANES]
            diag_ref[k * tiles + t : k * tiles + t + 1, :] = jnp.sum(block.T, axis=0, keepdims=True)


def over(start, count, step, run):
    steps = count // step
    if steps > 0:

        def body(i, _):
            run(pl.multiple_of(i * step + start, math.gcd(start, step)), step)
            return 0

        lax.fori_loop(0, steps, body, 0)
    if count % step:
        run(start + steps * step, count % step)


def strips_of(stride, low_ref, mid_ref, high_ref):
    strips = {}
    for s in range(-5, 0):
        strips[s] = (low_ref, s + 5)
    for s in range(stride):
        strips[s] = (mid_ref, s)
    for s in range(stride, stride + 5):
        strips[s] = (high_ref, s - stride)
    return strips


def shift_sums(chunk, stride, step, x, h, u, l, w, t):
    def mix(r0, size):
        for s in range(stride):
            here = (s, pl.ds(r0, size), slice(None))
            at = lambda ref, k, shift: ref[k, pl.ds(r0 + shift, size), :]
            hp = at(x, s + 8, -3) + at(x, s + 9, -4) + at(x, s + 10, -5)
            hm = at(x, s, 5) + at(x, s + 1, 4) + at(x, s + 2, 3)
            ahead, behind = at(x, s + 6, -1), at(x, s + 4, 1)
            lp = hp + (ahead + at(x, s + 7, -2))
            h[here] = hp
            u[here] = hp + hm
            l[here] = lp
            w[here] = lp + (hm + (behind + at(x, s + 3, 2)))
            t[here] = ahead + at(x, s + 5, 0) + behind

    over(8, chunk + 16, step, mix)


def four_sums(s, r0, size, h, u, l, w, t):
    at = lambda ref, shift: ref[s, pl.ds(r0 + shift, size), :]
    below, above = at(u, -1), at(u, 1)
    six = lambda ref: (at(ref, -5) + at(ref, -4) + at(ref, -3)) + (at(ref, 3) + at(ref, 4) + at(ref, 5))
    donut = six(w) + ((at(u, -2) + below) + (above + at(u, 2)))
    lower = (at(l, -5) + at(l, -4) + at(l, -3)) + (at(h, -2) + at(h, -1))
    return donut, lower, six(t), below + at(u, 0) + above


def observed_kernel(nd, nb, chunk, step, base, low_ref, mid_ref, high_ref, near_ref, fan_ref, out_ref, x_ref, *refs):
    stride = nb // LANES
    strips = strips_of(stride, low_ref, mid_ref, high_ref)

    def fill(r0, size):
        for s, (ref, k) in strips.items():
            w = ref[k, pl.ds(base + r0, size), :].astype(F32)
            near = jnp.broadcast_to(near_ref[8 + s : 9 + s, :], (size, LANES))
            x_ref[s + 5, pl.ds(r0, size), :] = w * near * fan_ref[pl.ds(base + r0 + 8 + s, size), :]

    over(0, chunk + 2 * RIM, step, fill)
    shift_sums(chunk, stride, step, x_ref, *refs)

    def emit(r0, size):
        for s in range(stride):
            sums = four_sums(s, r0, size, *refs)
            for k, value in enumerate(sums + (x_ref[s + 5, pl.ds(r0, size), :],)):
                out_ref[5 * s + k, pl.ds(r0 - RIM, size), :] = value

    over(RIM, chunk, step, emit)


def score_kernel(nd, nb, chunk, step, low_ref, mid_ref, high_ref, diag_ref, perm_ref, *rest):
    stride = nb // LANES
    count = nd // chunk
    seen_refs, out_hbm = rest[:count], rest[count]
    col_ref, out_ref, sems, x_ref = rest[count + 1 : count + 5]
    refs = rest[count + 5 :]
    strips = strips_of(stride, low_ref, mid_ref, high_ref)
    tiles = diag_ref.shape[0] // 2
    expected = diag_ref[:tiles, :] / jnp.maximum(diag_ref[tiles:, :], 1.0)
    expected = jnp.where(expected > 0.0, expected, 1.0)
    columns([expected[t : t + 1, :] for t in range(tiles)], col_ref)

    def leave(i):
        here = (pl.ds(pl.multiple_of(i * chunk, 32), chunk), slice(None))
        return pltpu.make_async_copy(out_ref.at[here], out_hbm.at[here], sems.at[i])

    def score(seen_ref, base, r0, size):
        e = col_ref[pl.ds(base + r0, size), :]
        inverse = 1.0 / e
        for s in range(stride):
            sums = four_sums(s, r0, size, *refs)
            seen = [seen_ref[5 * s + k, pl.ds(r0 - RIM, size), :] for k in range(5)]
            least = None
            for k in range(4):
                ratio = (sums[k] + e) / (seen[k] + e)
                least = ratio if least is None else jnp.minimum(least, ratio)
            value = least * (seen[4] * inverse)
            hi = value.astype(BF16)
            low = (value - hi.astype(F32)).astype(BF16)
            perm = perm_ref[s * LANES : (s + 1) * LANES, :]
            placed = jnp.dot(
                jnp.concatenate([hi, low], axis=1), jnp.concatenate([perm, perm], axis=0), preferred_element_type=F32
            )
            here = pl.ds(base + r0 - RIM, size)
            out_ref[here, :] = placed if s == 0 else out_ref[here, :] + placed

    def body(i, _):
        base = pl.multiple_of(i * chunk, 32)

        def fill(r0, size):
            e = col_ref[pl.ds(base + r0, size), :]
            for s, (ref, k) in strips.items():
                w = ref[k, pl.ds(base + r0, size), :].astype(F32)
                x_ref[s + 5, pl.ds(r0, size), :] = jnp.where(w > 0.0, e, 0.0)

        over(0, chunk + 2 * RIM, step, fill)
        shift_sums(chunk, stride, step, x_ref, *refs)
        for c in range(count):

            @pl.when(i == c)
            def _():
                over(RIM, chunk, chunk, functools.partial(score, seen_refs[c], base))

        leave(i).start()
        return 0

    lax.fori_loop(0, count, body, 0)
    for i in range(count):
        leave(i).wait()


def tie(x, state, names):
    x, values = lax.optimization_barrier((x, tuple(state[name] for name in names)))
    state.update(zip(names, values))
    return x


def total(x, axes, state=None, tasks={}, due={}):
    rounds = []
    for axis in axes:
        size, bit = lax.axis_size(axis), 1
        while bit < size:
            rounds.append((axis, [(i, i ^ bit) for i in range(size)]))
            bit *= 2
    for k, (axis, pairs) in enumerate(rounds):
        if k in tasks:
            x = tie(x, state, tasks[k][0])
        came = lax.ppermute(x, axis, pairs)
        if k in tasks:
            names, task = tasks[k]
            state.update(task(*[state[name] for name in names]))
        x = x + came
        if k in due:
            x = tie(x, state, due[k])
    return x


def shifted(x, axis, step):
    size = lax.axis_size(axis)
    pairs = [(i, i + 1) for i in range(size - 1)]
    return lax.ppermute(x, axis, pairs if step > 0 else [(j, i) for i, j in pairs])


def on_device(contacts, masked_bins, chrom_bounds):
    nd, nb = contacts.shape
    cols = nb // LANES
    bins = nb * lax.axis_size("genome")
    band = nd * lax.axis_size("offset")
    rows = bins // LANES
    span = -(-nd // LANES) + cols - 1
    tall = rows + -(-band // LANES) + 24
    total_rows = nd + 2 * RIM
    shape = jax.ShapeDtypeStruct
    f = lambda *dims: shape(dims, F32)

    w, part, keep, top, bottom = pl.pallas_call(
        functools.partial(first_kernel, nd, nb),
        out_shape=(shape((nd, nb), BF16), f(rows, LANES), f(rows, LANES), f(RIM, nb), f(RIM, nb)),
        in_specs=[HBM] * 3,
        out_specs=(VMEM,) * 5,
        scratch_shapes=[
            pltpu.VMEM((tall, LANES), F32),
            pltpu.VMEM((LANES, span * LANES), F32),
            pltpu.VMEM((LANES, span * LANES), F32),
            pltpu.VMEM((tall, LANES), F32),
            pltpu.SMEM(chrom_bounds.shape, jnp.int32),
            pltpu.VMEM((nd, nb), BF16),
            pltpu.VMEM((1,) + masked_bins.shape, jnp.int32),
            pltpu.SemaphoreType.DMA((3,)),
        ],
        compiler_params=params(12),
        name="first_sums",
    )(*(pltpu.with_memory_space_constraint(a, pltpu.HBM) for a in (chrom_bounds, contacts, masked_bins.reshape(1, -1))))

    def sides(w, above, below):
        return pl.pallas_call(
            functools.partial(side_kernel, nd, nb),
            out_shape=(f(SIDE, total_rows), f(SIDE, total_rows)),
            in_specs=[VMEM] * 3,
            out_specs=(VMEM,) * 2,
            compiler_params=params(16),
            name="sides",
        )(w, above, below)

    def first_side(w, above, below):
        left, right = sides(w, above, below)
        return dict(right=right, after=shifted(left, "genome", -1))

    state = dict(w=w, top=top, bottom=bottom)
    tasks = {
        0: (("bottom",), lambda bottom: dict(above=shifted(bottom, "offset", 1))),
        1: (("top",), lambda top: dict(below=shifted(top, "offset", -1))),
        3: (("w", "above", "below"), first_side),
    }
    sums = total(part, ("genome", "offset"), state, tasks, {1: ("above",), 2: ("below",)})
    w = state["w"]

    part, bias = pl.pallas_call(
        functools.partial(second_kernel, nd, nb),
        out_shape=(f(rows, LANES), f(rows, LANES)),
        in_specs=[VMEM] * 3,
        out_specs=(VMEM,) * 2,
        scratch_shapes=[
            pltpu.VMEM((tall, LANES), F32),
            pltpu.VMEM((LANES, span * LANES), F32),
            pltpu.VMEM((LANES, span * LANES), F32),
            pltpu.VMEM((tall, LANES), F32),
        ],
        compiler_params=params(),
        name="second_sums",
    )(w, sums, keep)

    def strip(name, first, count):
        def run(*operands):
            strips = pl.pallas_call(
                functools.partial(strip_kernel, nd, nb, first, count),
                out_shape=shape((count, total_rows, LANES), BF16),
                in_specs=[VMEM] * 5,
                out_specs=VMEM,
                scratch_shapes=[
                    pltpu.VMEM((nb, count * LANES), BF16),
                    pltpu.VMEM((total_rows, count * LANES), F32),
                ],
                compiler_params=params(24),
                name="strips",
            )(*operands)
            return {name: strips}

        side = dict(low="before", mid="above", high="after")[name]
        return ("w", "above", "below", side, side), run

    def back(_, right):
        matrix = pl.pallas_call(
            functools.partial(unstrip_kernel, nb),
            out_shape=shape((nb, nb), BF16),
            out_specs=VMEM,
            compiler_params=params(8),
            name="unstrip",
        )()
        return dict(perm=matrix, before=shifted(right, "genome", 1))

    tasks = {
        0: (("keep", "right"), back),
        1: strip("mid", 0, cols),
        2: strip("high", cols, 5),
        3: strip("low", -5, 5),
    }
    state["keep"] = keep
    due = {0: ("perm", "after"), 1: ("mid",), 2: ("high", "before"), 3: ("low",)}
    sums = total(part, ("genome", "offset"), state, tasks, due)
    low, high, mid, perm, keep = (state[name] for name in ("low", "high", "mid", "perm", "keep"))

    padded = -(-total_rows // LANES) * LANES
    fan_len = fan_rows(nd)
    reach = -(-(fan_len + cols * (LANES - 1) + 2 * LANES) // LANES) * LANES
    near = 24
    near_reach = -(-(near + cols * (LANES - 1) + LANES) // LANES) * LANES
    own, fans, nears, diag = pl.pallas_call(
        functools.partial(third_kernel, nd, nb),
        out_shape=(f(cols, LANES), f(fan_len, LANES), f(near, LANES), f(2 * padded // LANES, LANES)),
        in_specs=[VMEM] * 4,
        out_specs=(VMEM,) * 4,
        scratch_shapes=[
            pltpu.VMEM((tall + 8, LANES), F32),
            pltpu.VMEM((reach, LANES), F32),
            pltpu.VMEM((reach, LANES), F32),
            pltpu.VMEM((near_reach, LANES), F32),
            pltpu.VMEM((near_reach, LANES), F32),
            pltpu.VMEM((padded, 2 * LANES), F32),
        ],
        compiler_params=params(),
        name="diagonal_sums",
    )(mid, sums, keep, bias)
    chunk = next(c for c in (320, 256, 128, 64, 32) if nd % c == 0)
    count = nd // chunk
    tall = chunk + 2 * RIM
    scratch = [pltpu.VMEM((tiles, tall, LANES), F32) for tiles in (cols + 10,) + (cols,) * 5]

    def observe(*which):
        def run(*operands):
            made = {}
            for c in which:
                made[f"seen{c}"] = pl.pallas_call(
                    functools.partial(observed_kernel, nd, nb, chunk, STEP, c * chunk),
                    out_shape=f(5 * cols, chunk, LANES),
                    in_specs=[VMEM] * 5,
                    out_specs=VMEM,
                    scratch_shapes=scratch,
                    compiler_params=params(20),
                    name="observed",
                )(*operands)
            return made

        return ("low", "mid", "high", "near", "fan"), run

    rounds = (lax.axis_size("genome") - 1).bit_length()
    turns = {}
    for c in range(count):
        turns.setdefault((c + 1) * (rounds - 1) // count, []).append(c)
    state.update(near=nears, fan=fans)
    diag = total(
        diag,
        ("genome",),
        state,
        {k: observe(*which) for k, which in turns.items()},
        {k: tuple(f"seen{c}" for c in which) for k, which in turns.items()},
    )

    operands = (low, mid, high, diag, perm) + tuple(state[f"seen{c}"] for c in range(count))
    score = pl.pallas_call(
        functools.partial(score_kernel, nd, nb, chunk, STEP),
        out_shape=f(nd, nb),
        in_specs=[VMEM] * len(operands),
        out_specs=HBM,
        scratch_shapes=[
            pltpu.VMEM((padded, LANES), F32),
            pltpu.VMEM((nd, nb), F32),
            pltpu.SemaphoreType.DMA((count,)),
        ]
        + scratch,
        compiler_params=params(24),
        name="score",
    )(*operands)
    return score, own.reshape(nb)


def solution(mesh):
    return jax.shard_map(
        on_device,
        mesh=mesh,
        in_specs=(P("offset", "genome"), P(), P()),
        out_specs=(P("offset", "genome"), P("genome")),
        check_vma=False,
    )
```

```python
import functools
import math

import jax
import jax.numpy as jnp
from jax import lax
from jax.experimental import pallas as pl
from jax.experimental.pallas import tpu as pltpu
from jax.sharding import PartitionSpec as P

RIM = 16
STEP = 176
SIDE = 8
LANES = 128
F32 = jnp.float32
BF16 = jnp.bfloat16
TINY = 2.0**-126
VMEM = pl.BlockSpec(memory_space=pltpu.VMEM)
HBM = pl.BlockSpec(memory_space=pltpu.HBM)
ANY = pl.BlockSpec(memory_space=pl.ANY)
NT = (((1,), (1,)), ((), ()))


def params(mib=48):
    return pltpu.CompilerParams(vmem_limit_bytes=mib << 20)


def iota(shape, dim):
    return lax.broadcasted_iota(jnp.int32, shape, dim)


def place(nd, nb):
    first = lax.axis_index("genome") * nb
    partner = first + lax.axis_index("offset") * nd
    return first // LANES, partner // LANES, partner % LANES


def roll(x, shift):
    length = x.shape[1]
    if isinstance(shift, int):
        shift = shift % length
        if shift == 0:
            return x
    return pltpu.roll(x, shift, 1)


def hankel(rows_ref, row0, lane0, tiles, out_ref):
    extra = 1 if lane0 is None else 2
    base = jnp.concatenate(
        [jnp.broadcast_to(rows_ref[pl.ds(row0 + t, 1), :], (8, LANES)) for t in range(tiles + extra)],
        axis=1,
    )
    length = base.shape[1]
    if lane0 is not None:
        base = roll(base, length - lane0)
    sub = iota(base.shape, 0)
    for bit in (1, 2, 4):
        base = jnp.where((sub & bit) > 0, roll(base, length - bit), base)
    for r in range(16):
        out_ref[8 * r : 8 * r + 8, : tiles * LANES] = roll(base, length - 8 * r)[:, : tiles * LANES]


def antidiagonal(acc_ref, tiles, lane0):
    extra = 1 if lane0 is None else 2
    pad = jnp.zeros((8, extra * LANES), F32)
    parts = [jnp.concatenate([acc_ref[8 * r : 8 * r + 8, : tiles * LANES], pad], axis=1) for r in range(16)]
    shift = 8
    while len(parts) > 1:
        parts = [low + roll(high, shift) for low, high in zip(parts[::2], parts[1::2])]
        shift *= 2
    total = parts[0]
    sub = iota(total.shape, 0)
    for bit in (4, 2, 1):
        total = jnp.where((sub & bit) > 0, roll(total, bit), total)
    total = jnp.sum(total, axis=0, keepdims=True)
    if lane0 is not None:
        total = roll(total, lane0)
    return total


def spread(own, partner, row_own, row_partner, placed_ref, out_ref):
    placed_ref[...] = jnp.zeros_like(placed_ref)
    for t in range(partner.shape[1] // LANES):
        placed_ref[pl.ds(row_partner + t, 1), :] = partner[:, t * LANES : (t + 1) * LANES]
    for c in range(own.shape[1] // LANES):
        placed_ref[pl.ds(row_own + c, 1), :] += own[:, c * LANES : (c + 1) * LANES]
    out_ref[...] = placed_ref[: out_ref.shape[0], :]


def sweep(nd, nb, entry, weigh_own, weigh_partner, acc_ref):
    cols = nb // LANES
    full, rest = nd // LANES, nd % LANES
    first_diag = lax.axis_index("offset") * nd
    sub = iota((16, LANES), 0)

    def body(ms, fresh, r, own):
        own = list(own)
        q0 = pl.multiple_of(16 * r, 16)
        sums = {}
        for m in ms:
            for c in range(cols):
                w = entry(m, c, q0)
                own[c] = own[c] + weigh_own(w, m, c, q0)
                g = weigh_partner(w, c)
                if m == 0:
                    g = jnp.where(sub + q0 + first_diag > 0, g, 0.0)
                sums[m + c] = sums[m + c] + g if m + c in sums else g
        for t, value in sums.items():
            tile = (pl.ds(q0, 16), slice(t * LANES, (t + 1) * LANES))
            acc_ref[tile] = value if fresh else acc_ref[tile] + value
        return tuple(own)

    own = tuple(jnp.zeros((16, LANES), F32) for _ in range(cols))
    if rest:
        acc_ref[...] = jnp.zeros_like(acc_ref)
    own = lax.fori_loop(0, 8, functools.partial(body, range(full), not rest), own)
    if rest:
        own = lax.fori_loop(0, rest // 16, functools.partial(body, [full], False), own)
    return jnp.concatenate([jnp.sum(o, axis=0, keepdims=True) for o in own], axis=1)


def keep_of(masked, rows):
    count = masked.shape[1]
    in_row = (jnp.broadcast_to(masked >> 7, (rows, count)) == iota((rows, count), 0))
    in_lane = (jnp.broadcast_to(masked & 127, (LANES, count)) == iota((LANES, count), 0))
    hits = lax.dot_general(
        in_row.astype(F32).astype(BF16), in_lane.astype(F32).astype(BF16), NT, preferred_element_type=F32
    )
    return jnp.where(hits > 0.0, 0.0, 1.0)


def first_kernel(nd, nb, bounds_hbm, x_hbm, masked_hbm, w_ref, part_ref, keep_ref, top_ref, bottom_ref,
                 codes_ref, hank_ref, acc_ref, placed_ref, bounds_ref, x_ref, masked_ref, sems):
    copies = [
        pltpu.make_async_copy(source, target, sems.at[k])
        for k, (source, target) in enumerate(
            ((masked_hbm, masked_ref), (bounds_hbm, bounds_ref), (x_hbm, x_ref))
        )
    ]
    for copy in copies:
        copy.start()
    copies[0].wait()
    copies[1].wait()
    rows = keep_ref.shape[0]
    cols = nb // LANES
    span = -(-nd // LANES) + cols - 1
    row_own, row_partner, lane0 = place(nd, nb)
    lane0 = lane0 if nd % LANES else None
    keep = keep_of(masked_ref[...], rows)
    keep_ref[...] = keep
    bins = iota((rows, LANES), 0) * LANES + iota((rows, LANES), 1)
    chrom = jnp.zeros((rows, LANES), F32)
    for k in range(bounds_ref.shape[0]):
        chrom = chrom + jnp.where(bins >= bounds_ref[k], 1.0, 0.0)
    codes_ref[...] = jnp.full_like(codes_ref, -2.0)
    codes_ref[:rows, :] = jnp.where(keep > 0.0, chrom, -2.0)
    hankel(codes_ref, row_partner, lane0, span, hank_ref)
    code_own = []
    for c in range(cols):
        code = codes_ref[pl.ds(row_own + c, 1), :]
        code = jnp.where(code < 0.0, -1.0, code)
        code_own.append(jnp.broadcast_to(code, (16, LANES)))
    copies[2].wait()

    def entry(m, c, q0):
        here = (pl.ds(q0 + m * LANES, 16), slice(c * LANES, (c + 1) * LANES))
        code = hank_ref[pl.ds(q0, 16), (m + c) * LANES : (m + c + 1) * LANES]
        value = jnp.maximum(x_ref[here].astype(F32), TINY)
        w = jnp.where(code == code_own[c], value, 0.0)
        w_ref[here] = w.astype(BF16)
        return w

    own = sweep(nd, nb, entry, lambda w, m, c, q0: w, lambda w, c: w, acc_ref)
    spread(own, antidiagonal(acc_ref, span, lane0), row_own, row_partner, placed_ref, part_ref)
    top_ref[...] = w_ref[:RIM, :].astype(F32)
    bottom_ref[...] = w_ref[nd - RIM :, :].astype(F32)


def next_bias(keep, bias, sums):
    level = jnp.sum(sums * keep, keepdims=True) / jnp.sum(keep, keepdims=True)
    safe = jnp.where(keep > 0.0, sums, 1.0)
    return jnp.where(keep > 0.0, bias * level / safe, 0.0)


def second_kernel(nd, nb, w_ref, sums_ref, keep_ref, part_ref, bias_ref, window_ref, hank_ref, acc_ref, placed_ref):
    rows = keep_ref.shape[0]
    cols = nb // LANES
    span = -(-nd // LANES) + cols - 1
    row_own, row_partner, lane0 = place(nd, nb)
    lane0 = lane0 if nd % LANES else None
    bias = next_bias(keep_ref[...], keep_ref[...], sums_ref[...])
    bias_ref[...] = bias
    window_ref[...] = jnp.zeros_like(window_ref)
    window_ref[:rows, :] = bias
    hankel(window_ref, row_partner, lane0, span, hank_ref)
    rows_own = [window_ref[pl.ds(row_own + c, 1), :] for c in range(cols)]
    own_bias = [jnp.broadcast_to(b, (16, LANES)) for b in rows_own]

    def entry(m, c, q0):
        return w_ref[pl.ds(q0 + m * LANES, 16), c * LANES : (c + 1) * LANES].astype(F32)

    def weigh_own(w, m, c, q0):
        return w * hank_ref[pl.ds(q0, 16), (m + c) * LANES : (m + c + 1) * LANES]

    own = sweep(nd, nb, entry, weigh_own, lambda w, c: w * own_bias[c], acc_ref)
    own = own * jnp.concatenate(rows_own, axis=1)
    partner = antidiagonal(acc_ref, span, lane0)
    tiles = partner.shape[1] // LANES
    partner = partner * jnp.concatenate(
        [window_ref[pl.ds(row_partner + t, 1), :] for t in range(tiles)], axis=1
    )
    spread(own, partner, row_own, row_partner, placed_ref, part_ref)


def side_kernel(nd, nb, w_ref, top_ref, bottom_ref, left_ref, right_ref):
    row, lane = iota((SIDE, LANES), 0), iota((SIDE, LANES), 1)
    for out_ref, pick, first in (
        (left_ref, row == lane, 0),
        (right_ref, row + LANES - SIDE == lane, nb - LANES),
    ):
        pick = pick.astype(F32).astype(BF16)
        cols = slice(first, first + LANES)
        block = jnp.concatenate(
            [w_ref[:, cols], bottom_ref[:, cols].astype(BF16), top_ref[:, cols].astype(BF16)], axis=0
        )
        out_ref[...] = lax.dot_general(pick, block, NT, preferred_element_type=F32)


def strip_kernel(nd, nb, first, count, w_ref, top_ref, bottom_ref, left_ref, right_ref, out_ref, perm_ref, side_ref):
    stride = nb // LANES
    width = count * LANES
    lane = iota((nb, LANES), 1)
    row = iota((nb, LANES), 0)
    for k in range(count):
        hit = row == lane * stride + (first + k)
        perm_ref[:, k * LANES : (k + 1) * LANES] = hit.astype(F32).astype(BF16)
    perm = perm_ref[...]
    rims = []
    row, lane = iota((2 * SIDE, LANES), 0), iota((2 * SIDE, LANES), 1)
    bin_of = jnp.where(row < SIDE, row - SIDE, row - SIDE + nb)
    for k in range(count):
        rims.append((bin_of == lane * stride + (first + k)).astype(F32).astype(BF16))
    rims = jnp.concatenate(rims, axis=1)
    sides = jnp.concatenate([left_ref[...], right_ref[...]], axis=0).astype(BF16)
    outer = first < 0 or first + count > stride
    if outer:
        side_ref[...] = lax.dot_general(
            sides, rims, (((0,), (0,)), ((), ())), preferred_element_type=F32
        )

    def emit(block, at, side_at, rows):
        value = jnp.dot(block, perm, preferred_element_type=F32)
        if outer:
            value = value + side_ref[side_at : side_at + rows, :]
        for k in range(count):
            out_ref[k, at : at + rows, :] = value[:, k * LANES : (k + 1) * LANES].astype(BF16)

    emit(top_ref[...].astype(BF16), 0, nd + RIM, RIM)
    emit(bottom_ref[...].astype(BF16), nd + RIM, nd, RIM)
    emit(w_ref[...], RIM, 0, nd)


def unstrip_kernel(nb, out_ref):
    stride = nb // LANES
    row, lane = iota((LANES, nb), 0), iota((LANES, nb), 1)
    for s in range(stride):
        out_ref[s * LANES : (s + 1) * LANES, :] = (lane == row * stride + s).astype(F32).astype(BF16)


def columns(rows, out_ref):
    for k, row in enumerate(rows):
        out_ref[k * LANES : (k + 1) * LANES, :] = jnp.broadcast_to(row, (LANES, LANES)).T


def fan(col_ref, other_ref, start, rows, stride, out_ref):
    lane = {}
    source, offset = col_ref, start
    target = other_ref
    for bit in (64, 32, 16, 8, 4, 2, 1):
        need = rows + stride * (bit - 1)
        need = -(-need // 8) * 8
        if bit == 1:
            target = out_ref
        def move(at, size, source=source, target=target, offset=offset, bit=bit):
            low = source[pl.ds(offset + at, size), :]
            high = source[pl.ds(offset + at + stride * bit, size), :]
            odd = (iota((size, LANES), 1) & bit) > 0
            target[pl.ds(at, size), :] = jnp.where(odd, high, low)

        move(0, need)
        source, target, offset = target, source, 0


def fan_rows(nd):
    return nd + 2 * RIM + 32


def third_kernel(nd, nb, mid_ref, sums_ref, keep_ref, bias_ref, own_ref, fan_ref, near_ref, diag_ref,
                 window_ref, col_ref, other_ref, ncol_ref, nother_ref, total_ref):
    rows = keep_ref.shape[0]
    cols = nb // LANES
    stride = cols
    row_own, row_partner, lane0 = place(nd, nb)
    bias = next_bias(keep_ref[...], bias_ref[...], sums_ref[...])
    window_ref[...] = jnp.zeros_like(window_ref)
    window_ref[8 : 8 + rows, :] = bias
    for c in range(cols):
        own_ref[c : c + 1, :] = window_ref[pl.ds(8 + row_own + c, 1), :]
    tiles = col_ref.shape[0] // LANES
    columns([window_ref[pl.ds(7 + row_partner + t, 1), :] for t in range(tiles)], col_ref)
    start = LANES - RIM - 8
    if nd % LANES:
        start = start + lane0
    fan(col_ref, other_ref, start, fan_rows(nd), stride, fan_ref)
    columns([window_ref[pl.ds(7 + row_own + t, 1), :] for t in range(ncol_ref.shape[0] // LANES)], ncol_ref)
    fan(ncol_ref, nother_ref, LANES - 8, near_ref.shape[0], stride, near_ref)
    total_rows = nd + 2 * RIM

    def add(r0, size):
        total, count = None, None
        for s in range(stride):
            w = mid_ref[s, pl.ds(r0, size), :].astype(F32)
            near = jnp.broadcast_to(near_ref[8 + s : 9 + s, :], (size, LANES))
            b = w * near * fan_ref[pl.ds(r0 + 8 + s, size), :]
            v = jnp.where(w > 0.0, 1.0, 0.0)
            total = b if total is None else total + b
            count = v if count is None else count + v
        total_ref[pl.ds(r0, size), :LANES] = total
        total_ref[pl.ds(r0, size), LANES:] = count

    over(0, total_rows, total_rows // 2, add)
    padded = total_ref.shape[0]
    tiles = padded // LANES
    if padded > total_rows:
        total_ref[total_rows:, :] = jnp.zeros((padded - total_rows, 2 * LANES), F32)
    for t in range(tiles):
        for k in range(2):
            block = total_ref[t * LANES : (t + 1) * LANES, k * LANES : (k + 1) * LANES]
            diag_ref[k * tiles + t : k * tiles + t + 1, :] = jnp.sum(block.T, axis=0, keepdims=True)


def over(start, count, step, run):
    steps = count // step
    if steps > 0:

        def body(i, _):
            run(pl.multiple_of(i * step + start, math.gcd(start, step)), step)
            return 0

        lax.fori_loop(0, steps, body, 0)
    if count % step:
        run(start + steps * step, count % step)


STRIPS = ("low", "last", "mid", "high", "final")


def strips_of(refs):
    return dict(enumerate(((ref, k) for ref in refs for k in range(ref.shape[0])), -5))


def shift_sums(chunk, stride, step, x, h, u, l, w, t):
    def mix(r0, size):
        for s in range(stride):
            here = (s, pl.ds(r0, size), slice(None))
            at = lambda ref, k, shift: ref[k, pl.ds(r0 + shift, size), :]
            hp = at(x, s + 8, -3) + at(x, s + 9, -4) + at(x, s + 10, -5)
            hm = at(x, s, 5) + at(x, s + 1, 4) + at(x, s + 2, 3)
            ahead, behind = at(x, s + 6, -1), at(x, s + 4, 1)
            lp = hp + (ahead + at(x, s + 7, -2))
            h[here] = hp
            u[here] = hp + hm
            l[here] = lp
            w[here] = lp + (hm + (behind + at(x, s + 3, 2)))
            t[here] = ahead + at(x, s + 5, 0) + behind

    over(8, chunk + 16, step, mix)


def four_sums(s, r0, size, h, u, l, w, t):
    at = lambda ref, shift: ref[s, pl.ds(r0 + shift, size), :]
    below, above = at(u, -1), at(u, 1)
    six = lambda ref: (at(ref, -5) + at(ref, -4) + at(ref, -3)) + (at(ref, 3) + at(ref, 4) + at(ref, 5))
    donut = six(w) + ((at(u, -2) + below) + (above + at(u, 2)))
    lower = (at(l, -5) + at(l, -4) + at(l, -3)) + (at(h, -2) + at(h, -1))
    return donut, lower, six(t), below + at(u, 0) + above


def observed_kernel(nd, nb, chunk, step, base, *refs):
    stride = nb // LANES
    strips = strips_of(refs[: len(STRIPS)])
    near_ref, fan_ref, out_ref, x_ref, *refs = refs[len(STRIPS) :]

    def fill(r0, size):
        for s, (ref, k) in strips.items():
            w = ref[k, pl.ds(base + r0, size), :].astype(F32)
            near = jnp.broadcast_to(near_ref[8 + s : 9 + s, :], (size, LANES))
            x_ref[s + 5, pl.ds(r0, size), :] = w * near * fan_ref[pl.ds(base + r0 + 8 + s, size), :]

    over(0, chunk + 2 * RIM, step, fill)
    shift_sums(chunk, stride, step, x_ref, *refs)

    def emit(r0, size):
        for s in range(stride):
            sums = four_sums(s, r0, size, *refs)
            for k, value in enumerate(sums + (x_ref[s + 5, pl.ds(r0, size), :],)):
                out_ref[5 * s + k, pl.ds(r0 - RIM, size), :] = value

    over(RIM, chunk, step, emit)


def score_kernel(nd, nb, chunk, step, *rest):
    stride = nb // LANES
    count = nd // chunk
    strips = strips_of(rest[: len(STRIPS)])
    diag_ref, perm_ref, *rest = rest[len(STRIPS) :]
    seen_refs, out_hbm = rest[:count], rest[count]
    col_ref, out_ref, sems, x_ref = rest[count + 1 : count + 5]
    refs = rest[count + 5 :]
    tiles = diag_ref.shape[0] // 2
    expected = diag_ref[:tiles, :] / jnp.maximum(diag_ref[tiles:, :], 1.0)
    expected = jnp.where(expected > 0.0, expected, 1.0)
    columns([expected[t : t + 1, :] for t in range(tiles)], col_ref)

    def leave(i):
        here = (pl.ds(pl.multiple_of(i * chunk, 32), chunk), slice(None))
        return pltpu.make_async_copy(out_ref.at[here], out_hbm.at[here], sems.at[i])

    def score(seen_ref, base, r0, size):
        e = col_ref[pl.ds(base + r0, size), :]
        inverse = 1.0 / e
        for s in range(stride):
            sums = four_sums(s, r0, size, *refs)
            seen = [seen_ref[5 * s + k, pl.ds(r0 - RIM, size), :] for k in range(5)]
            least = None
            for k in range(4):
                ratio = (sums[k] + e) / (seen[k] + e)
                least = ratio if least is None else jnp.minimum(least, ratio)
            value = least * (seen[4] * inverse)
            hi = value.astype(BF16)
            low = (value - hi.astype(F32)).astype(BF16)
            perm = perm_ref[s * LANES : (s + 1) * LANES, :]
            placed = jnp.dot(
                jnp.concatenate([hi, low], axis=1), jnp.concatenate([perm, perm], axis=0), preferred_element_type=F32
            )
            here = pl.ds(base + r0 - RIM, size)
            out_ref[here, :] = placed if s == 0 else out_ref[here, :] + placed

    def body(i, _):
        base = pl.multiple_of(i * chunk, 32)

        def fill(r0, size):
            e = col_ref[pl.ds(base + r0, size), :]
            for s, (ref, k) in strips.items():
                w = ref[k, pl.ds(base + r0, size), :].astype(F32)
                x_ref[s + 5, pl.ds(r0, size), :] = jnp.where(w > 0.0, e, 0.0)

        over(0, chunk + 2 * RIM, step, fill)
        shift_sums(chunk, stride, step, x_ref, *refs)
        for c in range(count):

            @pl.when(i == c)
            def _():
                over(RIM, chunk, chunk, functools.partial(score, seen_refs[c], base))

        leave(i).start()
        return 0

    lax.fori_loop(0, count, body, 0)
    for i in range(count):
        leave(i).wait()


def tie(x, state, names):
    x, values = lax.optimization_barrier((x, tuple(state[name] for name in names)))
    state.update(zip(names, values))
    return x


def total(x, axes, state=None, tasks={}, due={}):
    rounds = []
    for axis in axes:
        size, bit = lax.axis_size(axis), 1
        while bit < size:
            rounds.append((axis, [(i, i ^ bit) for i in range(size)]))
            bit *= 2
    for k, (axis, pairs) in enumerate(rounds):
        if k in tasks:
            x = tie(x, state, tasks[k][0])
        came = lax.ppermute(x, axis, pairs)
        if k in tasks:
            names, task = tasks[k]
            state.update(task(*[state[name] for name in names]))
        x = x + came
        if k in due:
            x = tie(x, state, due[k])
    return x


def shifted(x, axis, step):
    size = lax.axis_size(axis)
    pairs = [(i, i + 1) for i in range(size - 1)]
    return lax.ppermute(x, axis, pairs if step > 0 else [(j, i) for i, j in pairs])


def on_device(contacts, masked_bins, chrom_bounds):
    nd, nb = contacts.shape
    cols = nb // LANES
    bins = nb * lax.axis_size("genome")
    band = nd * lax.axis_size("offset")
    rows = bins // LANES
    span = -(-nd // LANES) + cols - 1
    tall = rows + -(-band // LANES) + 24
    total_rows = nd + 2 * RIM
    shape = jax.ShapeDtypeStruct
    f = lambda *dims: shape(dims, F32)

    w, part, keep, top, bottom = pl.pallas_call(
        functools.partial(first_kernel, nd, nb),
        out_shape=(shape((nd, nb), BF16), f(rows, LANES), f(rows, LANES), f(RIM, nb), f(RIM, nb)),
        in_specs=[HBM] * 3,
        out_specs=(VMEM,) * 5,
        scratch_shapes=[
            pltpu.VMEM((tall, LANES), F32),
            pltpu.VMEM((LANES, span * LANES), F32),
            pltpu.VMEM((LANES, span * LANES), F32),
            pltpu.VMEM((tall, LANES), F32),
            pltpu.SMEM(chrom_bounds.shape, jnp.int32),
            pltpu.VMEM((nd, nb), BF16),
            pltpu.VMEM((1,) + masked_bins.shape, jnp.int32),
            pltpu.SemaphoreType.DMA((3,)),
        ],
        compiler_params=params(12),
        name="first_sums",
    )(*(pltpu.with_memory_space_constraint(a, pltpu.HBM) for a in (chrom_bounds, contacts, masked_bins.reshape(1, -1))))

    def sides(w, above, below):
        return pl.pallas_call(
            functools.partial(side_kernel, nd, nb),
            out_shape=(f(SIDE, total_rows), f(SIDE, total_rows)),
            in_specs=[VMEM] * 3,
            out_specs=(VMEM,) * 2,
            compiler_params=params(16),
            name="sides",
        )(w, above, below)

    def first_side(w, above, below):
        left, right = sides(w, above, below)
        return dict(right=right, after=shifted(left, "genome", -1))

    state = dict(w=w, top=top, bottom=bottom)
    tasks = {
        0: (("bottom",), lambda bottom: dict(above=shifted(bottom, "offset", 1))),
        1: (("top",), lambda top: dict(below=shifted(top, "offset", -1))),
        3: (("w", "above", "below"), first_side),
    }
    sums = total(part, ("offset", "genome"), state, tasks, {1: ("above",), 2: ("below",)})
    w = state["w"]

    part, bias = pl.pallas_call(
        functools.partial(second_kernel, nd, nb),
        out_shape=(f(rows, LANES), f(rows, LANES)),
        in_specs=[VMEM] * 3,
        out_specs=(VMEM,) * 2,
        scratch_shapes=[
            pltpu.VMEM((tall, LANES), F32),
            pltpu.VMEM((LANES, span * LANES), F32),
            pltpu.VMEM((LANES, span * LANES), F32),
            pltpu.VMEM((tall, LANES), F32),
        ],
        compiler_params=params(),
        name="second_sums",
    )(w, sums, keep)

    def strip(name, first, count):
        def run(*operands):
            strips = pl.pallas_call(
                functools.partial(strip_kernel, nd, nb, first, count),
                out_shape=shape((count, total_rows, LANES), BF16),
                in_specs=[VMEM] * 5,
                out_specs=VMEM,
                scratch_shapes=[
                    pltpu.VMEM((nb, count * LANES), BF16),
                    pltpu.VMEM((total_rows, count * LANES), F32),
                ],
                compiler_params=params(24),
                name="strips",
            )(*operands)
            return {name: strips}

        side = dict(low="before", last="before", mid="above", high="after", final="after")[name]
        return ("w", "above", "below", side, side), run

    def ends(w, above, below, before, after):
        made = strip("last", -1, 1)[1](w, above, below, before, before)
        made.update(strip("final", cols + 4, 1)[1](w, above, below, after, after))
        return made

    def back(_, right):
        matrix = pl.pallas_call(
            functools.partial(unstrip_kernel, nb),
            out_shape=shape((nb, nb), BF16),
            out_specs=VMEM,
            compiler_params=params(8),
            name="unstrip",
        )()
        return dict(perm=matrix, before=shifted(right, "genome", 1))

    tasks = {
        0: (("keep", "right"), back),
        1: strip("mid", 0, cols),
        2: strip("high", cols, 4),
        3: strip("low", -5, 4),
        4: (("w", "above", "below", "before", "after"), ends),
    }
    state["keep"] = keep
    due = {0: ("perm", "after"), 1: ("mid",), 2: ("high", "before"), 3: ("low",), 4: ("last", "final")}
    sums = total(part, ("offset", "genome"), state, tasks, due)
    mid, perm, keep = (state[name] for name in ("mid", "perm", "keep"))

    padded = -(-total_rows // LANES) * LANES
    fan_len = fan_rows(nd)
    reach = -(-(fan_len + cols * (LANES - 1) + 2 * LANES) // LANES) * LANES
    near = 24
    near_reach = -(-(near + cols * (LANES - 1) + LANES) // LANES) * LANES
    own, fans, nears, diag = pl.pallas_call(
        functools.partial(third_kernel, nd, nb),
        out_shape=(f(cols, LANES), f(fan_len, LANES), f(near, LANES), f(2 * padded // LANES, LANES)),
        in_specs=[VMEM] * 4,
        out_specs=(VMEM,) * 4,
        scratch_shapes=[
            pltpu.VMEM((tall + 8, LANES), F32),
            pltpu.VMEM((reach, LANES), F32),
            pltpu.VMEM((reach, LANES), F32),
            pltpu.VMEM((near_reach, LANES), F32),
            pltpu.VMEM((near_reach, LANES), F32),
            pltpu.VMEM((padded, 2 * LANES), F32),
        ],
        compiler_params=params(),
        name="diagonal_sums",
    )(mid, sums, keep, bias)
    chunk = next(c for c in (320, 256, 128, 64, 32) if nd % c == 0)
    count = nd // chunk
    tall = chunk + 2 * RIM
    scratch = [pltpu.VMEM((tiles, tall, LANES), F32) for tiles in (cols + 10,) + (cols,) * 5]

    def observe(*which):
        def run(*operands):
            made = {}
            for c in which:
                made[f"seen{c}"] = pl.pallas_call(
                    functools.partial(observed_kernel, nd, nb, chunk, STEP, c * chunk),
                    out_shape=f(5 * cols, chunk, LANES),
                    in_specs=[VMEM] * len(operands),
                    out_specs=VMEM,
                    scratch_shapes=scratch,
                    compiler_params=params(20),
                    name="observed",
                )(*operands)
            return made

        return STRIPS + ("near", "fan"), run

    rounds = (lax.axis_size("genome") - 1).bit_length()
    turns = {}
    for c in range(count):
        turns.setdefault((c + 1) * (rounds - 1) // count, []).append(c)
    state.update(near=nears, fan=fans)
    diag = total(
        diag,
        ("genome",),
        state,
        {k: observe(*which) for k, which in turns.items()},
        {k: tuple(f"seen{c}" for c in which) for k, which in turns.items()},
    )

    operands = tuple(state[name] for name in STRIPS) + (diag, perm) + tuple(state[f"seen{c}"] for c in range(count))
    score = pl.pallas_call(
        functools.partial(score_kernel, nd, nb, chunk, STEP),
        out_shape=f(nd, nb),
        in_specs=[VMEM] * len(operands),
        out_specs=HBM,
        scratch_shapes=[
            pltpu.VMEM((padded, LANES), F32),
            pltpu.VMEM((nd, nb), F32),
            pltpu.SemaphoreType.DMA((count,)),
        ]
        + scratch,
        compiler_params=params(24),
        name="score",
    )(*operands)
    return score, own.reshape(nb)


def solution(mesh):
    return jax.shard_map(
        on_device,
        mesh=mesh,
        in_specs=(P("offset", "genome"), P(), P()),
        out_specs=(P("offset", "genome"), P("genome")),
        check_vma=False,
    )
```

```python
import functools
import math

import jax
import jax.numpy as jnp
from jax import lax
from jax.experimental import pallas as pl
from jax.experimental.pallas import tpu as pltpu
from jax.sharding import PartitionSpec as P

RIM = 16
STEP = 88
SIDE = 8
LANES = 128
F32 = jnp.float32
BF16 = jnp.bfloat16
TINY = 2.0**-126
VMEM = pl.BlockSpec(memory_space=pltpu.VMEM)
HBM = pl.BlockSpec(memory_space=pltpu.HBM)
ANY = pl.BlockSpec(memory_space=pl.ANY)
NT = (((1,), (1,)), ((), ()))


def params(mib=48):
    return pltpu.CompilerParams(vmem_limit_bytes=mib << 20)


def iota(shape, dim):
    return lax.broadcasted_iota(jnp.int32, shape, dim)


def place(nd, nb):
    first = lax.axis_index("genome") * nb
    partner = first + lax.axis_index("offset") * nd
    return first // LANES, partner // LANES, partner % LANES


def roll(x, shift):
    length = x.shape[1]
    if isinstance(shift, int):
        shift = shift % length
        if shift == 0:
            return x
    return pltpu.roll(x, shift, 1)


def hankel(rows_ref, row0, lane0, tiles, out_ref):
    extra = 1 if lane0 is None else 2
    base = jnp.concatenate(
        [jnp.broadcast_to(rows_ref[pl.ds(row0 + t, 1), :], (8, LANES)) for t in range(tiles + extra)],
        axis=1,
    )
    length = base.shape[1]
    if lane0 is not None:
        base = roll(base, length - lane0)
    sub = iota(base.shape, 0)
    for bit in (1, 2, 4):
        base = jnp.where((sub & bit) > 0, roll(base, length - bit), base)
    for r in range(16):
        out_ref[8 * r : 8 * r + 8, : tiles * LANES] = roll(base, length - 8 * r)[:, : tiles * LANES]


def antidiagonal(acc_ref, tiles, lane0):
    extra = 1 if lane0 is None else 2
    pad = jnp.zeros((8, extra * LANES), F32)
    parts = [jnp.concatenate([acc_ref[8 * r : 8 * r + 8, : tiles * LANES], pad], axis=1) for r in range(16)]
    shift = 8
    while len(parts) > 1:
        parts = [low + roll(high, shift) for low, high in zip(parts[::2], parts[1::2])]
        shift *= 2
    total = parts[0]
    sub = iota(total.shape, 0)
    for bit in (4, 2, 1):
        total = jnp.where((sub & bit) > 0, roll(total, bit), total)
    total = jnp.sum(total, axis=0, keepdims=True)
    if lane0 is not None:
        total = roll(total, lane0)
    return total


def spread(own, partner, row_own, row_partner, placed_ref, out_ref):
    placed_ref[...] = jnp.zeros_like(placed_ref)
    for t in range(partner.shape[1] // LANES):
        placed_ref[pl.ds(row_partner + t, 1), :] = partner[:, t * LANES : (t + 1) * LANES]
    for c in range(own.shape[1] // LANES):
        placed_ref[pl.ds(row_own + c, 1), :] += own[:, c * LANES : (c + 1) * LANES]
    out_ref[...] = placed_ref[: out_ref.shape[0], :]


def sweep(nd, nb, entry, weigh_own, weigh_partner, acc_ref):
    cols = nb // LANES
    full, rest = nd // LANES, nd % LANES
    first_diag = lax.axis_index("offset") * nd
    sub = iota((16, LANES), 0)

    def body(ms, fresh, r, own):
        own = list(own)
        q0 = pl.multiple_of(16 * r, 16)
        sums = {}
        for m in ms:
            for c in range(cols):
                w = entry(m, c, q0)
                own[c] = own[c] + weigh_own(w, m, c, q0)
                g = weigh_partner(w, c)
                if m == 0:
                    g = jnp.where(sub + q0 + first_diag > 0, g, 0.0)
                sums[m + c] = sums[m + c] + g if m + c in sums else g
        for t, value in sums.items():
            tile = (pl.ds(q0, 16), slice(t * LANES, (t + 1) * LANES))
            acc_ref[tile] = value if fresh else acc_ref[tile] + value
        return tuple(own)

    own = tuple(jnp.zeros((16, LANES), F32) for _ in range(cols))
    if rest:
        acc_ref[...] = jnp.zeros_like(acc_ref)
    own = lax.fori_loop(0, 8, functools.partial(body, range(full), not rest), own)
    if rest:
        own = lax.fori_loop(0, rest // 16, functools.partial(body, [full], False), own)
    return jnp.concatenate([jnp.sum(o, axis=0, keepdims=True) for o in own], axis=1)


def keep_of(masked, rows):
    count = masked.shape[1]
    in_row = (jnp.broadcast_to(masked >> 7, (rows, count)) == iota((rows, count), 0))
    in_lane = (jnp.broadcast_to(masked & 127, (LANES, count)) == iota((LANES, count), 0))
    hits = lax.dot_general(
        in_row.astype(F32).astype(BF16), in_lane.astype(F32).astype(BF16), NT, preferred_element_type=F32
    )
    return jnp.where(hits > 0.0, 0.0, 1.0)


def first_kernel(nd, nb, bounds_hbm, x_hbm, masked_hbm, w_ref, part_ref, keep_ref, top_ref, bottom_ref,
                 codes_ref, hank_ref, acc_ref, placed_ref, bounds_ref, x_ref, masked_ref, sems):
    copies = [
        pltpu.make_async_copy(source, target, sems.at[k])
        for k, (source, target) in enumerate(
            ((masked_hbm, masked_ref), (bounds_hbm, bounds_ref), (x_hbm, x_ref))
        )
    ]
    for copy in copies:
        copy.start()
    copies[0].wait()
    copies[1].wait()
    rows = keep_ref.shape[0]
    cols = nb // LANES
    span = -(-nd // LANES) + cols - 1
    row_own, row_partner, lane0 = place(nd, nb)
    lane0 = lane0 if nd % LANES else None
    keep = keep_of(masked_ref[...], rows)
    keep_ref[...] = keep
    bins = iota((rows, LANES), 0) * LANES + iota((rows, LANES), 1)
    chrom = jnp.zeros((rows, LANES), F32)
    for k in range(bounds_ref.shape[0]):
        chrom = chrom + jnp.where(bins >= bounds_ref[k], 1.0, 0.0)
    codes_ref[...] = jnp.full_like(codes_ref, -2.0)
    codes_ref[:rows, :] = jnp.where(keep > 0.0, chrom, -2.0)
    hankel(codes_ref, row_partner, lane0, span, hank_ref)
    code_own = []
    for c in range(cols):
        code = codes_ref[pl.ds(row_own + c, 1), :]
        code = jnp.where(code < 0.0, -1.0, code)
        code_own.append(jnp.broadcast_to(code, (16, LANES)))
    copies[2].wait()

    def entry(m, c, q0):
        here = (pl.ds(q0 + m * LANES, 16), slice(c * LANES, (c + 1) * LANES))
        code = hank_ref[pl.ds(q0, 16), (m + c) * LANES : (m + c + 1) * LANES]
        value = jnp.maximum(x_ref[here].astype(F32), TINY)
        w = jnp.where(code == code_own[c], value, 0.0)
        w_ref[here] = w.astype(BF16)
        return w

    own = sweep(nd, nb, entry, lambda w, m, c, q0: w, lambda w, c: w, acc_ref)
    spread(own, antidiagonal(acc_ref, span, lane0), row_own, row_partner, placed_ref, part_ref)
    top_ref[...] = w_ref[:RIM, :].astype(F32)
    bottom_ref[...] = w_ref[nd - RIM :, :].astype(F32)


def next_bias(keep, bias, sums):
    level = jnp.sum(sums * keep, keepdims=True) / jnp.sum(keep, keepdims=True)
    safe = jnp.where(keep > 0.0, sums, 1.0)
    return jnp.where(keep > 0.0, bias * level / safe, 0.0)


def second_kernel(nd, nb, w_ref, sums_ref, keep_ref, part_ref, bias_ref, window_ref, hank_ref, acc_ref, placed_ref):
    rows = keep_ref.shape[0]
    cols = nb // LANES
    span = -(-nd // LANES) + cols - 1
    row_own, row_partner, lane0 = place(nd, nb)
    lane0 = lane0 if nd % LANES else None
    bias = next_bias(keep_ref[...], keep_ref[...], sums_ref[...])
    bias_ref[...] = bias
    window_ref[...] = jnp.zeros_like(window_ref)
    window_ref[:rows, :] = bias
    hankel(window_ref, row_partner, lane0, span, hank_ref)
    rows_own = [window_ref[pl.ds(row_own + c, 1), :] for c in range(cols)]
    own_bias = [jnp.broadcast_to(b, (16, LANES)) for b in rows_own]

    def entry(m, c, q0):
        return w_ref[pl.ds(q0 + m * LANES, 16), c * LANES : (c + 1) * LANES].astype(F32)

    def weigh_own(w, m, c, q0):
        return w * hank_ref[pl.ds(q0, 16), (m + c) * LANES : (m + c + 1) * LANES]

    own = sweep(nd, nb, entry, weigh_own, lambda w, c: w * own_bias[c], acc_ref)
    own = own * jnp.concatenate(rows_own, axis=1)
    partner = antidiagonal(acc_ref, span, lane0)
    tiles = partner.shape[1] // LANES
    partner = partner * jnp.concatenate(
        [window_ref[pl.ds(row_partner + t, 1), :] for t in range(tiles)], axis=1
    )
    spread(own, partner, row_own, row_partner, placed_ref, part_ref)


def side_kernel(nd, nb, w_ref, top_ref, bottom_ref, left_ref, right_ref):
    row, lane = iota((SIDE, LANES), 0), iota((SIDE, LANES), 1)
    for out_ref, pick, first in (
        (left_ref, row == lane, 0),
        (right_ref, row + LANES - SIDE == lane, nb - LANES),
    ):
        pick = pick.astype(F32).astype(BF16)
        cols = slice(first, first + LANES)
        block = jnp.concatenate(
            [w_ref[:, cols], bottom_ref[:, cols].astype(BF16), top_ref[:, cols].astype(BF16)], axis=0
        )
        out_ref[...] = lax.dot_general(pick, block, NT, preferred_element_type=F32)


def strip_kernel(nd, nb, first, count, w_ref, top_ref, bottom_ref, left_ref, right_ref, out_ref, perm_ref, side_ref):
    stride = nb // LANES
    width = count * LANES
    lane = iota((nb, LANES), 1)
    row = iota((nb, LANES), 0)
    for k in range(count):
        hit = row == lane * stride + (first + k)
        perm_ref[:, k * LANES : (k + 1) * LANES] = hit.astype(F32).astype(BF16)
    perm = perm_ref[...]
    rims = []
    row, lane = iota((2 * SIDE, LANES), 0), iota((2 * SIDE, LANES), 1)
    bin_of = jnp.where(row < SIDE, row - SIDE, row - SIDE + nb)
    for k in range(count):
        rims.append((bin_of == lane * stride + (first + k)).astype(F32).astype(BF16))
    rims = jnp.concatenate(rims, axis=1)
    sides = jnp.concatenate([left_ref[...], right_ref[...]], axis=0).astype(BF16)
    outer = first < 0 or first + count > stride
    if outer:
        side_ref[...] = lax.dot_general(
            sides, rims, (((0,), (0,)), ((), ())), preferred_element_type=F32
        )

    def emit(block, at, side_at, rows):
        value = jnp.dot(block, perm, preferred_element_type=F32)
        if outer:
            value = value + side_ref[side_at : side_at + rows, :]
        for k in range(count):
            out_ref[k, at : at + rows, :] = value[:, k * LANES : (k + 1) * LANES].astype(BF16)

    emit(top_ref[...].astype(BF16), 0, nd + RIM, RIM)
    emit(bottom_ref[...].astype(BF16), nd + RIM, nd, RIM)
    emit(w_ref[...], RIM, 0, nd)


def unstrip_kernel(nb, out_ref):
    stride = nb // LANES
    row, lane = iota((LANES, nb), 0), iota((LANES, nb), 1)
    for s in range(stride):
        out_ref[s * LANES : (s + 1) * LANES, :] = (lane == row * stride + s).astype(F32).astype(BF16)


def columns(rows, out_ref):
    for k, row in enumerate(rows):
        out_ref[k * LANES : (k + 1) * LANES, :] = jnp.broadcast_to(row, (LANES, LANES)).T


def fan(col_ref, other_ref, start, rows, stride, out_ref):
    lane = {}
    source, offset = col_ref, start
    target = other_ref
    for bit in (64, 32, 16, 8, 4, 2, 1):
        need = rows + stride * (bit - 1)
        need = -(-need // 8) * 8
        if bit == 1:
            target = out_ref
        def move(at, size, source=source, target=target, offset=offset, bit=bit):
            low = source[pl.ds(offset + at, size), :]
            high = source[pl.ds(offset + at + stride * bit, size), :]
            odd = (iota((size, LANES), 1) & bit) > 0
            target[pl.ds(at, size), :] = jnp.where(odd, high, low)

        move(0, need)
        source, target, offset = target, source, 0


def fan_rows(nd):
    return nd + 2 * RIM + 32


def third_kernel(nd, nb, mid_ref, sums_ref, keep_ref, bias_ref, own_ref, fan_ref, near_ref, diag_ref,
                 window_ref, col_ref, other_ref, ncol_ref, nother_ref, total_ref):
    rows = keep_ref.shape[0]
    cols = nb // LANES
    stride = cols
    row_own, row_partner, lane0 = place(nd, nb)
    bias = next_bias(keep_ref[...], bias_ref[...], sums_ref[...])
    window_ref[...] = jnp.zeros_like(window_ref)
    window_ref[8 : 8 + rows, :] = bias
    for c in range(cols):
        own_ref[c : c + 1, :] = window_ref[pl.ds(8 + row_own + c, 1), :]
    tiles = col_ref.shape[0] // LANES
    columns([window_ref[pl.ds(7 + row_partner + t, 1), :] for t in range(tiles)], col_ref)
    start = LANES - RIM - 8
    if nd % LANES:
        start = start + lane0
    fan(col_ref, other_ref, start, fan_rows(nd), stride, fan_ref)
    columns([window_ref[pl.ds(7 + row_own + t, 1), :] for t in range(ncol_ref.shape[0] // LANES)], ncol_ref)
    fan(ncol_ref, nother_ref, LANES - 8, near_ref.shape[0], stride, near_ref)
    total_rows = nd + 2 * RIM

    def add(r0, size):
        total, count = None, None
        for s in range(stride):
            w = mid_ref[s, pl.ds(r0, size), :].astype(F32)
            near = jnp.broadcast_to(near_ref[8 + s : 9 + s, :], (size, LANES))
            b = w * near * fan_ref[pl.ds(r0 + 8 + s, size), :]
            v = jnp.where(w > 0.0, 1.0, 0.0)
            total = b if total is None else total + b
            count = v if count is None else count + v
        total_ref[pl.ds(r0, size), :LANES] = total
        total_ref[pl.ds(r0, size), LANES:] = count

    over(0, total_rows, total_rows // 2, add)
    padded = total_ref.shape[0]
    tiles = padded // LANES
    if padded > total_rows:
        total_ref[total_rows:, :] = jnp.zeros((padded - total_rows, 2 * LANES), F32)
    for t in range(tiles):
        for k in range(2):
            block = total_ref[t * LANES : (t + 1) * LANES, k * LANES : (k + 1) * LANES]
            diag_ref[k * tiles + t : k * tiles + t + 1, :] = jnp.sum(block.T, axis=0, keepdims=True)


def over(start, count, step, run):
    steps = count // step
    if steps > 0:

        def body(i, _):
            run(pl.multiple_of(i * step + start, math.gcd(start, step)), step)
            return 0

        lax.fori_loop(0, steps, body, 0)
    if count % step:
        run(start + steps * step, count % step)


STRIPS = ("low", "last", "mid", "high", "final")


def strips_of(refs):
    return dict(enumerate(((ref, k) for ref in refs for k in range(ref.shape[0])), -5))


def shift_sums(chunk, stride, step, x, h, u, l, w, t):
    def mix(r0, size):
        for s in range(stride):
            here = (s, pl.ds(r0, size), slice(None))
            at = lambda ref, k, shift: ref[k, pl.ds(r0 + shift, size), :]
            hp = at(x, s + 8, -3) + at(x, s + 9, -4) + at(x, s + 10, -5)
            hm = at(x, s, 5) + at(x, s + 1, 4) + at(x, s + 2, 3)
            ahead, behind = at(x, s + 6, -1), at(x, s + 4, 1)
            lp = hp + (ahead + at(x, s + 7, -2))
            h[here] = hp
            u[here] = hp + hm
            l[here] = lp
            w[here] = lp + (hm + (behind + at(x, s + 3, 2)))
            t[here] = ahead + at(x, s + 5, 0) + behind

    over(8, chunk + 16, step, mix)


def four_sums(s, r0, size, h, u, l, w, t):
    at = lambda ref, shift: ref[s, pl.ds(r0 + shift, size), :]
    below, above = at(u, -1), at(u, 1)
    six = lambda ref: (at(ref, -5) + at(ref, -4) + at(ref, -3)) + (at(ref, 3) + at(ref, 4) + at(ref, 5))
    donut = six(w) + ((at(u, -2) + below) + (above + at(u, 2)))
    lower = (at(l, -5) + at(l, -4) + at(l, -3)) + (at(h, -2) + at(h, -1))
    return donut, lower, six(t), below + at(u, 0) + above


def observed_kernel(nd, nb, chunk, step, base, *refs):
    stride = nb // LANES
    strips = strips_of(refs[: len(STRIPS)])
    near_ref, fan_ref, out_ref, x_ref, *refs = refs[len(STRIPS) :]

    def fill(r0, size):
        for s, (ref, k) in strips.items():
            w = ref[k, pl.ds(base + r0, size), :].astype(F32)
            near = jnp.broadcast_to(near_ref[8 + s : 9 + s, :], (size, LANES))
            x_ref[s + 5, pl.ds(r0, size), :] = w * near * fan_ref[pl.ds(base + r0 + 8 + s, size), :]

    over(0, chunk + 2 * RIM, 2 * step, fill)
    shift_sums(chunk, stride, step, x_ref, *refs)

    def emit(r0, size):
        for s in range(stride):
            sums = four_sums(s, r0, size, *refs)
            for k, value in enumerate(sums + (x_ref[s + 5, pl.ds(r0, size), :],)):
                out_ref[5 * s + k, pl.ds(r0 - RIM, size), :] = value

    over(RIM, chunk, step, emit)


def score_kernel(nd, nb, chunk, step, *rest):
    stride = nb // LANES
    count = nd // chunk
    strips = strips_of(rest[: len(STRIPS)])
    diag_ref, perm_ref, *rest = rest[len(STRIPS) :]
    seen_refs, out_hbm = rest[:count], rest[count]
    col_ref, out_ref, sems, x_ref = rest[count + 1 : count + 5]
    refs = rest[count + 5 :]
    tiles = diag_ref.shape[0] // 2
    expected = diag_ref[:tiles, :] / jnp.maximum(diag_ref[tiles:, :], 1.0)
    expected = jnp.where(expected > 0.0, expected, 1.0)
    columns([expected[t : t + 1, :] for t in range(tiles)], col_ref)

    def leave(i):
        here = (pl.ds(pl.multiple_of(i * chunk, 32), chunk), slice(None))
        return pltpu.make_async_copy(out_ref.at[here], out_hbm.at[here], sems.at[i])

    def score(seen_ref, base, r0, size):
        e = col_ref[pl.ds(base + r0, size), :]
        inverse = 1.0 / e
        for s in range(stride):
            sums = four_sums(s, r0, size, *refs)
            seen = [seen_ref[5 * s + k, pl.ds(r0 - RIM, size), :] for k in range(5)]
            least = None
            for k in range(4):
                ratio = (sums[k] + e) / (seen[k] + e)
                least = ratio if least is None else jnp.minimum(least, ratio)
            value = least * (seen[4] * inverse)
            hi = value.astype(BF16)
            low = (value - hi.astype(F32)).astype(BF16)
            perm = perm_ref[s * LANES : (s + 1) * LANES, :]
            placed = jnp.dot(
                jnp.concatenate([hi, low], axis=1), jnp.concatenate([perm, perm], axis=0), preferred_element_type=F32
            )
            here = pl.ds(base + r0 - RIM, size)
            out_ref[here, :] = placed if s == 0 else out_ref[here, :] + placed

    def body(i, _):
        base = pl.multiple_of(i * chunk, 32)

        def fill(r0, size):
            e = col_ref[pl.ds(base + r0, size), :]
            for s, (ref, k) in strips.items():
                w = ref[k, pl.ds(base + r0, size), :].astype(F32)
                x_ref[s + 5, pl.ds(r0, size), :] = jnp.where(w > 0.0, e, 0.0)

        over(0, chunk + 2 * RIM, 2 * step, fill)
        shift_sums(chunk, stride, step, x_ref, *refs)
        for c in range(count):

            @pl.when(i == c)
            def _():
                over(RIM, chunk, chunk, functools.partial(score, seen_refs[c], base))

        leave(i).start()
        return 0

    lax.fori_loop(0, count, body, 0)
    for i in range(count):
        leave(i).wait()


def tie(x, state, names):
    x, values = lax.optimization_barrier((x, tuple(state[name] for name in names)))
    state.update(zip(names, values))
    return x


def total(x, axes, state=None, tasks={}, due={}):
    rounds = []
    for axis in axes:
        size, bit = lax.axis_size(axis), 1
        while bit < size:
            rounds.append((axis, [(i, i ^ bit) for i in range(size)]))
            bit *= 2
    for k, (axis, pairs) in enumerate(rounds):
        if k in tasks:
            x = tie(x, state, tasks[k][0])
        came = lax.ppermute(x, axis, pairs)
        if k in tasks:
            names, task = tasks[k]
            state.update(task(*[state[name] for name in names]))
        x = x + came
        if k in due:
            x = tie(x, state, due[k])
    return x


def shifted(x, axis, step):
    size = lax.axis_size(axis)
    pairs = [(i, i + 1) for i in range(size - 1)]
    return lax.ppermute(x, axis, pairs if step > 0 else [(j, i) for i, j in pairs])


def on_device(contacts, masked_bins, chrom_bounds):
    nd, nb = contacts.shape
    cols = nb // LANES
    bins = nb * lax.axis_size("genome")
    band = nd * lax.axis_size("offset")
    rows = bins // LANES
    span = -(-nd // LANES) + cols - 1
    tall = rows + -(-band // LANES) + 24
    total_rows = nd + 2 * RIM
    shape = jax.ShapeDtypeStruct
    f = lambda *dims: shape(dims, F32)

    w, part, keep, top, bottom = pl.pallas_call(
        functools.partial(first_kernel, nd, nb),
        out_shape=(shape((nd, nb), BF16), f(rows, LANES), f(rows, LANES), f(RIM, nb), f(RIM, nb)),
        in_specs=[HBM] * 3,
        out_specs=(VMEM,) * 5,
        scratch_shapes=[
            pltpu.VMEM((tall, LANES), F32),
            pltpu.VMEM((LANES, span * LANES), F32),
            pltpu.VMEM((LANES, span * LANES), F32),
            pltpu.VMEM((tall, LANES), F32),
            pltpu.SMEM(chrom_bounds.shape, jnp.int32),
            pltpu.VMEM((nd, nb), BF16),
            pltpu.VMEM((1,) + masked_bins.shape, jnp.int32),
            pltpu.SemaphoreType.DMA((3,)),
        ],
        compiler_params=params(12),
        name="first_sums",
    )(*(pltpu.with_memory_space_constraint(a, pltpu.HBM) for a in (chrom_bounds, contacts, masked_bins.reshape(1, -1))))

    def sides(w, above, below):
        return pl.pallas_call(
            functools.partial(side_kernel, nd, nb),
            out_shape=(f(SIDE, total_rows), f(SIDE, total_rows)),
            in_specs=[VMEM] * 3,
            out_specs=(VMEM,) * 2,
            compiler_params=params(16),
            name="sides",
        )(w, above, below)

    def first_side(w, above, below):
        left, right = sides(w, above, below)
        return dict(right=right, after=shifted(left, "genome", -1))

    state = dict(w=w, top=top, bottom=bottom)
    tasks = {
        0: (("bottom",), lambda bottom: dict(above=shifted(bottom, "offset", 1))),
        1: (("top",), lambda top: dict(below=shifted(top, "offset", -1))),
        3: (("w", "above", "below"), first_side),
    }
    sums = total(part, ("offset", "genome"), state, tasks, {1: ("above",), 2: ("below",)})
    w = state["w"]

    part, bias = pl.pallas_call(
        functools.partial(second_kernel, nd, nb),
        out_shape=(f(rows, LANES), f(rows, LANES)),
        in_specs=[VMEM] * 3,
        out_specs=(VMEM,) * 2,
        scratch_shapes=[
            pltpu.VMEM((tall, LANES), F32),
            pltpu.VMEM((LANES, span * LANES), F32),
            pltpu.VMEM((LANES, span * LANES), F32),
            pltpu.VMEM((tall, LANES), F32),
        ],
        compiler_params=params(),
        name="second_sums",
    )(w, sums, keep)

    def strip(name, first, count):
        def run(*operands):
            strips = pl.pallas_call(
                functools.partial(strip_kernel, nd, nb, first, count),
                out_shape=shape((count, total_rows, LANES), BF16),
                in_specs=[VMEM] * 5,
                out_specs=VMEM,
                scratch_shapes=[
                    pltpu.VMEM((nb, count * LANES), BF16),
                    pltpu.VMEM((total_rows, count * LANES), F32),
                ],
                compiler_params=params(24),
                name="strips",
            )(*operands)
            return {name: strips}

        side = dict(low="before", last="before", mid="above", high="after", final="after")[name]
        return ("w", "above", "below", side, side), run

    def ends(w, above, below, before, after):
        made = strip("last", -1, 1)[1](w, above, below, before, before)
        made.update(strip("final", cols + 4, 1)[1](w, above, below, after, after))
        return made

    def back(_, right):
        matrix = pl.pallas_call(
            functools.partial(unstrip_kernel, nb),
            out_shape=shape((nb, nb), BF16),
            out_specs=VMEM,
            compiler_params=params(8),
            name="unstrip",
        )()
        return dict(perm=matrix, before=shifted(right, "genome", 1))

    tasks = {
        0: (("keep", "right"), back),
        1: strip("mid", 0, cols),
        2: strip("high", cols, 4),
        3: strip("low", -5, 4),
        4: (("w", "above", "below", "before", "after"), ends),
    }
    state["keep"] = keep
    due = {0: ("perm", "after"), 1: ("mid",), 2: ("high", "before"), 3: ("low",), 4: ("last", "final")}
    sums = total(part, ("offset", "genome"), state, tasks, due)
    mid, perm, keep = (state[name] for name in ("mid", "perm", "keep"))

    padded = -(-total_rows // LANES) * LANES
    fan_len = fan_rows(nd)
    reach = -(-(fan_len + cols * (LANES - 1) + 2 * LANES) // LANES) * LANES
    near = 24
    near_reach = -(-(near + cols * (LANES - 1) + LANES) // LANES) * LANES
    own, fans, nears, diag = pl.pallas_call(
        functools.partial(third_kernel, nd, nb),
        out_shape=(f(cols, LANES), f(fan_len, LANES), f(near, LANES), f(2 * padded // LANES, LANES)),
        in_specs=[VMEM] * 4,
        out_specs=(VMEM,) * 4,
        scratch_shapes=[
            pltpu.VMEM((tall + 8, LANES), F32),
            pltpu.VMEM((reach, LANES), F32),
            pltpu.VMEM((reach, LANES), F32),
            pltpu.VMEM((near_reach, LANES), F32),
            pltpu.VMEM((near_reach, LANES), F32),
            pltpu.VMEM((padded, 2 * LANES), F32),
        ],
        compiler_params=params(),
        name="diagonal_sums",
    )(mid, sums, keep, bias)
    chunk = next(c for c in (320, 256, 128, 64, 32) if nd % c == 0)
    count = nd // chunk
    tall = chunk + 2 * RIM
    scratch = [pltpu.VMEM((tiles, tall, LANES), F32) for tiles in (cols + 10,) + (cols,) * 5]

    def observe(*which):
        def run(*operands):
            made = {}
            for c in which:
                made[f"seen{c}"] = pl.pallas_call(
                    functools.partial(observed_kernel, nd, nb, chunk, STEP, c * chunk),
                    out_shape=f(5 * cols, chunk, LANES),
                    in_specs=[VMEM] * len(operands),
                    out_specs=VMEM,
                    scratch_shapes=scratch,
                    compiler_params=params(20),
                    name="observed",
                )(*operands)
            return made

        return STRIPS + ("near", "fan"), run

    rounds = (lax.axis_size("genome") - 1).bit_length()
    turns = {}
    for c in range(count):
        turns.setdefault((c + 1) * (rounds - 1) // count, []).append(c)
    state.update(near=nears, fan=fans)
    diag = total(
        diag,
        ("genome",),
        state,
        {k: observe(*which) for k, which in turns.items()},
        {k: tuple(f"seen{c}" for c in which) for k, which in turns.items()},
    )

    operands = tuple(state[name] for name in STRIPS) + (diag, perm) + tuple(state[f"seen{c}"] for c in range(count))
    score = pl.pallas_call(
        functools.partial(score_kernel, nd, nb, chunk, STEP),
        out_shape=f(nd, nb),
        in_specs=[VMEM] * len(operands),
        out_specs=HBM,
        scratch_shapes=[
            pltpu.VMEM((padded, LANES), F32),
            pltpu.VMEM((nd, nb), F32),
            pltpu.SemaphoreType.DMA((count,)),
        ]
        + scratch,
        compiler_params=params(24),
        name="score",
    )(*operands)
    return score, own.reshape(nb)


def solution(mesh):
    return jax.shard_map(
        on_device,
        mesh=mesh,
        in_specs=(P("offset", "genome"), P(), P()),
        out_specs=(P("offset", "genome"), P("genome")),
        check_vma=False,
    )
```

```python
import functools
import math

import jax
import jax.numpy as jnp
from jax import lax
from jax.experimental import pallas as pl
from jax.experimental.pallas import tpu as pltpu
from jax.sharding import PartitionSpec as P

RIM = 16
STEP = 64
SIDE = 8
LANES = 128
F32 = jnp.float32
BF16 = jnp.bfloat16
TINY = 2.0**-126
VMEM = pl.BlockSpec(memory_space=pltpu.VMEM)
HBM = pl.BlockSpec(memory_space=pltpu.HBM)
ANY = pl.BlockSpec(memory_space=pl.ANY)
NT = (((1,), (1,)), ((), ()))


def params(mib=48):
    return pltpu.CompilerParams(vmem_limit_bytes=mib << 20)


def iota(shape, dim):
    return lax.broadcasted_iota(jnp.int32, shape, dim)


def place(nd, nb):
    first = lax.axis_index("genome") * nb
    partner = first + lax.axis_index("offset") * nd
    return first // LANES, partner // LANES, partner % LANES


def roll(x, shift):
    length = x.shape[1]
    if isinstance(shift, int):
        shift = shift % length
        if shift == 0:
            return x
    return pltpu.roll(x, shift, 1)


def hankel(rows_ref, row0, lane0, tiles, out_ref):
    extra = 1 if lane0 is None else 2
    base = jnp.concatenate(
        [jnp.broadcast_to(rows_ref[pl.ds(row0 + t, 1), :], (8, LANES)) for t in range(tiles + extra)],
        axis=1,
    )
    length = base.shape[1]
    if lane0 is not None:
        base = roll(base, length - lane0)
    sub = iota(base.shape, 0)
    for bit in (1, 2, 4):
        base = jnp.where((sub & bit) > 0, roll(base, length - bit), base)
    for r in range(16):
        out_ref[8 * r : 8 * r + 8, : tiles * LANES] = roll(base, length - 8 * r)[:, : tiles * LANES]


def antidiagonal(acc_ref, tiles, lane0):
    extra = 1 if lane0 is None else 2
    pad = jnp.zeros((8, extra * LANES), F32)
    parts = [jnp.concatenate([acc_ref[8 * r : 8 * r + 8, : tiles * LANES], pad], axis=1) for r in range(16)]
    shift = 8
    while len(parts) > 1:
        parts = [low + roll(high, shift) for low, high in zip(parts[::2], parts[1::2])]
        shift *= 2
    total = parts[0]
    sub = iota(total.shape, 0)
    for bit in (4, 2, 1):
        total = jnp.where((sub & bit) > 0, roll(total, bit), total)
    total = jnp.sum(total, axis=0, keepdims=True)
    if lane0 is not None:
        total = roll(total, lane0)
    return total


def spread(own, partner, row_own, row_partner, placed_ref, out_ref):
    placed_ref[...] = jnp.zeros_like(placed_ref)
    for t in range(partner.shape[1] // LANES):
        placed_ref[pl.ds(row_partner + t, 1), :] = partner[:, t * LANES : (t + 1) * LANES]
    for c in range(own.shape[1] // LANES):
        placed_ref[pl.ds(row_own + c, 1), :] += own[:, c * LANES : (c + 1) * LANES]
    out_ref[...] = placed_ref[: out_ref.shape[0], :]


def sweep(nd, nb, entry, weigh_own, weigh_partner, acc_ref):
    cols = nb // LANES
    full, rest = nd // LANES, nd % LANES
    first_diag = lax.axis_index("offset") * nd
    sub = iota((16, LANES), 0)

    def body(ms, fresh, r, own):
        own = list(own)
        q0 = pl.multiple_of(16 * r, 16)
        sums = {}
        for m in ms:
            for c in range(cols):
                w = entry(m, c, q0)
                own[c] = own[c] + weigh_own(w, m, c, q0)
                g = weigh_partner(w, c)
                if m == 0:
                    g = jnp.where(sub + q0 + first_diag > 0, g, 0.0)
                sums[m + c] = sums[m + c] + g if m + c in sums else g
        for t, value in sums.items():
            tile = (pl.ds(q0, 16), slice(t * LANES, (t + 1) * LANES))
            acc_ref[tile] = value if fresh else acc_ref[tile] + value
        return tuple(own)

    own = tuple(jnp.zeros((16, LANES), F32) for _ in range(cols))
    if rest:
        acc_ref[...] = jnp.zeros_like(acc_ref)
    own = lax.fori_loop(0, 8, functools.partial(body, range(full), not rest), own)
    if rest:
        own = lax.fori_loop(0, rest // 16, functools.partial(body, [full], False), own)
    return jnp.concatenate([jnp.sum(o, axis=0, keepdims=True) for o in own], axis=1)


def keep_of(masked, rows):
    count = masked.shape[1]
    in_row = (jnp.broadcast_to(masked >> 7, (rows, count)) == iota((rows, count), 0))
    in_lane = (jnp.broadcast_to(masked & 127, (LANES, count)) == iota((LANES, count), 0))
    hits = lax.dot_general(
        in_row.astype(F32).astype(BF16), in_lane.astype(F32).astype(BF16), NT, preferred_element_type=F32
    )
    return jnp.where(hits > 0.0, 0.0, 1.0)


def first_kernel(nd, nb, bounds_hbm, x_hbm, masked_hbm, w_ref, part_ref, keep_ref, top_ref, bottom_ref,
                 codes_ref, hank_ref, acc_ref, placed_ref, bounds_ref, x_ref, masked_ref, sems):
    copies = [
        pltpu.make_async_copy(source, target, sems.at[k])
        for k, (source, target) in enumerate(
            ((masked_hbm, masked_ref), (bounds_hbm, bounds_ref), (x_hbm, x_ref))
        )
    ]
    for copy in copies:
        copy.start()
    copies[0].wait()
    copies[1].wait()
    rows = keep_ref.shape[0]
    cols = nb // LANES
    span = -(-nd // LANES) + cols - 1
    row_own, row_partner, lane0 = place(nd, nb)
    lane0 = lane0 if nd % LANES else None
    keep = keep_of(masked_ref[...], rows)
    keep_ref[...] = keep
    bins = iota((rows, LANES), 0) * LANES + iota((rows, LANES), 1)
    chrom = jnp.zeros((rows, LANES), F32)
    for k in range(bounds_ref.shape[0]):
        chrom = chrom + jnp.where(bins >= bounds_ref[k], 1.0, 0.0)
    codes_ref[...] = jnp.full_like(codes_ref, -2.0)
    codes_ref[:rows, :] = jnp.where(keep > 0.0, chrom, -2.0)
    hankel(codes_ref, row_partner, lane0, span, hank_ref)
    code_own = []
    for c in range(cols):
        code = codes_ref[pl.ds(row_own + c, 1), :]
        code = jnp.where(code < 0.0, -1.0, code)
        code_own.append(jnp.broadcast_to(code, (16, LANES)))
    copies[2].wait()

    def entry(m, c, q0):
        here = (pl.ds(q0 + m * LANES, 16), slice(c * LANES, (c + 1) * LANES))
        code = hank_ref[pl.ds(q0, 16), (m + c) * LANES : (m + c + 1) * LANES]
        value = jnp.maximum(x_ref[here].astype(F32), TINY)
        w = jnp.where(code == code_own[c], value, 0.0)
        w_ref[here] = w.astype(BF16)
        return w

    own = sweep(nd, nb, entry, lambda w, m, c, q0: w, lambda w, c: w, acc_ref)
    spread(own, antidiagonal(acc_ref, span, lane0), row_own, row_partner, placed_ref, part_ref)
    top_ref[...] = w_ref[:RIM, :].astype(F32)
    bottom_ref[...] = w_ref[nd - RIM :, :].astype(F32)


def next_bias(keep, bias, sums):
    level = jnp.sum(sums * keep, keepdims=True) / jnp.sum(keep, keepdims=True)
    safe = jnp.where(keep > 0.0, sums, 1.0)
    return jnp.where(keep > 0.0, bias * level / safe, 0.0)


def second_kernel(nd, nb, w_ref, sums_ref, keep_ref, part_ref, bias_ref, window_ref, hank_ref, acc_ref, placed_ref):
    rows = keep_ref.shape[0]
    cols = nb // LANES
    span = -(-nd // LANES) + cols - 1
    row_own, row_partner, lane0 = place(nd, nb)
    lane0 = lane0 if nd % LANES else None
    bias = next_bias(keep_ref[...], keep_ref[...], sums_ref[...])
    bias_ref[...] = bias
    window_ref[...] = jnp.zeros_like(window_ref)
    window_ref[:rows, :] = bias
    hankel(window_ref, row_partner, lane0, span, hank_ref)
    rows_own = [window_ref[pl.ds(row_own + c, 1), :] for c in range(cols)]
    own_bias = [jnp.broadcast_to(b, (16, LANES)) for b in rows_own]

    def entry(m, c, q0):
        return w_ref[pl.ds(q0 + m * LANES, 16), c * LANES : (c + 1) * LANES].astype(F32)

    def weigh_own(w, m, c, q0):
        return w * hank_ref[pl.ds(q0, 16), (m + c) * LANES : (m + c + 1) * LANES]

    own = sweep(nd, nb, entry, weigh_own, lambda w, c: w * own_bias[c], acc_ref)
    own = own * jnp.concatenate(rows_own, axis=1)
    partner = antidiagonal(acc_ref, span, lane0)
    tiles = partner.shape[1] // LANES
    partner = partner * jnp.concatenate(
        [window_ref[pl.ds(row_partner + t, 1), :] for t in range(tiles)], axis=1
    )
    spread(own, partner, row_own, row_partner, placed_ref, part_ref)


def side_kernel(nd, nb, w_ref, top_ref, bottom_ref, left_ref, right_ref):
    row, lane = iota((SIDE, LANES), 0), iota((SIDE, LANES), 1)
    for out_ref, pick, first in (
        (left_ref, row == lane, 0),
        (right_ref, row + LANES - SIDE == lane, nb - LANES),
    ):
        pick = pick.astype(F32).astype(BF16)
        cols = slice(first, first + LANES)
        block = jnp.concatenate(
            [w_ref[:, cols], bottom_ref[:, cols].astype(BF16), top_ref[:, cols].astype(BF16)], axis=0
        )
        out_ref[...] = lax.dot_general(pick, block, NT, preferred_element_type=F32)


def strip_kernel(nd, nb, first, count, w_ref, top_ref, bottom_ref, left_ref, right_ref, out_ref, perm_ref, side_ref):
    stride = nb // LANES
    width = count * LANES
    lane = iota((nb, LANES), 1)
    row = iota((nb, LANES), 0)
    for k in range(count):
        hit = row == lane * stride + (first + k)
        perm_ref[:, k * LANES : (k + 1) * LANES] = hit.astype(F32).astype(BF16)
    perm = perm_ref[...]
    rims = []
    row, lane = iota((2 * SIDE, LANES), 0), iota((2 * SIDE, LANES), 1)
    bin_of = jnp.where(row < SIDE, row - SIDE, row - SIDE + nb)
    for k in range(count):
        rims.append((bin_of == lane * stride + (first + k)).astype(F32).astype(BF16))
    rims = jnp.concatenate(rims, axis=1)
    sides = jnp.concatenate([left_ref[...], right_ref[...]], axis=0).astype(BF16)
    outer = first < 0 or first + count > stride
    if outer:
        side_ref[...] = lax.dot_general(
            sides, rims, (((0,), (0,)), ((), ())), preferred_element_type=F32
        )

    def emit(block, at, side_at, rows):
        value = jnp.dot(block, perm, preferred_element_type=F32)
        if outer:
            value = value + side_ref[side_at : side_at + rows, :]
        for k in range(count):
            out_ref[k, at : at + rows, :] = value[:, k * LANES : (k + 1) * LANES].astype(BF16)

    emit(top_ref[...].astype(BF16), 0, nd + RIM, RIM)
    emit(bottom_ref[...].astype(BF16), nd + RIM, nd, RIM)
    emit(w_ref[...], RIM, 0, nd)


def unstrip_kernel(nb, out_ref):
    stride = nb // LANES
    row, lane = iota((LANES, nb), 0), iota((LANES, nb), 1)
    for s in range(stride):
        out_ref[s * LANES : (s + 1) * LANES, :] = (lane == row * stride + s).astype(F32).astype(BF16)


def columns(rows, out_ref):
    for k, row in enumerate(rows):
        out_ref[k * LANES : (k + 1) * LANES, :] = jnp.broadcast_to(row, (LANES, LANES)).T


def fan(col_ref, other_ref, start, rows, stride, out_ref):
    lane = {}
    source, offset = col_ref, start
    target = other_ref
    for bit in (64, 32, 16, 8, 4, 2, 1):
        need = rows + stride * (bit - 1)
        need = -(-need // 8) * 8
        if bit == 1:
            target = out_ref
        def move(at, size, source=source, target=target, offset=offset, bit=bit):
            low = source[pl.ds(offset + at, size), :]
            high = source[pl.ds(offset + at + stride * bit, size), :]
            odd = (iota((size, LANES), 1) & bit) > 0
            target[pl.ds(at, size), :] = jnp.where(odd, high, low)

        move(0, need)
        source, target, offset = target, source, 0


def fan_rows(nd):
    return nd + 2 * RIM + 32


def third_kernel(nd, nb, mid_ref, sums_ref, keep_ref, bias_ref, own_ref, fan_ref, near_ref, diag_ref,
                 window_ref, col_ref, other_ref, ncol_ref, nother_ref, total_ref):
    rows = keep_ref.shape[0]
    cols = nb // LANES
    stride = cols
    row_own, row_partner, lane0 = place(nd, nb)
    bias = next_bias(keep_ref[...], bias_ref[...], sums_ref[...])
    window_ref[...] = jnp.zeros_like(window_ref)
    window_ref[8 : 8 + rows, :] = bias
    for c in range(cols):
        own_ref[c : c + 1, :] = window_ref[pl.ds(8 + row_own + c, 1), :]
    tiles = col_ref.shape[0] // LANES
    columns([window_ref[pl.ds(7 + row_partner + t, 1), :] for t in range(tiles)], col_ref)
    start = LANES - RIM - 8
    if nd % LANES:
        start = start + lane0
    fan(col_ref, other_ref, start, fan_rows(nd), stride, fan_ref)
    columns([window_ref[pl.ds(7 + row_own + t, 1), :] for t in range(ncol_ref.shape[0] // LANES)], ncol_ref)
    fan(ncol_ref, nother_ref, LANES - 8, near_ref.shape[0], stride, near_ref)
    total_rows = nd + 2 * RIM

    def add(r0, size):
        total, count = None, None
        for s in range(stride):
            w = mid_ref[s, pl.ds(r0, size), :].astype(F32)
            near = jnp.broadcast_to(near_ref[8 + s : 9 + s, :], (size, LANES))
            b = w * near * fan_ref[pl.ds(r0 + 8 + s, size), :]
            v = jnp.where(w > 0.0, 1.0, 0.0)
            total = b if total is None else total + b
            count = v if count is None else count + v
        total_ref[pl.ds(r0, size), :LANES] = total
        total_ref[pl.ds(r0, size), LANES:] = count

    over(0, total_rows, total_rows // 2, add)
    padded = total_ref.shape[0]
    tiles = padded // LANES
    if padded > total_rows:
        total_ref[total_rows:, :] = jnp.zeros((padded - total_rows, 2 * LANES), F32)
    for t in range(tiles):
        for k in range(2):
            block = total_ref[t * LANES : (t + 1) * LANES, k * LANES : (k + 1) * LANES]
            diag_ref[k * tiles + t : k * tiles + t + 1, :] = jnp.sum(block.T, axis=0, keepdims=True)


def over(start, count, step, run):
    steps = count // step
    if steps > 0:

        def body(i, _):
            run(pl.multiple_of(i * step + start, math.gcd(start, step)), step)
            return 0

        lax.fori_loop(0, steps, body, 0)
    if count % step:
        run(start + steps * step, count % step)


STRIPS = ("low", "last", "mid", "high", "final")


def strips_of(refs):
    return dict(enumerate(((ref, k) for ref in refs for k in range(ref.shape[0])), -5))


def shift_sums(chunk, stride, step, x, h, u, l, w, t):
    def mix(r0, size):
        for s in range(stride):
            here = (s, pl.ds(r0, size), slice(None))
            at = lambda ref, k, shift: ref[k, pl.ds(r0 + shift, size), :]
            hp = at(x, s + 8, -3) + at(x, s + 9, -4) + at(x, s + 10, -5)
            hm = at(x, s, 5) + at(x, s + 1, 4) + at(x, s + 2, 3)
            ahead, behind = at(x, s + 6, -1), at(x, s + 4, 1)
            lp = hp + (ahead + at(x, s + 7, -2))
            h[here] = hp
            u[here] = hp + hm
            l[here] = lp
            w[here] = lp + (hm + (behind + at(x, s + 3, 2)))
            t[here] = ahead + at(x, s + 5, 0) + behind

    over(8, chunk + 16, step, mix)


def four_sums(s, r0, size, h, u, l, w, t):
    at = lambda ref, shift: ref[s, pl.ds(r0 + shift, size), :]
    below, above = at(u, -1), at(u, 1)
    six = lambda ref: (at(ref, -5) + at(ref, -4) + at(ref, -3)) + (at(ref, 3) + at(ref, 4) + at(ref, 5))
    donut = six(w) + ((at(u, -2) + below) + (above + at(u, 2)))
    lower = (at(l, -5) + at(l, -4) + at(l, -3)) + (at(h, -2) + at(h, -1))
    return donut, lower, six(t), below + at(u, 0) + above


def observed_kernel(nd, nb, chunk, step, base, *refs):
    stride = nb // LANES
    strips = strips_of(refs[: len(STRIPS)])
    near_ref, fan_ref, out_ref, x_ref, *refs = refs[len(STRIPS) :]

    def fill(r0, size):
        for s, (ref, k) in strips.items():
            w = ref[k, pl.ds(base + r0, size), :].astype(F32)
            near = jnp.broadcast_to(near_ref[8 + s : 9 + s, :], (size, LANES))
            x_ref[s + 5, pl.ds(r0, size), :] = w * near * fan_ref[pl.ds(base + r0 + 8 + s, size), :]

    over(0, chunk + 2 * RIM, 2 * step, fill)
    shift_sums(chunk, stride, step, x_ref, *refs)

    def emit(r0, size):
        for s in range(stride):
            sums = four_sums(s, r0, size, *refs)
            for k, value in enumerate(sums + (x_ref[s + 5, pl.ds(r0, size), :],)):
                out_ref[5 * s + k, pl.ds(r0 - RIM, size), :] = value

    over(RIM, chunk, step, emit)


def score_kernel(nd, nb, chunk, step, *rest):
    stride = nb // LANES
    count = nd // chunk
    strips = strips_of(rest[: len(STRIPS)])
    diag_ref, perm_ref, *rest = rest[len(STRIPS) :]
    seen_refs, out_hbm = rest[:count], rest[count]
    col_ref, out_ref, sems, x_ref = rest[count + 1 : count + 5]
    refs = rest[count + 5 :]
    tiles = diag_ref.shape[0] // 2
    expected = diag_ref[:tiles, :] / jnp.maximum(diag_ref[tiles:, :], 1.0)
    expected = jnp.where(expected > 0.0, expected, 1.0)
    columns([expected[t : t + 1, :] for t in range(tiles)], col_ref)

    def leave(i):
        here = (pl.ds(pl.multiple_of(i * chunk, 32), chunk), slice(None))
        return pltpu.make_async_copy(out_ref.at[here], out_hbm.at[here], sems.at[i])

    def score(seen_ref, base, r0, size):
        e = col_ref[pl.ds(base + r0, size), :]
        inverse = 1.0 / e
        for s in range(stride):
            sums = four_sums(s, r0, size, *refs)
            seen = [seen_ref[5 * s + k, pl.ds(r0 - RIM, size), :] for k in range(5)]
            least = None
            for k in range(4):
                ratio = (sums[k] + e) / (seen[k] + e)
                least = ratio if least is None else jnp.minimum(least, ratio)
            value = least * (seen[4] * inverse)
            hi = value.astype(BF16)
            low = (value - hi.astype(F32)).astype(BF16)
            perm = perm_ref[s * LANES : (s + 1) * LANES, :]
            placed = jnp.dot(
                jnp.concatenate([hi, low], axis=1), jnp.concatenate([perm, perm], axis=0), preferred_element_type=F32
            )
            here = pl.ds(base + r0 - RIM, size)
            out_ref[here, :] = placed if s == 0 else out_ref[here, :] + placed

    def body(i, _):
        base = pl.multiple_of(i * chunk, 32)

        def fill(r0, size):
            e = col_ref[pl.ds(base + r0, size), :]
            for s, (ref, k) in strips.items():
                w = ref[k, pl.ds(base + r0, size), :].astype(F32)
                x_ref[s + 5, pl.ds(r0, size), :] = jnp.where(w > 0.0, e, 0.0)

        over(0, chunk + 2 * RIM, 2 * step, fill)
        shift_sums(chunk, stride, step, x_ref, *refs)
        for c in range(count):

            @pl.when(i == c)
            def _():
                over(RIM, chunk, chunk, functools.partial(score, seen_refs[c], base))

        leave(i).start()
        return 0

    lax.fori_loop(0, count, body, 0)
    for i in range(count):
        leave(i).wait()


def tie(x, state, names):
    x, values = lax.optimization_barrier((x, tuple(state[name] for name in names)))
    state.update(zip(names, values))
    return x


def total(x, axes, state=None, tasks={}, due={}):
    rounds = []
    for axis in axes:
        size, bit = lax.axis_size(axis), 1
        while bit < size:
            rounds.append((axis, [(i, i ^ bit) for i in range(size)]))
            bit *= 2
    for k, (axis, pairs) in enumerate(rounds):
        if k in tasks:
            x = tie(x, state, tasks[k][0])
        came = lax.ppermute(x, axis, pairs)
        if k in tasks:
            names, task = tasks[k]
            state.update(task(*[state[name] for name in names]))
        x = x + came
        if k in due:
            x = tie(x, state, due[k])
    return x


def shifted(x, axis, step):
    size = lax.axis_size(axis)
    pairs = [(i, i + 1) for i in range(size - 1)]
    return lax.ppermute(x, axis, pairs if step > 0 else [(j, i) for i, j in pairs])


def on_device(contacts, masked_bins, chrom_bounds):
    nd, nb = contacts.shape
    cols = nb // LANES
    bins = nb * lax.axis_size("genome")
    band = nd * lax.axis_size("offset")
    rows = bins // LANES
    span = -(-nd // LANES) + cols - 1
    tall = rows + -(-band // LANES) + 24
    total_rows = nd + 2 * RIM
    shape = jax.ShapeDtypeStruct
    f = lambda *dims: shape(dims, F32)

    w, part, keep, top, bottom = pl.pallas_call(
        functools.partial(first_kernel, nd, nb),
        out_shape=(shape((nd, nb), BF16), f(rows, LANES), f(rows, LANES), f(RIM, nb), f(RIM, nb)),
        in_specs=[HBM] * 3,
        out_specs=(VMEM,) * 5,
        scratch_shapes=[
            pltpu.VMEM((tall, LANES), F32),
            pltpu.VMEM((LANES, span * LANES), F32),
            pltpu.VMEM((LANES, span * LANES), F32),
            pltpu.VMEM((tall, LANES), F32),
            pltpu.SMEM(chrom_bounds.shape, jnp.int32),
            pltpu.VMEM((nd, nb), BF16),
            pltpu.VMEM((1,) + masked_bins.shape, jnp.int32),
            pltpu.SemaphoreType.DMA((3,)),
        ],
        compiler_params=params(12),
        name="first_sums",
    )(*(pltpu.with_memory_space_constraint(a, pltpu.HBM) for a in (chrom_bounds, contacts, masked_bins.reshape(1, -1))))

    def sides(w, above, below):
        return pl.pallas_call(
            functools.partial(side_kernel, nd, nb),
            out_shape=(f(SIDE, total_rows), f(SIDE, total_rows)),
            in_specs=[VMEM] * 3,
            out_specs=(VMEM,) * 2,
            compiler_params=params(16),
            name="sides",
        )(w, above, below)

    def first_side(w, above, below):
        left, right = sides(w, above, below)
        return dict(right=right, after=shifted(left, "genome", -1))

    state = dict(w=w, top=top, bottom=bottom)
    tasks = {
        0: (("bottom",), lambda bottom: dict(above=shifted(bottom, "offset", 1))),
        1: (("top",), lambda top: dict(below=shifted(top, "offset", -1))),
        3: (("w", "above", "below"), first_side),
    }
    sums = total(part, ("offset", "genome"), state, tasks, {1: ("above",), 2: ("below",)})
    w = state["w"]

    part, bias = pl.pallas_call(
        functools.partial(second_kernel, nd, nb),
        out_shape=(f(rows, LANES), f(rows, LANES)),
        in_specs=[VMEM] * 3,
        out_specs=(VMEM,) * 2,
        scratch_shapes=[
            pltpu.VMEM((tall, LANES), F32),
            pltpu.VMEM((LANES, span * LANES), F32),
            pltpu.VMEM((LANES, span * LANES), F32),
            pltpu.VMEM((tall, LANES), F32),
        ],
        compiler_params=params(),
        name="second_sums",
    )(w, sums, keep)

    def strip(name, first, count):
        def run(*operands):
            strips = pl.pallas_call(
                functools.partial(strip_kernel, nd, nb, first, count),
                out_shape=shape((count, total_rows, LANES), BF16),
                in_specs=[VMEM] * 5,
                out_specs=VMEM,
                scratch_shapes=[
                    pltpu.VMEM((nb, count * LANES), BF16),
                    pltpu.VMEM((total_rows, count * LANES), F32),
                ],
                compiler_params=params(24),
                name="strips",
            )(*operands)
            return {name: strips}

        side = dict(low="before", last="before", mid="above", high="after", final="after")[name]
        return ("w", "above", "below", side, side), run

    def ends(w, above, below, before, after):
        made = strip("last", -1, 1)[1](w, above, below, before, before)
        made.update(strip("final", cols + 4, 1)[1](w, above, below, after, after))
        return made

    def back(_, right):
        matrix = pl.pallas_call(
            functools.partial(unstrip_kernel, nb),
            out_shape=shape((nb, nb), BF16),
            out_specs=VMEM,
            compiler_params=params(8),
            name="unstrip",
        )()
        return dict(perm=matrix, before=shifted(right, "genome", 1))

    tasks = {
        0: (("keep", "right"), back),
        1: strip("mid", 0, cols),
        2: strip("high", cols, 4),
        3: strip("low", -5, 4),
        4: (("w", "above", "below", "before", "after"), ends),
    }
    state["keep"] = keep
    due = {0: ("perm", "after"), 1: ("mid",), 2: ("high", "before"), 3: ("low",), 4: ("last", "final")}
    sums = total(part, ("offset", "genome"), state, tasks, due)
    mid, perm, keep = (state[name] for name in ("mid", "perm", "keep"))

    padded = -(-total_rows // LANES) * LANES
    fan_len = fan_rows(nd)
    reach = -(-(fan_len + cols * (LANES - 1) + 2 * LANES) // LANES) * LANES
    near = 24
    near_reach = -(-(near + cols * (LANES - 1) + LANES) // LANES) * LANES
    own, fans, nears, diag = pl.pallas_call(
        functools.partial(third_kernel, nd, nb),
        out_shape=(f(cols, LANES), f(fan_len, LANES), f(near, LANES), f(2 * padded // LANES, LANES)),
        in_specs=[VMEM] * 4,
        out_specs=(VMEM,) * 4,
        scratch_shapes=[
            pltpu.VMEM((tall + 8, LANES), F32),
            pltpu.VMEM((reach, LANES), F32),
            pltpu.VMEM((reach, LANES), F32),
            pltpu.VMEM((near_reach, LANES), F32),
            pltpu.VMEM((near_reach, LANES), F32),
            pltpu.VMEM((padded, 2 * LANES), F32),
        ],
        compiler_params=params(),
        name="diagonal_sums",
    )(mid, sums, keep, bias)
    chunk = next(c for c in (320, 256, 128, 64, 32) if nd % c == 0)
    count = nd // chunk
    tall = chunk + 2 * RIM
    scratch = [pltpu.VMEM((tiles, tall, LANES), F32) for tiles in (cols + 10,) + (cols,) * 5]

    def observe(*which):
        def run(*operands):
            made = {}
            for c in which:
                made[f"seen{c}"] = pl.pallas_call(
                    functools.partial(observed_kernel, nd, nb, chunk, STEP, c * chunk),
                    out_shape=f(5 * cols, chunk, LANES),
                    in_specs=[VMEM] * len(operands),
                    out_specs=VMEM,
                    scratch_shapes=scratch,
                    compiler_params=params(20),
                    name="observed",
                )(*operands)
            return made

        return STRIPS + ("near", "fan"), run

    rounds = (lax.axis_size("genome") - 1).bit_length()
    turns = {}
    for c in range(count):
        turns.setdefault((c + 1) * (rounds - 1) // count, []).append(c)
    state.update(near=nears, fan=fans)
    diag = total(
        diag,
        ("genome",),
        state,
        {k: observe(*which) for k, which in turns.items()},
        {k: tuple(f"seen{c}" for c in which) for k, which in turns.items()},
    )

    operands = tuple(state[name] for name in STRIPS) + (diag, perm) + tuple(state[f"seen{c}"] for c in range(count))
    score = pl.pallas_call(
        functools.partial(score_kernel, nd, nb, chunk, STEP),
        out_shape=f(nd, nb),
        in_specs=[VMEM] * len(operands),
        out_specs=HBM,
        scratch_shapes=[
            pltpu.VMEM((padded, LANES), F32),
            pltpu.VMEM((nd, nb), F32),
            pltpu.SemaphoreType.DMA((count,)),
        ]
        + scratch,
        compiler_params=params(24),
        name="score",
    )(*operands)
    return score, own.reshape(nb)


def solution(mesh):
    return jax.shard_map(
        on_device,
        mesh=mesh,
        in_specs=(P("offset", "genome"), P(), P()),
        out_specs=(P("offset", "genome"), P("genome")),
        check_vma=False,
    )
```
